32 devices in a mesh: groups: 2 (over y), seq: 4 (over z), wt: 2 (over x), head: 2 (over core).
Axes of the slice: x: 2, y: 2, z: 4, core: 2. Of those that a mesh axis runs over, the one named last changes fastest.
Arguments:
- queries: bfloat16 [1280, 3072], P(('groups', 'seq'), ('wt', 'head')), parts along dimension 0, may hold values from -6 to 6
- key_vectors: bfloat16 [1280, 3072], P(('groups', 'seq'), ('wt', 'head')), parts along dimension 0, may hold values from -8 to 8
- value_vectors: bfloat16 [1280, 3072], P(('groups', 'seq'), ('wt', 'head')), parts along dimension 0, may hold values from -6 to 6
- out_weight: bfloat16 [3072, 5120], P(('wt', 'head'), 'seq'), may hold values from -0.15625 to 0.15625
- gate_values: float32 [10240], P(('groups', 'wt', 'head')), parts along dimension 0, may hold values from 0.5 to 2
- hidden_state: float32 [1280, 5120], P(('groups', 'seq'), ('wt', 'head')), parts along dimension 0, may hold values from -6 to 6
- cached_deltas: float32 [4, 1280, 5120], P(None, ('groups', 'seq'), ('wt', 'head')), parts along dimension 1, may hold values from -3 to 3
- skip_flags: int32 [8], P('groups'), parts along dimension 0, may hold values from 0 to 1, as said below
Outputs:
- mixed_state: float32 [1280, 5120], P(('groups', 'seq'), ('wt', 'head')), parts along dimension 0
- fresh_delta: float32 [1280, 5120], P(('groups', 'seq'), ('wt', 'head')), parts along dimension 0
The draws below stay inside these ranges and needn't reach their ends.
There are 2 independent parts, one for each index of `groups`. The reference program is written for one: setup_inputs(seed, part) draws one part's arguments, and reference() takes and returns one part's arrays. A program takes and returns all parts, laid end to end along the dimension named above; an argument that names none is the same for every part. Nothing has to cross between parts.
Inputs may be any that keep to these rules, and one draw needn't show every extreme that they name: `skip_flags`: exactly one of the 4 entries is 0, the others are 1.
All inputs are finite; a program needn't handle non-finite values.
Results may differ from the reference program's by a relative error of at most 0.0095.
Values may be sent and summed in bfloat16 or wider, within the bound.
No kernel may reach another device: no remote copies, remote signals or barrier semaphores. Data moves between devices by JAX's collectives and lax.ppermute only.
A program may use at most 64 MiB of HBM per device.

```python
import jax
import jax.numpy as jnp
from jax import lax

D = 5120
HEAD_DIM = 128
HEADS = 24
LAYERS = 4
TOKENS = 640


def draw_queries(key, part):
    key = jax.random.fold_in(key, 1)
    result = jax.random.truncated_normal(key, -4.0, 4.0, (TOKENS, HEADS * HEAD_DIM), jnp.float32)
    return result.astype(jnp.bfloat16)


def draw_key_vectors(key, part):
    key = jax.random.fold_in(key, 2)
    result = 2.0 * jax.random.truncated_normal(key, -4.0, 4.0, (TOKENS, HEADS * HEAD_DIM), jnp.float32)
    return result.astype(jnp.bfloat16)


def draw_skip_flags(key, part):
    key = jax.random.fold_in(key, 5)
    computed = jax.random.randint(key, (), 0, LAYERS)
    return (jnp.arange(LAYERS) != computed).astype(jnp.int32)


def spiked(array, stream_key, source, target, parts, factor):
    def block_of(axis_at):
        return (jnp.arange(array.shape[axis_at]) // (array.shape[axis_at] // parts)).reshape((-1,) + (1,) * (array.ndim - 1 - axis_at))

    near = jax.random.permutation(stream_key, parts)[block_of(target)]
    far = (block_of(target) + parts // 2) % parts
    return jnp.where((block_of(source) == near) | (block_of(source) == far), factor * array, array)


def level_of(key, extent, pieces, low, top_value):
    factor_of, own = 1.0, jax.random.fold_in(key, 6)
    for dim, blocks in pieces:
        draws = jnp.exp(jax.random.uniform(jax.random.fold_in(own, dim), (blocks,), jnp.float32, low / len(pieces), top_value / len(pieces)))
        factor_of = factor_of * jnp.repeat(draws, extent[dim] // blocks).reshape([-1 if axis == dim else 1 for axis in range(len(extent))])
    return factor_of


def scatter_about(rng, dims, deviation, most, shards=(), kind=jnp.bfloat16):
    gain = level_of(rng, dims, shards, -0.22, 0.18) if shards else 1.0
    values = jax.random.normal(rng, dims, jnp.float32) * deviation * gain
    return jnp.minimum(jnp.maximum(values, -most), most).astype(kind)


def noise_with(own_key, extent, spread, limit, shards, heavy, held_as=jnp.bfloat16):
    entries = spread * jax.random.normal(own_key, extent, jnp.float32)
    if shards:
        entries = entries * level_of(own_key, extent, shards, -0.22, 0.18)
    return jnp.clip(spiked(entries, jax.random.fold_in(own_key, 3), *heavy), -limit, limit).astype(held_as)


def setup_inputs(seed: int = 0, part: int = 0) -> dict:
    keys = jax.random.split(jax.random.key(seed), 9)
    own_keys = jax.random.split(jax.random.fold_in(keys[8], part), 9)
    return {
        "queries": draw_queries(jax.random.fold_in(jax.random.fold_in(keys[8], part), 71), part),
        "key_vectors": draw_key_vectors(jax.random.fold_in(jax.random.fold_in(keys[8], part), 71), part),
        "value_vectors": scatter_about(own_keys[2], (TOKENS, HEADS * HEAD_DIM), 1.0, 6.0, ((0, 4), (1, 4))),
        "out_weight": noise_with(keys[3], (HEADS * HEAD_DIM, D), (HEADS * HEAD_DIM) ** -0.5, 0.15625, ((0, 4), (1, 4)), (0, 1, 4, 2.0)),
        "gate_values": jnp.clip(0.5 + 1.5 * jax.random.uniform(own_keys[4], (D,), jnp.float32) ** level_of(own_keys[4], (D,), ((0, 4),), -0.2, 0.2), 0.5, 2.0),
        "hidden_state": scatter_about(own_keys[5], (TOKENS, D), 1.0, 6.0, ((0, 4), (1, 4)), jnp.float32),
        "cached_deltas": scatter_about(own_keys[6], (LAYERS, TOKENS, D), 0.5, 3.0, ((1, 4), (2, 4)), jnp.float32),
        "skip_flags": draw_skip_flags(jax.random.fold_in(jax.random.fold_in(keys[8], part), 71), part),
    }


def one_head(operands):
    query_head, key_head, value_head = operands
    scores = jnp.dot(query_head, key_head.T, preferred_element_type=jnp.float32) * (HEAD_DIM ** -0.5)
    row_peak = jnp.max(scores, axis=1, keepdims=True)
    exp_scores = jnp.exp(scores - row_peak)
    row_total = jnp.sum(exp_scores, axis=1, keepdims=True)
    weighted = jnp.dot(exp_scores.astype(jnp.bfloat16), value_head, preferred_element_type=jnp.float32)
    return (weighted / row_total).astype(jnp.bfloat16)


def split_heads(matrix):
    return matrix.reshape(TOKENS, HEADS, HEAD_DIM).transpose(1, 0, 2)


def reference(queries, key_vectors, value_vectors, out_weight, gate_values, hidden_state, cached_deltas, skip_flags):
    per_head = lax.map(one_head, (split_heads(queries), split_heads(key_vectors), split_heads(value_vectors)))
    attention_out = per_head.transpose(1, 0, 2).reshape(TOKENS, HEADS * HEAD_DIM)
    projected = jnp.dot(attention_out, out_weight, preferred_element_type=jnp.float32)
    fresh_delta = projected * gate_values[None, :]
    kept_deltas = jnp.sum(skip_flags.astype(jnp.float32)[:, None, None] * cached_deltas, axis=0)
    mixed_state = hidden_state + kept_deltas + fresh_delta
    return mixed_state, fresh_delta
```

```python
import functools

import jax
import jax.numpy as jnp
from jax import lax
from jax.experimental import pallas as pl
from jax.experimental.pallas import tpu as pltpu
from jax.sharding import PartitionSpec as P

HEAD_DIM = 128
VMEM_BYTES = 48 * 1024 * 1024


def attend(state_in, key_rows, value_rows, query_heads, score_scale):
    key_count = key_rows.shape[0]
    head_count = query_heads.shape[1]
    blocks = -(-key_count // 1024)
    while key_count % blocks:
        blocks = blocks + 1
    block_size = key_count // blocks

    def one_block(block_index, state_now):
        row_peak, row_total, weighted = state_now
        start_row = block_index * block_size
        key_block = lax.dynamic_slice_in_dim(key_rows, start_row, block_size, 0)
        value_block = lax.dynamic_slice_in_dim(value_rows, start_row, block_size, 0)
        key_heads = key_block.reshape(block_size, head_count, HEAD_DIM)
        value_heads = value_block.reshape(block_size, head_count, HEAD_DIM)
        scores = (
            jnp.einsum("ihd,jhd->hij", query_heads, key_heads, preferred_element_type=jnp.float32)
            * score_scale
        )
        new_peak = jnp.maximum(row_peak, jnp.max(scores, axis=2))
        exp_scores = jnp.exp(scores - new_peak[:, :, None])
        rescale = jnp.exp(row_peak - new_peak)
        row_total = row_total * rescale + jnp.sum(exp_scores, axis=2)
        weighted = weighted * rescale[:, :, None] + jnp.einsum(
            "hij,jhd->hid",
            exp_scores.astype(jnp.bfloat16),
            value_heads,
            preferred_element_type=jnp.float32,
        )
        return (new_peak, row_total, weighted)

    return lax.fori_loop(0, blocks, one_block, state_in)


def finish(state_out, row_count):
    row_peak, row_total, weighted = state_out
    normed = weighted / row_total[:, :, None]
    return normed.transpose(1, 0, 2).reshape(row_count, -1).astype(jnp.bfloat16)


def local_general(
    queries,
    key_vectors,
    value_vectors,
    out_weight,
    gate_values,
    hidden_state,
    cached_deltas,
    skip_flags,
):
    row_count = queries.shape[0]
    head_count = queries.shape[1] // HEAD_DIM
    score_scale = HEAD_DIM ** (-0.5)
    query_heads = queries.reshape(row_count, head_count, HEAD_DIM)
    start_state = (
        jnp.full((head_count, row_count), -1e30, jnp.float32),
        jnp.zeros((head_count, row_count), jnp.float32),
        jnp.zeros((head_count, row_count, HEAD_DIM), jnp.float32),
    )
    gathered_keys, gathered_values, gathered_weight = (
        lax.all_gather(key_vectors, "seq", axis=0, tiled=True),
        lax.all_gather(value_vectors, "seq", axis=0, tiled=True),
        lax.all_gather(out_weight, "seq", axis=1, tiled=True),
    )
    final_state = attend(start_state, gathered_keys, gathered_values, query_heads, score_scale)
    attention_out = finish(final_state, row_count)
    partial_sums = jnp.dot(attention_out, gathered_weight, preferred_element_type=jnp.float32)
    head_total = lax.psum_scatter(
        partial_sums.astype(jnp.bfloat16), ("wt", "head"), scatter_dimension=1, tiled=True
    ).astype(jnp.float32)
    fresh_delta = head_total * gate_values[None, :]
    kept_deltas = jnp.sum(skip_flags.astype(jnp.float32)[:, None, None] * cached_deltas, axis=0)
    mixed_state = hidden_state + kept_deltas + fresh_delta
    return (mixed_state, fresh_delta)


def pack_kernel(place, queries, keys, values, *outs):
    half, width = outs[0].shape[0] // 2, outs[0].shape[1]
    for k in range(4):
        rows = pl.ds(pl.multiple_of(place[2 * k], 16), half)
        columns = pl.ds(pl.multiple_of(place[2 * k + 1], 128), width)
        outs[k][:half, :] = keys[rows, columns]
        outs[k][half:, :] = values[rows, columns]
        outs[4 + k][...] = queries[rows, columns]


def attention_kernel(place, *refs):
    kv_blocks, query_blocks = refs[:8], refs[8:12]
    own, other, key_all, value_all, query_all, both = refs[12:]
    half = query_blocks[0].shape[0]
    for k in range(8):
        key_all[k * half : (k + 1) * half, :] = kv_blocks[k][:half, :]
        value_all[k * half : (k + 1) * half, :] = kv_blocks[k][half:, :]
    for k in range(4):
        query_all[k * half : (k + 1) * half, :] = query_blocks[k][...]
    for h in range(own.shape[1] // HEAD_DIM):
        columns = slice(h * HEAD_DIM, (h + 1) * HEAD_DIM)
        scores = lax.dot_general(
            query_all[:, columns],
            key_all[:, columns],
            (((1,), (1,)), ((), ())),
            preferred_element_type=jnp.float32,
        ) * (HEAD_DIM ** (-0.5))
        weights = jnp.exp(scores - jnp.max(scores, axis=1, keepdims=True))
        total = jnp.sum(weights, axis=1, keepdims=True)
        result = jnp.dot(
            weights.astype(jnp.bfloat16), value_all[:, columns], preferred_element_type=jnp.float32
        )
        result = (result / total).astype(jnp.bfloat16)
        for k in range(4):
            both[place[2 * k], pl.ds(pl.multiple_of(place[2 * k + 1], 16), half), columns] = result[
                k * half : (k + 1) * half
            ]
    own[...] = both[0]
    other[...] = both[1]


def project_kernel(place, *refs):
    shards, weights = refs[:10], refs[10:14]
    out0, out1, held, weight_held, total, sems = refs[14:]
    copies = [
        pltpu.make_async_copy(weights[b], weight_held.at[b], sems.at[b]) for b in range(4)
    ]
    for copy in copies:
        copy.start()
    for side in range(2):
        for m in range(3):
            held[side, m] = shards[2 * m + side][...]
        far = place[4] == 1

        @pl.when(far)
        def _():
            held[side, 3] = shards[8 + side][...]

        @pl.when(jnp.logical_not(far))
        def _():
            held[side, 3] = shards[6 + side][...]

    width = held.shape[3]
    for b in range(4):
        side, other_core = b // 2, b % 2
        copies[b].wait()
        part = jnp.dot(
            held[side, place[2 * other_core]],
            weight_held[b, :width, :],
            preferred_element_type=jnp.float32,
        )
        part = part + jnp.dot(
            held[side, place[2 * other_core + 1]],
            weight_held[b, width:, :],
            preferred_element_type=jnp.float32,
        )
        if b == 0:
            total[...] = part
        else:
            total[...] += part
    half = out0.shape[0]
    first = pl.ds(pl.multiple_of(place[5], 16), half)
    second = pl.ds(pl.multiple_of(half - place[5], 16), half)
    out0[...] = total[first, :].astype(out0.dtype)
    out1[...] = total[second, :].astype(out1.dtype)


def call(kernel, place, args, outs, scratch=(), in_any=(), cost=None):
    specs = [pl.BlockSpec(memory_space=pltpu.SMEM)]
    for i, _ in enumerate(args):
        specs.append(pl.BlockSpec(memory_space=pl.ANY if i in in_any else pltpu.VMEM))
    return pl.pallas_call(
        kernel,
        in_specs=specs,
        out_specs=[pl.BlockSpec(memory_space=pltpu.VMEM)] * len(outs),
        out_shape=[jax.ShapeDtypeStruct(shape, jnp.bfloat16) for shape in outs],
        scratch_shapes=list(scratch),
        compiler_params=pltpu.CompilerParams(vmem_limit_bytes=VMEM_BYTES),
        cost_estimate=cost,
    )(place, *args)


def scalars(*values):
    return jnp.stack([jnp.asarray(v, jnp.int32) for v in values])


def local_heads(
    queries,
    key_vectors,
    value_vectors,
    out_weight,
    gate_values,
    hidden_state,
    cached_deltas,
    skip_flags,
):
    rows, features = queries.shape
    half, width = rows // 2, features // 2
    z, x, c = lax.axis_index("seq"), lax.axis_index("wt"), lax.axis_index("head")
    zh, zl = z // 2, z % 2
    swap = [(0, 1), (1, 0)]

    weight_x = lax.ppermute(out_weight, "wt", swap)
    weight_c = lax.ppermute(out_weight, "head", swap)
    weight_xc = lax.ppermute(weight_x, "head", swap)

    place = []
    for k in range(4):
        k1, k0 = k // 2, k % 2
        place += [(zh ^ k1) * half, (zl ^ k0) * width]
    packed = call(
        pack_kernel,
        scalars(*place),
        (queries, key_vectors, value_vectors),
        [(rows, width)] * 4 + [(half, width)] * 4,
    )
    moved = []
    for order in range(2):
        for k in range(4):
            k1, k0 = k // 2, k % 2
            pairs = []
            for zz in range(4):
                for cc in range(2):
                    to_z = 2 * cc + ((zz % 2) ^ k0)
                    pairs.append((zz * 2 + cc, to_z * 2 + ((zz // 2) ^ k1)))
            moved.append(lax.ppermute(packed[4 * order + k], ("seq", "head"), pairs))
    kv_blocks, query_blocks = moved[:4], moved[4:]
    kv_sibling = [lax.ppermute(block, "head", swap) for block in kv_blocks]

    place = []
    for k in range(4):
        k1, k0 = k // 2, k % 2
        place += [zl ^ k0 ^ x, (c ^ k1) * half]
    own, other = call(
        attention_kernel,
        scalars(*place),
        kv_blocks + kv_sibling + query_blocks,
        [(rows, width)] * 2,
        [
            pltpu.VMEM((4 * rows, width), jnp.bfloat16),
            pltpu.VMEM((4 * rows, width), jnp.bfloat16),
            pltpu.VMEM((2 * rows, width), jnp.bfloat16),
            pltpu.VMEM((2, rows, width), jnp.bfloat16),
        ],
    )
    cross = lax.ppermute(other, "wt", swap)

    shards = []
    for shard in (own, cross):
        near = lax.ppermute(shard, "seq", [(0, 1), (1, 0), (2, 3), (3, 2)])
        two = lax.ppermute(shard, "seq", [(0, 2), (2, 0), (1, 3), (3, 1)])
        middle = lax.ppermute(shard, "seq", [(1, 2), (2, 1)])
        ends = lax.ppermute(two, "seq", [(1, 0), (2, 3)])
        shards.append([shard, near, two, middle, ends])
    flat = [shards[side][m] for m in range(5) for side in range(2)]

    place = []
    for other_core in range(2):
        for low in range(2):
            place.append((2 * (c ^ other_core) + low) ^ z)
    place += [(zh == zl).astype(jnp.int32), c * half]
    depth, columns = out_weight.shape
    out0, out1 = call(
        project_kernel,
        scalars(*place),
        flat + [out_weight, weight_c, weight_x, weight_xc],
        [(half, columns)] * 2,
        [
            pltpu.VMEM((2, 4, rows, width), jnp.bfloat16),
            pltpu.VMEM((4, depth, columns), jnp.bfloat16),
            pltpu.VMEM((rows, columns), jnp.float32),
            pltpu.SemaphoreType.DMA((4,)),
        ],
        in_any=range(10, 14),
    )

    arrived = []
    for p, block in enumerate((out0, out1)):
        pairs = []
        for zz in range(4):
            for xx in range(2):
                for cc in range(2):
                    to = ((2 * (p ^ cc) + xx) * 2 + zz // 2) * 2 + zz % 2
                    pairs.append(((zz * 2 + xx) * 2 + cc, to))
        arrived.append(lax.ppermute(block, ("seq", "wt", "head"), pairs))
    straight = zh == 0
    head_total = jnp.concatenate(
        [
            jnp.where(straight, arrived[0], arrived[1]),
            jnp.where(straight, arrived[1], arrived[0]),
        ],
        axis=0,
    ).astype(jnp.float32)
    kept_deltas = jnp.sum(skip_flags.astype(jnp.float32)[:, None, None] * cached_deltas, axis=0)
    resting = hidden_state + kept_deltas
    fresh_delta = head_total * gate_values[None, :]
    mixed_state = resting + fresh_delta
    return (mixed_state, fresh_delta)


def solution(mesh):
    placed = (
        P(("groups", "seq"), ("wt", "head")),
        P(("groups", "seq"), ("wt", "head")),
        P(("groups", "seq"), ("wt", "head")),
        P(("wt", "head"), "seq"),
        P(("groups", "wt", "head")),
        P(("groups", "seq"), ("wt", "head")),
        P(None, ("groups", "seq"), ("wt", "head")),
        P("groups"),
    )

    def local(*args):
        sizes = tuple(mesh.shape[name] for name in ("seq", "wt", "head"))
        rows, features = args[0].shape
        if sizes == (4, 2, 2) and rows % 32 == 0 and features % (2 * HEAD_DIM) == 0:
            return local_heads(*args)
        return local_general(*args)

    return jax.shard_map(
        local,
        mesh=mesh,
        in_specs=placed,
        out_specs=(P(("groups", "seq"), ("wt", "head")), P(("groups", "seq"), ("wt", "head"))),
        check_vma=False,
    )
```

```python
import functools

import jax
import jax.numpy as jnp
from jax import lax
from jax.experimental import pallas as pl
from jax.experimental.pallas import tpu as pltpu
from jax.sharding import PartitionSpec as P

HEAD_DIM = 128
VMEM_BYTES = 16 * 1024 * 1024


def attend(state_in, key_rows, value_rows, query_heads, score_scale):
    key_count = key_rows.shape[0]
    head_count = query_heads.shape[1]
    blocks = -(-key_count // 1024)
    while key_count % blocks:
        blocks = blocks + 1
    block_size = key_count // blocks

    def one_block(block_index, state_now):
        row_peak, row_total, weighted = state_now
        start_row = block_index * block_size
        key_block = lax.dynamic_slice_in_dim(key_rows, start_row, block_size, 0)
        value_block = lax.dynamic_slice_in_dim(value_rows, start_row, block_size, 0)
        key_heads = key_block.reshape(block_size, head_count, HEAD_DIM)
        value_heads = value_block.reshape(block_size, head_count, HEAD_DIM)
        scores = (
            jnp.einsum("ihd,jhd->hij", query_heads, key_heads, preferred_element_type=jnp.float32)
            * score_scale
        )
        new_peak = jnp.maximum(row_peak, jnp.max(scores, axis=2))
        exp_scores = jnp.exp(scores - new_peak[:, :, None])
        rescale = jnp.exp(row_peak - new_peak)
        row_total = row_total * rescale + jnp.sum(exp_scores, axis=2)
        weighted = weighted * rescale[:, :, None] + jnp.einsum(
            "hij,jhd->hid",
            exp_scores.astype(jnp.bfloat16),
            value_heads,
            preferred_element_type=jnp.float32,
        )
        return (new_peak, row_total, weighted)

    return lax.fori_loop(0, blocks, one_block, state_in)


def finish(state_out, row_count):
    row_peak, row_total, weighted = state_out
    normed = weighted / row_total[:, :, None]
    return normed.transpose(1, 0, 2).reshape(row_count, -1).astype(jnp.bfloat16)


def local_general(
    queries,
    key_vectors,
    value_vectors,
    out_weight,
    gate_values,
    hidden_state,
    cached_deltas,
    skip_flags,
):
    row_count = queries.shape[0]
    head_count = queries.shape[1] // HEAD_DIM
    score_scale = HEAD_DIM ** (-0.5)
    query_heads = queries.reshape(row_count, head_count, HEAD_DIM)
    start_state = (
        jnp.full((head_count, row_count), -1e30, jnp.float32),
        jnp.zeros((head_count, row_count), jnp.float32),
        jnp.zeros((head_count, row_count, HEAD_DIM), jnp.float32),
    )
    gathered_keys, gathered_values, gathered_weight = (
        lax.all_gather(key_vectors, "seq", axis=0, tiled=True),
        lax.all_gather(value_vectors, "seq", axis=0, tiled=True),
        lax.all_gather(out_weight, "seq", axis=1, tiled=True),
    )
    final_state = attend(start_state, gathered_keys, gathered_values, query_heads, score_scale)
    attention_out = finish(final_state, row_count)
    partial_sums = jnp.dot(attention_out, gathered_weight, preferred_element_type=jnp.float32)
    head_total = lax.psum_scatter(
        partial_sums.astype(jnp.bfloat16), ("wt", "head"), scatter_dimension=1, tiled=True
    ).astype(jnp.float32)
    fresh_delta = head_total * gate_values[None, :]
    kept_deltas = jnp.sum(skip_flags.astype(jnp.float32)[:, None, None] * cached_deltas, axis=0)
    mixed_state = hidden_state + kept_deltas + fresh_delta
    return (mixed_state, fresh_delta)


def pack_kernel(place, queries, keys, values, *refs):
    outs, sems = refs[:4], refs[4]
    half, width = outs[0].shape[0] // 3, outs[0].shape[1]
    copies = []
    for k in range(4):
        rows = pl.ds(pl.multiple_of(place[2 * k], 16), half)
        columns = pl.ds(pl.multiple_of(place[2 * k + 1], 128), width)
        for i, source in enumerate((keys, values, queries)):
            copies.append(
                pltpu.make_async_copy(
                    source.at[rows, columns],
                    outs[k].at[pl.ds(i * half, half), :],
                    sems.at[3 * k + i],
                )
            )
    for copy in copies:
        copy.start()
    for copy in copies:
        copy.wait()


def join_kernel(place, *refs):
    blocks, joined = refs[:-1], refs[-1]
    rows = joined.shape[0] // len(blocks)
    for k, block in enumerate(blocks):
        joined[k * rows : (k + 1) * rows, :] = block[:rows, :]


def attention_kernel(place, *refs):
    blocks, sibling = refs[:4], refs[4]
    own, other, key_all, value_all, query_all, both = refs[5:]
    half = blocks[0].shape[0] // 3
    for k in range(4):
        key_all[k * half : (k + 1) * half, :] = blocks[k][:half, :]
        value_all[k * half : (k + 1) * half, :] = blocks[k][half : 2 * half, :]
        query_all[k * half : (k + 1) * half, :] = blocks[k][2 * half :, :]
        key_all[(4 + k) * half : (5 + k) * half, :] = sibling[2 * k * half : (2 * k + 1) * half, :]
        value_all[(4 + k) * half : (5 + k) * half, :] = sibling[
            (2 * k + 1) * half : (2 * k + 2) * half, :
        ]
    for h in range(own.shape[1] // HEAD_DIM):
        columns = slice(h * HEAD_DIM, (h + 1) * HEAD_DIM)
        scores = lax.dot_general(
            query_all[:, columns],
            key_all[:, columns],
            (((1,), (1,)), ((), ())),
            preferred_element_type=jnp.float32,
        ) * (HEAD_DIM ** (-0.5))
        weights = jnp.exp(scores - jnp.max(scores, axis=1, keepdims=True))
        total = jnp.sum(weights, axis=1, keepdims=True)
        result = jnp.dot(
            weights.astype(jnp.bfloat16), value_all[:, columns], preferred_element_type=jnp.float32
        )
        result = (result / total).astype(jnp.bfloat16)
        for k in range(4):
            both[place[2 * k], pl.ds(pl.multiple_of(place[2 * k + 1], 16), half), columns] = result[
                k * half : (k + 1) * half
            ]
    own[...] = both[0]
    other[...] = both[1]


def add_term(total, left, pick, row, first, second):
    rows = pl.ds(pl.multiple_of(row, 128), left.shape[1])
    for value, weight in enumerate((first, second)):

        @pl.when(pick == value)
        def _():
            total[...] += jnp.dot(left, weight[rows, :], preferred_element_type=jnp.float32)


def early_kernel(place, own, near, two, weight, weight_c, total):
    width = own.shape[1] // 2
    total[...] = jnp.zeros_like(total)
    for m, shard in enumerate((own, near, two)):
        add_term(total, shard[:, :width], place[2 * m], place[2 * m + 1], weight, weight_c)


def late_kernel(place, *refs):
    total_in, shards, weights = refs[0], refs[1:6], refs[6:12]
    out0, out1, held, left, total = refs[12:]
    far = jnp.where(place[5] == 1, shards[4][...], shards[3][...])
    width = far.shape[1] // 2
    for m in range(3):
        held[m] = shards[m][:, width:]
    held[3] = far[:, width:]
    total[...] = total_in[...]
    add_term(total, far[:, :width], place[6], place[7], weights[0], weights[1])
    for b in range(2):
        for low in range(2):
            left[b, :, low * width : (low + 1) * width] = held[place[2 * b + low]]
        row = 0
        for block in weights[2 + 2 * b : 4 + 2 * b]:
            total[...] += jnp.dot(
                left[b, :, row : row + block.shape[0]],
                block[...],
                preferred_element_type=jnp.float32,
            )
            row += block.shape[0]
    half = out0.shape[0]
    first = pl.ds(pl.multiple_of(place[4], 16), half)
    second = pl.ds(pl.multiple_of(half - place[4], 16), half)
    out0[...] = total[first, :].astype(out0.dtype)
    out1[...] = total[second, :].astype(out1.dtype)


def call(kernel, place, args, outs, scratch=(), in_any=(), vmem=VMEM_BYTES, dtype=jnp.bfloat16, flops=0):
    specs = [pl.BlockSpec(memory_space=pltpu.SMEM)]
    for i, _ in enumerate(args):
        specs.append(pl.BlockSpec(memory_space=pltpu.HBM if i in in_any else pltpu.VMEM))
    return pl.pallas_call(
        kernel,
        in_specs=specs,
        out_specs=[pl.BlockSpec(memory_space=pltpu.VMEM)] * len(outs),
        out_shape=[jax.ShapeDtypeStruct(shape, dtype) for shape in outs],
        scratch_shapes=list(scratch),
        compiler_params=pltpu.CompilerParams(vmem_limit_bytes=vmem),
        cost_estimate=pl.CostEstimate(flops=flops, bytes_accessed=0, transcendentals=0),
    )(place, *args)


def scalars(*values):
    return jnp.stack([jnp.asarray(v, jnp.int32) for v in values])


def local_heads(
    queries,
    key_vectors,
    value_vectors,
    out_weight,
    gate_values,
    hidden_state,
    cached_deltas,
    skip_flags,
):
    rows, features = queries.shape
    half, width = rows // 2, features // 2
    z, x, c = lax.axis_index("seq"), lax.axis_index("wt"), lax.axis_index("head")
    zh, zl = z // 2, z % 2
    swap = [(0, 1), (1, 0)]

    depth, columns = out_weight.shape
    cut = depth * 2 // 3 // HEAD_DIM * HEAD_DIM
    weight_x0 = lax.ppermute(out_weight[:cut], "wt", swap)
    weight_x1 = lax.ppermute(out_weight[cut:], "wt", swap)

    place = []
    for k in range(4):
        k1, k0 = k // 2, k % 2
        place += [(zh ^ k1) * half, (zl ^ k0) * width]
    packed = call(
        pack_kernel,
        scalars(*place),
        (queries, key_vectors, value_vectors),
        [(3 * half, width)] * 4,
        [pltpu.SemaphoreType.DMA((12,))],
        in_any=range(3),
        vmem=60 * 1024 * 1024,
    )
    moved = []
    for k in range(4):
        k1, k0 = k // 2, k % 2
        pairs = []
        for zz in range(4):
            for cc in range(2):
                to_z = 2 * cc + ((zz % 2) ^ k0)
                pairs.append((zz * 2 + cc, to_z * 2 + ((zz // 2) ^ k1)))
        moved.append(lax.ppermute(packed[k], ("seq", "head"), pairs))
    (joined,) = call(join_kernel, scalars(0), moved, [(4 * rows, width)])
    sibling = lax.ppermute(joined, "head", swap)

    place = []
    for k in range(4):
        k1, k0 = k // 2, k % 2
        place += [zl ^ k0 ^ x, (c ^ k1) * half]
    own, other = call(
        attention_kernel,
        scalars(*place),
        moved + [sibling],
        [(rows, width)] * 2,
        [
            pltpu.VMEM((4 * rows, width), jnp.bfloat16),
            pltpu.VMEM((4 * rows, width), jnp.bfloat16),
            pltpu.VMEM((2 * rows, width), jnp.bfloat16),
            pltpu.VMEM((2, rows, width), jnp.bfloat16),
        ],
        flops=4 * (2 * rows) * (4 * rows) * width,
    )
    cross = lax.ppermute(other, "wt", swap)

    shard = jnp.concatenate([own, cross], axis=1)
    near = lax.ppermute(shard, "seq", [(0, 1), (1, 0), (2, 3), (3, 2)])
    two = lax.ppermute(shard, "seq", [(0, 2), (2, 0), (1, 3), (3, 1)])
    late_c, _ = lax.optimization_barrier((out_weight, cross))
    weight_c = lax.ppermute(late_c, "head", swap)
    late_shard, late_two, _ = lax.optimization_barrier((shard, two, near))
    middle = lax.ppermute(late_shard, "seq", [(1, 2), (2, 1)])
    ends = lax.ppermute(late_two, "seq", [(1, 0), (2, 3)])
    place = []
    for m in range(4):
        place += [(zh ^ (m // 2)) ^ c, (zl ^ (m % 2)) * width]
    (early,) = call(
        early_kernel,
        scalars(*place[:6]),
        (shard, near, two, out_weight, weight_c),
        [(rows, columns)],
        dtype=jnp.float32,
        flops=6 * rows * width * columns,
    )
    late_x0, _ = lax.optimization_barrier((weight_x0, cross))
    late_x1, _, _ = lax.optimization_barrier((weight_x1, middle, ends))
    weight_xc0 = lax.ppermute(late_x0, "head", swap)
    weight_xc1 = lax.ppermute(late_x1, "head", swap)
    late_place = [(2 * (c ^ b) + low) ^ z for b in range(2) for low in range(2)]
    late_place += [c * half, (zh == zl).astype(jnp.int32)] + place[6:]
    out0, out1 = call(
        late_kernel,
        scalars(*late_place),
        [early, shard, near, two, middle, ends, out_weight, weight_c]
        + [weight_x0, weight_x1, weight_xc0, weight_xc1],
        [(half, columns)] * 2,
        [
            pltpu.VMEM((4, rows, width), jnp.bfloat16),
            pltpu.VMEM((2, rows, 2 * width), jnp.bfloat16),
            pltpu.VMEM((rows, columns), jnp.float32),
        ],
        flops=10 * rows * width * columns,
    )

    arrived = []
    for p, block in enumerate((out0, out1)):
        pairs = []
        for zz in range(4):
            for xx in range(2):
                for cc in range(2):
                    to = ((2 * (p ^ cc) + xx) * 2 + zz // 2) * 2 + zz % 2
                    pairs.append(((zz * 2 + xx) * 2 + cc, to))
        arrived.append(lax.ppermute(block, ("seq", "wt", "head"), pairs))
    straight = zh == 0
    head_total = jnp.concatenate(
        [
            jnp.where(straight, arrived[0], arrived[1]),
            jnp.where(straight, arrived[1], arrived[0]),
        ],
        axis=0,
    ).astype(jnp.float32)
    kept_deltas = jnp.sum(skip_flags.astype(jnp.float32)[:, None, None] * cached_deltas, axis=0)
    resting = hidden_state + kept_deltas
    fresh_delta = head_total * gate_values[None, :]
    mixed_state = resting + fresh_delta
    return (mixed_state, fresh_delta)


def solution(mesh):
    placed = (
        P(("groups", "seq"), ("wt", "head")),
        P(("groups", "seq"), ("wt", "head")),
        P(("groups", "seq"), ("wt", "head")),
        P(("wt", "head"), "seq"),
        P(("groups", "wt", "head")),
        P(("groups", "seq"), ("wt", "head")),
        P(None, ("groups", "seq"), ("wt", "head")),
        P("groups"),
    )

    def local(*args):
        sizes = tuple(mesh.shape[name] for name in ("seq", "wt", "head"))
        rows, features = args[0].shape
        if sizes == (4, 2, 2) and rows % 32 == 0 and features % (2 * HEAD_DIM) == 0:
            return local_heads(*args)
        return local_general(*args)

    return jax.shard_map(
        local,
        mesh=mesh,
        in_specs=placed,
        out_specs=(P(("groups", "seq"), ("wt", "head")), P(("groups", "seq"), ("wt", "head"))),
        check_vma=False,
    )
```

```python
import functools

import jax
import jax.numpy as jnp
from jax import lax
from jax.experimental import pallas as pl
from jax.experimental.pallas import tpu as pltpu
from jax.sharding import PartitionSpec as P

HEAD_DIM = 128
VMEM_BYTES = 48 * 1024 * 1024


def attend(state_in, key_rows, value_rows, query_heads, score_scale):
    key_count = key_rows.shape[0]
    head_count = query_heads.shape[1]
    blocks = -(-key_count // 1024)
    while key_count % blocks:
        blocks = blocks + 1
    block_size = key_count // blocks

    def one_block(block_index, state_now):
        row_peak, row_total, weighted = state_now
        start_row = block_index * block_size
        key_block = lax.dynamic_slice_in_dim(key_rows, start_row, block_size, 0)
        value_block = lax.dynamic_slice_in_dim(value_rows, start_row, block_size, 0)
        key_heads = key_block.reshape(block_size, head_count, HEAD_DIM)
        value_heads = value_block.reshape(block_size, head_count, HEAD_DIM)
        scores = (
            jnp.einsum("ihd,jhd->hij", query_heads, key_heads, preferred_element_type=jnp.float32)
            * score_scale
        )
        new_peak = jnp.maximum(row_peak, jnp.max(scores, axis=2))
        exp_scores = jnp.exp(scores - new_peak[:, :, None])
        rescale = jnp.exp(row_peak - new_peak)
        row_total = row_total * rescale + jnp.sum(exp_scores, axis=2)
        weighted = weighted * rescale[:, :, None] + jnp.einsum(
            "hij,jhd->hid",
            exp_scores.astype(jnp.bfloat16),
            value_heads,
            preferred_element_type=jnp.float32,
        )
        return (new_peak, row_total, weighted)

    return lax.fori_loop(0, blocks, one_block, state_in)


def finish(state_out, row_count):
    row_peak, row_total, weighted = state_out
    normed = weighted / row_total[:, :, None]
    return normed.transpose(1, 0, 2).reshape(row_count, -1).astype(jnp.bfloat16)


def local_general(
    queries,
    key_vectors,
    value_vectors,
    out_weight,
    gate_values,
    hidden_state,
    cached_deltas,
    skip_flags,
):
    row_count = queries.shape[0]
    head_count = queries.shape[1] // HEAD_DIM
    score_scale = HEAD_DIM ** (-0.5)
    query_heads = queries.reshape(row_count, head_count, HEAD_DIM)
    start_state = (
        jnp.full((head_count, row_count), -1e30, jnp.float32),
        jnp.zeros((head_count, row_count), jnp.float32),
        jnp.zeros((head_count, row_count, HEAD_DIM), jnp.float32),
    )
    gathered_keys, gathered_values, gathered_weight = (
        lax.all_gather(key_vectors, "seq", axis=0, tiled=True),
        lax.all_gather(value_vectors, "seq", axis=0, tiled=True),
        lax.all_gather(out_weight, "seq", axis=1, tiled=True),
    )
    final_state = attend(start_state, gathered_keys, gathered_values, query_heads, score_scale)
    attention_out = finish(final_state, row_count)
    partial_sums = jnp.dot(attention_out, gathered_weight, preferred_element_type=jnp.float32)
    head_total = lax.psum_scatter(
        partial_sums.astype(jnp.bfloat16), ("wt", "head"), scatter_dimension=1, tiled=True
    ).astype(jnp.float32)
    fresh_delta = head_total * gate_values[None, :]
    kept_deltas = jnp.sum(skip_flags.astype(jnp.float32)[:, None, None] * cached_deltas, axis=0)
    mixed_state = hidden_state + kept_deltas + fresh_delta
    return (mixed_state, fresh_delta)


def bits():
    z = lax.axis_index("seq")
    return lax.div(z, 2), lax.rem(z, 2)


def flip(bit, value):
    return 1 - bit if value else bit


def run(copies):
    for copy in copies:
        copy.start()
    for copy in copies:
        copy.wait()


def pack_kernel(queries, keys, values, *refs):
    outs, sems = refs[:4], refs[4]
    half, width = outs[0].shape[0] // 3, outs[0].shape[1]
    zh, zl = bits()
    copies = []
    for k in range(4):
        rows = pl.ds(pl.multiple_of(flip(zh, k // 2) * half, 16), half)
        columns = pl.ds(pl.multiple_of(flip(zl, k % 2) * width, 128), width)
        for i, source in enumerate((keys, values, queries)):
            copies.append(
                pltpu.make_async_copy(
                    source.at[rows, columns],
                    outs[k].at[pl.ds(i * half, half), :],
                    sems.at[3 * k + i],
                )
            )
    run(copies)


def join_kernel(*refs):
    blocks, joined, sems = refs[:4], refs[4], refs[5]
    rows = joined.shape[0] // 4
    run(
        [
            pltpu.make_async_copy(
                block.at[pl.ds(0, rows), :], joined.at[pl.ds(k * rows, rows), :], sems.at[k]
            )
            for k, block in enumerate(blocks)
        ]
    )


def attention_kernel(*refs):
    blocks, sibling, out = refs[:4], refs[4], refs[5]
    key_all, value_all, query_all, sems = refs[6:]
    half = blocks[0].shape[0] // 3
    _, zl = bits()
    core = lax.axis_index("head")

    def rows(k):
        return pl.ds(k * half, half)

    copies = []
    for k in range(4):
        source = 2 * flip(core, k // 2) + flip(zl, k % 2)
        at = pl.ds(pl.multiple_of(source * half, 16), half)
        parts = (
            (blocks[k].at[rows(0), :], key_all.at[rows(k), :]),
            (blocks[k].at[rows(1), :], value_all.at[rows(k), :]),
            (blocks[k].at[rows(2), :], query_all.at[at, :]),
            (sibling.at[rows(2 * k), :], key_all.at[rows(4 + k), :]),
            (sibling.at[rows(2 * k + 1), :], value_all.at[rows(4 + k), :]),
        )
        for i, (start, end) in enumerate(parts):
            copies.append(pltpu.make_async_copy(start, end, sems.at[5 * k + i]))
    run(copies)
    for h in range(out.shape[1] // HEAD_DIM):
        columns = slice(h * HEAD_DIM, (h + 1) * HEAD_DIM)
        scores = lax.dot_general(
            query_all[:, columns],
            key_all[:, columns],
            (((1,), (1,)), ((), ())),
            preferred_element_type=jnp.float32,
        ) * (HEAD_DIM ** (-0.5))
        weights = jnp.exp(scores - jnp.max(scores, axis=1, keepdims=True))
        total = jnp.sum(weights, axis=1, keepdims=True)
        result = jnp.dot(
            weights.astype(jnp.bfloat16), value_all[:, columns], preferred_element_type=jnp.float32
        )
        out[:, columns] = (result / total).astype(out.dtype)


def project_kernel(gathered, weight, weight_c, *refs):
    keeps, sends = refs[0:2], refs[2:4]
    left, rights, total, sems = refs[4:]
    rows, depth = left.shape[1], weight.shape[0]
    core, x = lax.axis_index("head"), lax.axis_index("wt")
    copies = [
        pltpu.make_async_copy(weight, rights.at[core], sems.at[0]),
        pltpu.make_async_copy(weight_c, rights.at[1 - core], sems.at[1]),
    ]
    for m in range(4):
        copies.append(
            pltpu.make_async_copy(gathered.at[pl.ds(m * rows, rows), :], left.at[m], sems.at[2 + m])
        )
    run(copies)
    block = rows // 4
    count = sends[0].shape[1]
    for h in range(2):
        columns = slice(h * count, (h + 1) * count)
        for m in range(4):
            term = jnp.dot(
                left[m],
                rights[m // 2, (m % 2) * depth // 2 : (m % 2 + 1) * depth // 2, columns],
                preferred_element_type=jnp.float32,
            )
            if m == 0:
                total[...] = term
            else:
                total[...] += term
        for high in range(2):
            kept = pl.ds(pl.multiple_of((2 * high + x) * block, 16), block)
            sent = pl.ds(pl.multiple_of((2 * high + 1 - x) * block, 16), block)
            at = slice(high * block, (high + 1) * block)
            keeps[h][at, :] = total[kept, :]
            sends[h][at, :] = total[sent, :].astype(sends[h].dtype)


def add_kernel(keep, arrived, out0, out1):
    half = out0.shape[0]
    core = lax.axis_index("head")
    first = pl.ds(pl.multiple_of(core * half, 16), half)
    second = pl.ds(pl.multiple_of((1 - core) * half, 16), half)
    for out, at in ((out0, first), (out1, second)):
        out[...] = (keep[at, :] + arrived[at, :].astype(jnp.float32)).astype(out.dtype)


def call(kernel, args, outs, scratch=(), far_in=True, far_out=False, flops=0, vmem=VMEM_BYTES):
    place = {True: pl.ANY, False: pltpu.VMEM}
    return pl.pallas_call(
        kernel,
        in_specs=[pl.BlockSpec(memory_space=place[far_in])] * len(args),
        out_specs=[pl.BlockSpec(memory_space=place[far_out])] * len(outs),
        out_shape=[jax.ShapeDtypeStruct(shape, dtype) for shape, dtype in outs],
        scratch_shapes=list(scratch),
        compiler_params=pltpu.CompilerParams(vmem_limit_bytes=vmem),
        cost_estimate=pl.CostEstimate(flops=flops, bytes_accessed=0, transcendentals=0),
    )(*args)


def local_heads(
    queries,
    key_vectors,
    value_vectors,
    out_weight,
    gate_values,
    hidden_state,
    cached_deltas,
    skip_flags,
):
    rows, features = queries.shape
    half, width = rows // 2, features // 2
    depth, columns = out_weight.shape
    count = columns // 2
    zh = lax.axis_index("seq") // 2
    swap = [(0, 1), (1, 0)]
    bf16 = jnp.bfloat16

    weight_c = lax.ppermute(out_weight, "head", swap)

    packed = call(
        pack_kernel,
        (queries, key_vectors, value_vectors),
        [((3 * half, width), bf16)] * 4,
        [pltpu.SemaphoreType.DMA((12,))],
        far_out=True,
        vmem=60 * 1024 * 1024,
    )
    moved = []
    for k in range(4):
        k1, k0 = k // 2, k % 2
        pairs = []
        for zz in range(4):
            for cc in range(2):
                to_z = 2 * cc + ((zz % 2) ^ k0)
                pairs.append((zz * 2 + cc, to_z * 2 + ((zz // 2) ^ k1)))
        moved.append(lax.ppermute(packed[k], ("seq", "head"), pairs))
    (joined,) = call(
        join_kernel,
        moved,
        [((4 * rows, width), bf16)],
        [pltpu.SemaphoreType.DMA((4,))],
        far_out=True,
    )
    sibling = lax.ppermute(joined, "head", swap)
    (attention_out,) = call(
        attention_kernel,
        moved + [sibling],
        [((2 * rows, width), bf16)],
        [
            pltpu.VMEM((4 * rows, width), bf16),
            pltpu.VMEM((4 * rows, width), bf16),
            pltpu.VMEM((2 * rows, width), bf16),
            pltpu.SemaphoreType.DMA((20,)),
        ],
        flops=4 * (2 * rows) * (4 * rows) * width,
    )
    gathered = lax.all_gather(attention_out, "seq", axis=0, tiled=True)

    outs = call(
        project_kernel,
        (gathered, out_weight, weight_c),
        [((rows, count), jnp.float32)] * 2 + [((rows, count), bf16)] * 2,
        [
            pltpu.VMEM((4, 2 * rows, width), bf16),
            pltpu.VMEM((2, depth, columns), bf16),
            pltpu.VMEM((2 * rows, count), jnp.float32),
            pltpu.SemaphoreType.DMA((6,)),
        ],
        flops=4 * (2 * rows) * depth * columns,
    )
    summed = []
    for keep, send in zip(outs[:2], outs[2:]):
        arrived = lax.ppermute(send, "wt", swap)
        pieces = call(add_kernel, (keep, arrived), [((half, count), bf16)] * 2, far_in=False)
        owned = []
        for p, piece in enumerate(pieces):
            pairs = []
            for zz in range(4):
                for xx in range(2):
                    for cc in range(2):
                        to = ((2 * (p ^ cc) + xx) * 2 + zz // 2) * 2 + zz % 2
                        pairs.append(((zz * 2 + xx) * 2 + cc, to))
            owned.append(lax.ppermute(piece, ("seq", "wt", "head"), pairs))
        straight = zh == 0
        summed.append(
            jnp.concatenate(
                [
                    jnp.where(straight, owned[0], owned[1]),
                    jnp.where(straight, owned[1], owned[0]),
                ],
                axis=0,
            )
        )
    head_total = jnp.concatenate(summed, axis=1).astype(jnp.float32)
    kept_deltas = jnp.sum(skip_flags.astype(jnp.float32)[:, None, None] * cached_deltas, axis=0)
    resting = hidden_state + kept_deltas
    fresh_delta = head_total * gate_values[None, :]
    mixed_state = resting + fresh_delta
    return (mixed_state, fresh_delta)


def solution(mesh):
    placed = (
        P(("groups", "seq"), ("wt", "head")),
        P(("groups", "seq"), ("wt", "head")),
        P(("groups", "seq"), ("wt", "head")),
        P(("wt", "head"), "seq"),
        P(("groups", "wt", "head")),
        P(("groups", "seq"), ("wt", "head")),
        P(None, ("groups", "seq"), ("wt", "head")),
        P("groups"),
    )

    def local(*args):
        sizes = tuple(mesh.shape[name] for name in ("seq", "wt", "head"))
        rows, features = args[0].shape
        if sizes == (4, 2, 2) and rows % 32 == 0 and features % (2 * HEAD_DIM) == 0 and args[3].shape[1] % 256 == 0:
            return local_heads(*args)
        return local_general(*args)

    return jax.shard_map(
        local,
        mesh=mesh,
        in_specs=placed,
        out_specs=(P(("groups", "seq"), ("wt", "head")), P(("groups", "seq"), ("wt", "head"))),
        check_vma=False,
    )
```

```python
import functools

import jax
import jax.numpy as jnp
from jax import lax
from jax.experimental import pallas as pl
from jax.experimental.pallas import tpu as pltpu
from jax.sharding import PartitionSpec as P

HEAD_DIM = 128
VMEM_BYTES = 48 * 1024 * 1024
PACK_BYTES = 59 * 1024 * 1024 + 400 * 1024
LOG2_E = 1.4426950408889634


def attend(state_in, key_rows, value_rows, query_heads, score_scale):
    key_count = key_rows.shape[0]
    head_count = query_heads.shape[1]
    blocks = -(-key_count // 1024)
    while key_count % blocks:
        blocks = blocks + 1
    block_size = key_count // blocks

    def one_block(block_index, state_now):
        row_peak, row_total, weighted = state_now
        start_row = block_index * block_size
        key_block = lax.dynamic_slice_in_dim(key_rows, start_row, block_size, 0)
        value_block = lax.dynamic_slice_in_dim(value_rows, start_row, block_size, 0)
        key_heads = key_block.reshape(block_size, head_count, HEAD_DIM)
        value_heads = value_block.reshape(block_size, head_count, HEAD_DIM)
        scores = (
            jnp.einsum("ihd,jhd->hij", query_heads, key_heads, preferred_element_type=jnp.float32)
            * score_scale
        )
        new_peak = jnp.maximum(row_peak, jnp.max(scores, axis=2))
        exp_scores = jnp.exp(scores - new_peak[:, :, None])
        rescale = jnp.exp(row_peak - new_peak)
        row_total = row_total * rescale + jnp.sum(exp_scores, axis=2)
        weighted = weighted * rescale[:, :, None] + jnp.einsum(
            "hij,jhd->hid",
            exp_scores.astype(jnp.bfloat16),
            value_heads,
            preferred_element_type=jnp.float32,
        )
        return (new_peak, row_total, weighted)

    return lax.fori_loop(0, blocks, one_block, state_in)


def finish(state_out, row_count):
    row_peak, row_total, weighted = state_out
    normed = weighted / row_total[:, :, None]
    return normed.transpose(1, 0, 2).reshape(row_count, -1).astype(jnp.bfloat16)


def local_general(
    queries,
    key_vectors,
    value_vectors,
    out_weight,
    gate_values,
    hidden_state,
    cached_deltas,
    skip_flags,
):
    row_count = queries.shape[0]
    head_count = queries.shape[1] // HEAD_DIM
    score_scale = HEAD_DIM ** (-0.5)
    query_heads = queries.reshape(row_count, head_count, HEAD_DIM)
    start_state = (
        jnp.full((head_count, row_count), -1e30, jnp.float32),
        jnp.zeros((head_count, row_count), jnp.float32),
        jnp.zeros((head_count, row_count, HEAD_DIM), jnp.float32),
    )
    gathered_keys, gathered_values, gathered_weight = (
        lax.all_gather(key_vectors, "seq", axis=0, tiled=True),
        lax.all_gather(value_vectors, "seq", axis=0, tiled=True),
        lax.all_gather(out_weight, "seq", axis=1, tiled=True),
    )
    final_state = attend(start_state, gathered_keys, gathered_values, query_heads, score_scale)
    attention_out = finish(final_state, row_count)
    partial_sums = jnp.dot(attention_out, gathered_weight, preferred_element_type=jnp.float32)
    head_total = lax.psum_scatter(
        partial_sums.astype(jnp.bfloat16), ("wt", "head"), scatter_dimension=1, tiled=True
    ).astype(jnp.float32)
    fresh_delta = head_total * gate_values[None, :]
    kept_deltas = jnp.sum(skip_flags.astype(jnp.float32)[:, None, None] * cached_deltas, axis=0)
    mixed_state = hidden_state + kept_deltas + fresh_delta
    return (mixed_state, fresh_delta)


def bits():
    z = lax.axis_index("seq")
    return lax.div(z, 2), lax.rem(z, 2)


def flip(bit, value):
    return 1 - bit if value else bit


def pack_kernel(queries, keys, values, *refs):
    outs, sems = refs[:4], refs[4]
    rows, width = queries.shape[0], outs[0].shape[1]
    half = rows // 2
    zh, zl = bits()
    copies = []
    for k in range(4):
        part = pl.ds(pl.multiple_of(flip(zh, k // 2) * half, 16), half)
        columns = pl.ds(pl.multiple_of(flip(zl, k % 2) * width, 128), width)
        moves = [
            (keys.at[part, columns], outs[k].at[pl.ds(0, half), :]),
            (values.at[part, columns], outs[k].at[pl.ds(half, half), :]),
        ]
        if k < 2:
            moves.append((queries.at[:, columns], outs[k].at[pl.ds(rows, rows), :]))
        for start, end in moves:
            copies.append(pltpu.make_async_copy(start, end, sems.at[len(copies)]))
    for copy in copies:
        copy.start()
    for copy in copies:
        copy.wait()


def join_kernel(*refs):
    blocks, joined = refs[:4], refs[4]
    rows = joined.shape[0] // 4
    for k, block in enumerate(blocks):
        joined[k * rows : (k + 1) * rows, :] = block[:rows, :]


def attention_kernel(*refs):
    blocks, sibling, out = refs[:4], refs[4], refs[5]
    key_all, value_all, query_all = refs[6:]
    rows = query_all.shape[0] // 2
    half = rows // 2
    for k in range(4):
        here, there = slice(k * half, (k + 1) * half), slice((4 + k) * half, (5 + k) * half)
        key_all[here, :] = blocks[k][:half, :]
        value_all[here, :] = blocks[k][half:rows, :]
        key_all[there, :] = sibling[k * rows : k * rows + half, :]
        value_all[there, :] = sibling[k * rows + half : (k + 1) * rows, :]
    _, zl = bits()
    for k in range(2):
        at = pl.ds(pl.multiple_of(flip(zl, k) * rows, 16), rows)
        query_all[at, :] = blocks[k][rows:, :]
    for h in range(out.shape[1] // HEAD_DIM):
        columns = slice(h * HEAD_DIM, (h + 1) * HEAD_DIM)
        scores = lax.dot_general(
            query_all[:, columns],
            key_all[:, columns],
            (((1,), (1,)), ((), ())),
            preferred_element_type=jnp.float32,
        )
        peak = jnp.max(scores, axis=1, keepdims=True)
        weights = jnp.exp2((scores - peak) * (LOG2_E * HEAD_DIM ** (-0.5)))
        total = jnp.sum(weights, axis=1, keepdims=True)
        result = jnp.dot(
            weights.astype(jnp.bfloat16), value_all[:, columns], preferred_element_type=jnp.float32
        )
        out[:, columns] = (result / total).astype(out.dtype)


def project_kernel(first, gathered, weight, weight_c, keep, send):
    rows, count = keep.shape
    core, x = lax.axis_index("head"), lax.axis_index("wt")
    columns = slice(first, first + count)
    total = None
    for other, block in enumerate((weight, weight_c)):
        start = 2 * flip(core, other) * 2 * rows
        left = jnp.concatenate(
            [
                gathered[pl.ds(pl.multiple_of(start + low * 2 * rows, 16), 2 * rows), :]
                for low in range(2)
            ],
            axis=1,
        )
        term = jnp.dot(left, block[:, columns], preferred_element_type=jnp.float32)
        total = term if total is None else total + term
    for low in range(2):
        part = total[low * rows : (low + 1) * rows]

        @pl.when(x == low)
        def _():
            keep[...] = part

        @pl.when(x != low)
        def _():
            send[...] = part.astype(send.dtype)


def add_kernel(keep, arrived, out):
    out[...] = (keep[...] + arrived[...].astype(jnp.float32)).astype(out.dtype)


def call(kernel, args, outs, scratch=(), far_in=False, flops=0, vmem=VMEM_BYTES):
    place = pl.ANY if far_in else pltpu.VMEM
    return pl.pallas_call(
        kernel,
        in_specs=[pl.BlockSpec(memory_space=place)] * len(args),
        out_specs=[pl.BlockSpec(memory_space=pltpu.VMEM)] * len(outs),
        out_shape=[jax.ShapeDtypeStruct(shape, dtype) for shape, dtype in outs],
        scratch_shapes=list(scratch),
        compiler_params=pltpu.CompilerParams(vmem_limit_bytes=vmem),
        cost_estimate=pl.CostEstimate(flops=flops, bytes_accessed=0, transcendentals=0),
    )(*args)


def local_heads(
    queries,
    key_vectors,
    value_vectors,
    out_weight,
    gate_values,
    hidden_state,
    cached_deltas,
    skip_flags,
):
    rows, features = queries.shape
    width = features // 2
    depth, columns = out_weight.shape
    swap = [(0, 1), (1, 0)]
    bf16 = jnp.bfloat16

    weight_c = lax.ppermute(out_weight, "head", swap)

    packed = call(
        pack_kernel,
        (queries, key_vectors, value_vectors),
        [((2 * rows, width), bf16)] * 2 + [((rows, width), bf16)] * 2,
        [pltpu.SemaphoreType.DMA((10,))],
        far_in=True,
        vmem=PACK_BYTES,
    )
    moved = []
    for k in range(4):
        k1, k0 = k // 2, k % 2
        pairs = []
        for zz in range(4):
            for cc in range(2):
                to_z = 2 * cc + ((zz % 2) ^ k0)
                pairs.append((zz * 2 + cc, to_z * 2 + ((zz // 2) ^ k1)))
        moved.append(lax.ppermute(packed[k], ("seq", "head"), pairs))
    (joined,) = call(join_kernel, moved, [((4 * rows, width), bf16)])
    sibling = lax.ppermute(joined, "head", swap)
    (attention_out,) = call(
        attention_kernel,
        moved + [sibling],
        [((2 * rows, width), bf16)],
        [
            pltpu.VMEM((4 * rows, width), bf16),
            pltpu.VMEM((4 * rows, width), bf16),
            pltpu.VMEM((2 * rows, width), bf16),
        ],
        flops=4 * (2 * rows) * (4 * rows) * width,
    )
    gathered = lax.all_gather(attention_out, "seq", axis=0, tiled=True)

    pairs = []
    for zz in range(4):
        for xx in range(2):
            for cc in range(2):
                to = ((2 * cc + xx) * 2 + zz // 2) * 2 + zz % 2
                pairs.append(((zz * 2 + xx) * 2 + cc, to))
    cut = columns * 2 // 5 // 256 * 256
    owned = []
    for first, count in ((0, cut), (cut, columns - cut)):
        keep, send = call(
            functools.partial(project_kernel, first),
            (gathered, out_weight, weight_c),
            [((rows, count), jnp.float32), ((rows, count), bf16)],
            flops=4 * (2 * rows) * depth * count,
        )
        gathered, _ = lax.optimization_barrier((gathered, send))
        arrived = lax.ppermute(send, "wt", swap)
        (summed,) = call(add_kernel, (keep, arrived), [((rows, count), bf16)])
        owned.append(lax.ppermute(summed, ("seq", "wt", "head"), pairs))
    head_total = jnp.concatenate(owned, axis=1).astype(jnp.float32)
    kept_deltas = jnp.sum(skip_flags.astype(jnp.float32)[:, None, None] * cached_deltas, axis=0)
    resting = hidden_state + kept_deltas
    fresh_delta = head_total * gate_values[None, :]
    mixed_state = resting + fresh_delta
    return (mixed_state, fresh_delta)


def solution(mesh):
    placed = (
        P(("groups", "seq"), ("wt", "head")),
        P(("groups", "seq"), ("wt", "head")),
        P(("groups", "seq"), ("wt", "head")),
        P(("wt", "head"), "seq"),
        P(("groups", "wt", "head")),
        P(("groups", "seq"), ("wt", "head")),
        P(None, ("groups", "seq"), ("wt", "head")),
        P("groups"),
    )

    def local(*args):
        sizes = tuple(mesh.shape[name] for name in ("seq", "wt", "head"))
        rows, features = args[0].shape
        if sizes == (4, 2, 2) and rows % 32 == 0 and features % (2 * HEAD_DIM) == 0 and args[3].shape[1] % 256 == 0 and args[3].shape[1] >= 640:
            return local_heads(*args)
        return local_general(*args)

    return jax.shard_map(
        local,
        mesh=mesh,
        in_specs=placed,
        out_specs=(P(("groups", "seq"), ("wt", "head")), P(("groups", "seq"), ("wt", "head"))),
        check_vma=False,
    )
```

```python
import jax
import jax.numpy as jnp
from jax import lax
from jax.experimental import pallas as pl
from jax.experimental.pallas import tpu as pltpu
from jax.sharding import PartitionSpec as P

HEAD_DIM = 128
VMEM_BYTES = 48 * 1024 * 1024
PACK_BYTES = 59 * 1024 * 1024 + 400 * 1024
LOG2_E = 1.4426950408889634


def attend(state_in, key_rows, value_rows, query_heads, score_scale):
    key_count = key_rows.shape[0]
    head_count = query_heads.shape[1]
    blocks = -(-key_count // 1024)
    while key_count % blocks:
        blocks = blocks + 1
    block_size = key_count // blocks

    def one_block(block_index, state_now):
        row_peak, row_total, weighted = state_now
        start_row = block_index * block_size
        key_block = lax.dynamic_slice_in_dim(key_rows, start_row, block_size, 0)
        value_block = lax.dynamic_slice_in_dim(value_rows, start_row, block_size, 0)
        key_heads = key_block.reshape(block_size, head_count, HEAD_DIM)
        value_heads = value_block.reshape(block_size, head_count, HEAD_DIM)
        scores = (
            jnp.einsum("ihd,jhd->hij", query_heads, key_heads, preferred_element_type=jnp.float32)
            * score_scale
        )
        new_peak = jnp.maximum(row_peak, jnp.max(scores, axis=2))
        exp_scores = jnp.exp(scores - new_peak[:, :, None])
        rescale = jnp.exp(row_peak - new_peak)
        row_total = row_total * rescale + jnp.sum(exp_scores, axis=2)
        weighted = weighted * rescale[:, :, None] + jnp.einsum(
            "hij,jhd->hid",
            exp_scores.astype(jnp.bfloat16),
            value_heads,
            preferred_element_type=jnp.float32,
        )
        return (new_peak, row_total, weighted)

    return lax.fori_loop(0, blocks, one_block, state_in)


def finish(state_out, row_count):
    row_peak, row_total, weighted = state_out
    normed = weighted / row_total[:, :, None]
    return normed.transpose(1, 0, 2).reshape(row_count, -1).astype(jnp.bfloat16)


def local_general(
    queries,
    key_vectors,
    value_vectors,
    out_weight,
    gate_values,
    hidden_state,
    cached_deltas,
    skip_flags,
):
    row_count = queries.shape[0]
    head_count = queries.shape[1] // HEAD_DIM
    score_scale = HEAD_DIM ** (-0.5)
    query_heads = queries.reshape(row_count, head_count, HEAD_DIM)
    start_state = (
        jnp.full((head_count, row_count), -1e30, jnp.float32),
        jnp.zeros((head_count, row_count), jnp.float32),
        jnp.zeros((head_count, row_count, HEAD_DIM), jnp.float32),
    )
    gathered_keys, gathered_values, gathered_weight = (
        lax.all_gather(key_vectors, "seq", axis=0, tiled=True),
        lax.all_gather(value_vectors, "seq", axis=0, tiled=True),
        lax.all_gather(out_weight, "seq", axis=1, tiled=True),
    )
    final_state = attend(start_state, gathered_keys, gathered_values, query_heads, score_scale)
    attention_out = finish(final_state, row_count)
    partial_sums = jnp.dot(attention_out, gathered_weight, preferred_element_type=jnp.float32)
    head_total = lax.psum_scatter(
        partial_sums.astype(jnp.bfloat16), ("wt", "head"), scatter_dimension=1, tiled=True
    ).astype(jnp.float32)
    fresh_delta = head_total * gate_values[None, :]
    kept_deltas = jnp.sum(skip_flags.astype(jnp.float32)[:, None, None] * cached_deltas, axis=0)
    mixed_state = hidden_state + kept_deltas + fresh_delta
    return (mixed_state, fresh_delta)


def bits():
    z = lax.axis_index("seq")
    return lax.div(z, 2), lax.rem(z, 2)


def flip(bit, value):
    return 1 - bit if value else bit


def pack_kernel(queries, keys, values, *refs):
    outs, sems = refs[:4], refs[4]
    rows, width = queries.shape[0], outs[0].shape[1]
    half = rows // 2
    zh, zl = bits()
    copies = []
    for k in range(4):
        part = pl.ds(pl.multiple_of(flip(zh, k // 2) * half, 16), half)
        columns = pl.ds(pl.multiple_of(flip(zl, k % 2) * width, 128), width)
        moves = [
            (keys.at[part, columns], outs[k].at[pl.ds(0, half), :]),
            (values.at[part, columns], outs[k].at[pl.ds(half, half), :]),
        ]
        if k < 2:
            moves.append((queries.at[:, columns], outs[k].at[pl.ds(rows, rows), :]))
        for start, end in moves:
            copies.append(pltpu.make_async_copy(start, end, sems.at[len(copies)]))
    for copy in copies:
        copy.start()
    for copy in copies:
        copy.wait()


def join_kernel(*refs):
    blocks, joined = refs[:4], refs[4]
    rows = joined.shape[0] // 4
    for k, block in enumerate(blocks):
        joined[k * rows : (k + 1) * rows, :] = block[:rows, :]


def attention_kernel(*refs):
    blocks, sibling = refs[:4], refs[4]
    sent, kept, key_all, value_all, query_all = refs[5:]
    rows = sent.shape[0]
    half = rows // 2
    for k in range(4):
        here, there = slice(k * half, (k + 1) * half), slice((4 + k) * half, (5 + k) * half)
        key_all[here, :] = blocks[k][:half, :]
        value_all[here, :] = blocks[k][half:rows, :]
        key_all[there, :] = sibling[k * rows : k * rows + half, :]
        value_all[there, :] = sibling[k * rows + half : (k + 1) * rows, :]
    _, zl = bits()
    x = lax.axis_index("wt")
    for k in range(2):
        for part in range(2):
            at = rows + flip(x, part == 0) * half
            to = (part * 2 + flip(zl, k)) * half
            query_all[pl.ds(pl.multiple_of(to, 16), half), :] = blocks[k][
                pl.ds(pl.multiple_of(at, 16), half), :
            ]
    for h in range(sent.shape[1] // HEAD_DIM):
        columns = slice(h * HEAD_DIM, (h + 1) * HEAD_DIM)
        scores = lax.dot_general(
            query_all[:, columns],
            key_all[:, columns],
            (((1,), (1,)), ((), ())),
            preferred_element_type=jnp.float32,
        )
        peak = jnp.max(scores, axis=1, keepdims=True)
        weights = jnp.exp2((scores - peak) * (LOG2_E * HEAD_DIM ** (-0.5)))
        total = jnp.sum(weights, axis=1, keepdims=True)
        result = jnp.dot(
            weights.astype(jnp.bfloat16), value_all[:, columns], preferred_element_type=jnp.float32
        )
        result = (result / total).astype(sent.dtype)
        sent[:, columns] = result[:rows]
        kept[:, columns] = result[rows:]


def multiply(gathered, weight, weight_c):
    rows = gathered.shape[0] // 4
    core = lax.axis_index("head")
    total = None
    for other, block in enumerate((weight, weight_c)):
        start = 2 * flip(core, other) * rows
        left = jnp.concatenate(
            [
                gathered[pl.ds(pl.multiple_of(start + low * rows, 16), rows), :]
                for low in range(2)
            ],
            axis=1,
        )
        term = jnp.dot(left, block[...], preferred_element_type=jnp.float32)
        total = term if total is None else total + term
    return total


def sent_kernel(gathered, weight, weight_c, out):
    out[...] = multiply(gathered, weight, weight_c).astype(out.dtype)


def kept_kernel(gathered, weight, weight_c, arrived, out0, out1):
    total = multiply(gathered, weight, weight_c) + arrived[...].astype(jnp.float32)
    half = out0.shape[0]
    x = lax.axis_index("wt")
    for low in range(2):
        part = total[low * half : (low + 1) * half].astype(out0.dtype)

        @pl.when(x == low)
        def _():
            out0[...] = part

        @pl.when(x != low)
        def _():
            out1[...] = part


def call(kernel, args, outs, scratch=(), far_in=False, flops=0, vmem=VMEM_BYTES):
    place = pl.ANY if far_in else pltpu.VMEM
    return pl.pallas_call(
        kernel,
        in_specs=[pl.BlockSpec(memory_space=place)] * len(args),
        out_specs=[pl.BlockSpec(memory_space=pltpu.VMEM)] * len(outs),
        out_shape=[jax.ShapeDtypeStruct(shape, dtype) for shape, dtype in outs],
        scratch_shapes=list(scratch),
        compiler_params=pltpu.CompilerParams(vmem_limit_bytes=vmem),
        cost_estimate=pl.CostEstimate(flops=flops, bytes_accessed=0, transcendentals=0),
    )(*args)


def local_heads(
    queries,
    key_vectors,
    value_vectors,
    out_weight,
    gate_values,
    hidden_state,
    cached_deltas,
    skip_flags,
):
    rows, features = queries.shape
    width = features // 2
    depth, columns = out_weight.shape
    swap = [(0, 1), (1, 0)]
    bf16 = jnp.bfloat16

    half = rows // 2
    zl = lax.axis_index("seq") % 2

    packed = call(
        pack_kernel,
        (queries, key_vectors, value_vectors),
        [((2 * rows, width), bf16)] * 2 + [((rows, width), bf16)] * 2,
        [pltpu.SemaphoreType.DMA((10,))],
        far_in=True,
        vmem=PACK_BYTES,
    )
    moved = []
    for k in range(4):
        k1, k0 = k // 2, k % 2
        pairs = []
        for zz in range(4):
            for cc in range(2):
                to_z = 2 * cc + ((zz % 2) ^ k0)
                pairs.append((zz * 2 + cc, to_z * 2 + ((zz // 2) ^ k1)))
        moved.append(lax.ppermute(packed[k], ("seq", "head"), pairs))
    (joined,) = call(join_kernel, moved, [((4 * rows, width), bf16)])
    sibling = lax.ppermute(joined, "head", swap)
    late_weight, _ = lax.optimization_barrier((out_weight, sibling))
    weight_c = lax.ppermute(late_weight, "head", swap)
    sent_rows, kept_rows = call(
        attention_kernel,
        moved + [sibling],
        [((rows, width), bf16)] * 2,
        [
            pltpu.VMEM((4 * rows, width), bf16),
            pltpu.VMEM((4 * rows, width), bf16),
            pltpu.VMEM((2 * rows, width), bf16),
        ],
        flops=4 * (2 * rows) * (4 * rows) * width,
    )

    flops = 4 * rows * depth * columns
    gathered = lax.all_gather(sent_rows, "seq", axis=0, tiled=True)
    (send,) = call(
        sent_kernel, (gathered, out_weight, weight_c), [((rows, columns), bf16)], flops=flops
    )
    arrived = lax.ppermute(send, "wt", swap)
    kept_rows, _ = lax.optimization_barrier((kept_rows, send))
    gathered = lax.all_gather(kept_rows, "seq", axis=0, tiled=True)
    sums = call(
        kept_kernel,
        (gathered, out_weight, weight_c, arrived),
        [((half, columns), bf16)] * 2,
        flops=flops,
    )

    owned = []
    for p, part in enumerate(sums):
        pairs = []
        for zz in range(4):
            for xx in range(2):
                for cc in range(2):
                    to = ((2 * cc + (p ^ xx)) * 2 + zz // 2) * 2 + zz % 2
                    pairs.append(((zz * 2 + xx) * 2 + cc, to))
        owned.append(lax.ppermute(part, ("seq", "wt", "head"), pairs))
    head_total = jnp.concatenate(
        [
            jnp.where(zl == 0, owned[0], owned[1]),
            jnp.where(zl == 0, owned[1], owned[0]),
        ],
        axis=0,
    ).astype(jnp.float32)
    kept_deltas = jnp.sum(skip_flags.astype(jnp.float32)[:, None, None] * cached_deltas, axis=0)
    resting = hidden_state + kept_deltas
    fresh_delta = head_total * gate_values[None, :]
    mixed_state = resting + fresh_delta
    return (mixed_state, fresh_delta)


def solution(mesh):
    placed = (
        P(("groups", "seq"), ("wt", "head")),
        P(("groups", "seq"), ("wt", "head")),
        P(("groups", "seq"), ("wt", "head")),
        P(("wt", "head"), "seq"),
        P(("groups", "wt", "head")),
        P(("groups", "seq"), ("wt", "head")),
        P(None, ("groups", "seq"), ("wt", "head")),
        P("groups"),
    )

    def local(*args):
        sizes = tuple(mesh.shape[name] for name in ("seq", "wt", "head"))
        rows, features = args[0].shape
        if sizes == (4, 2, 2) and rows % 32 == 0 and features % (2 * HEAD_DIM) == 0:
            return local_heads(*args)
        return local_general(*args)

    return jax.shard_map(
        local,
        mesh=mesh,
        in_specs=placed,
        out_specs=(P(("groups", "seq"), ("wt", "head")), P(("groups", "seq"), ("wt", "head"))),
        check_vma=False,
    )
```

```python
import functools

import jax
import jax.numpy as jnp
from jax import lax
from jax.experimental import pallas as pl
from jax.experimental.pallas import tpu as pltpu
from jax.sharding import PartitionSpec as P

HEAD_DIM = 128
VMEM_BYTES = 48 * 1024 * 1024
PACK_BYTES = 59 * 1024 * 1024 + 400 * 1024
LOG2_E = 1.4426950408889634


def attend(state_in, key_rows, value_rows, query_heads, score_scale):
    key_count = key_rows.shape[0]
    head_count = query_heads.shape[1]
    blocks = -(-key_count // 1024)
    while key_count % blocks:
        blocks = blocks + 1
    block_size = key_count // blocks

    def one_block(block_index, state_now):
        row_peak, row_total, weighted = state_now
        start_row = block_index * block_size
        key_block = lax.dynamic_slice_in_dim(key_rows, start_row, block_size, 0)
        value_block = lax.dynamic_slice_in_dim(value_rows, start_row, block_size, 0)
        key_heads = key_block.reshape(block_size, head_count, HEAD_DIM)
        value_heads = value_block.reshape(block_size, head_count, HEAD_DIM)
        scores = (
            jnp.einsum("ihd,jhd->hij", query_heads, key_heads, preferred_element_type=jnp.float32)
            * score_scale
        )
        new_peak = jnp.maximum(row_peak, jnp.max(scores, axis=2))
        exp_scores = jnp.exp(scores - new_peak[:, :, None])
        rescale = jnp.exp(row_peak - new_peak)
        row_total = row_total * rescale + jnp.sum(exp_scores, axis=2)
        weighted = weighted * rescale[:, :, None] + jnp.einsum(
            "hij,jhd->hid",
            exp_scores.astype(jnp.bfloat16),
            value_heads,
            preferred_element_type=jnp.float32,
        )
        return (new_peak, row_total, weighted)

    return lax.fori_loop(0, blocks, one_block, state_in)


def finish(state_out, row_count):
    row_peak, row_total, weighted = state_out
    normed = weighted / row_total[:, :, None]
    return normed.transpose(1, 0, 2).reshape(row_count, -1).astype(jnp.bfloat16)


def local_general(
    queries,
    key_vectors,
    value_vectors,
    out_weight,
    gate_values,
    hidden_state,
    cached_deltas,
    skip_flags,
):
    row_count = queries.shape[0]
    head_count = queries.shape[1] // HEAD_DIM
    score_scale = HEAD_DIM ** (-0.5)
    query_heads = queries.reshape(row_count, head_count, HEAD_DIM)
    start_state = (
        jnp.full((head_count, row_count), -1e30, jnp.float32),
        jnp.zeros((head_count, row_count), jnp.float32),
        jnp.zeros((head_count, row_count, HEAD_DIM), jnp.float32),
    )
    gathered_keys, gathered_values, gathered_weight = (
        lax.all_gather(key_vectors, "seq", axis=0, tiled=True),
        lax.all_gather(value_vectors, "seq", axis=0, tiled=True),
        lax.all_gather(out_weight, "seq", axis=1, tiled=True),
    )
    final_state = attend(start_state, gathered_keys, gathered_values, query_heads, score_scale)
    attention_out = finish(final_state, row_count)
    partial_sums = jnp.dot(attention_out, gathered_weight, preferred_element_type=jnp.float32)
    head_total = lax.psum_scatter(
        partial_sums.astype(jnp.bfloat16), ("wt", "head"), scatter_dimension=1, tiled=True
    ).astype(jnp.float32)
    fresh_delta = head_total * gate_values[None, :]
    kept_deltas = jnp.sum(skip_flags.astype(jnp.float32)[:, None, None] * cached_deltas, axis=0)
    mixed_state = hidden_state + kept_deltas + fresh_delta
    return (mixed_state, fresh_delta)


def bits():
    z = lax.axis_index("seq")
    return lax.div(z, 2), lax.rem(z, 2)


def flip(bit, value):
    return 1 - bit if value else bit


def pack_kernel(queries, keys, values, *refs):
    outs, sems = refs[:4], refs[4]
    rows, width = queries.shape[0], outs[0].shape[1]
    half = rows // 2
    zh, zl = bits()
    copies = []
    for k in range(4):
        part = pl.ds(pl.multiple_of(flip(zh, k // 2) * half, 16), half)
        columns = pl.ds(pl.multiple_of(flip(zl, k % 2) * width, 128), width)
        moves = [
            (keys.at[part, columns], outs[k].at[pl.ds(0, half), :]),
            (values.at[part, columns], outs[k].at[pl.ds(half, half), :]),
        ]
        if k < 2:
            moves.append((queries.at[:, columns], outs[k].at[pl.ds(rows, rows), :]))
        for start, end in moves:
            copies.append(pltpu.make_async_copy(start, end, sems.at[len(copies)]))
    for copy in copies:
        copy.start()
    for copy in copies:
        copy.wait()


def join_kernel(*refs):
    blocks, joined = refs[:4], refs[4]
    rows = joined.shape[0] // 4
    for k, block in enumerate(blocks):
        joined[k * rows : (k + 1) * rows, :] = block[:rows, :]


def attention_kernel(part, *refs):
    blocks, sibling = refs[:4], refs[4]
    out, key_all, value_all, query_all = refs[5:]
    rows = out.shape[0]
    half = rows // 2
    for k in range(4):
        here, there = slice(k * half, (k + 1) * half), slice((4 + k) * half, (5 + k) * half)
        key_all[here, :] = blocks[k][:half, :]
        value_all[here, :] = blocks[k][half:rows, :]
        key_all[there, :] = sibling[k * rows : k * rows + half, :]
        value_all[there, :] = sibling[k * rows + half : (k + 1) * rows, :]
    _, zl = bits()
    start = rows + flip(lax.axis_index("wt"), part == 0) * half
    for k in range(2):
        query_all[pl.ds(pl.multiple_of(flip(zl, k) * half, 16), half), :] = blocks[k][
            pl.ds(pl.multiple_of(start, 16), half), :
        ]
    for h in range(out.shape[1] // HEAD_DIM):
        columns = slice(h * HEAD_DIM, (h + 1) * HEAD_DIM)
        scores = lax.dot_general(
            query_all[:, columns],
            key_all[:, columns],
            (((1,), (1,)), ((), ())),
            preferred_element_type=jnp.float32,
        )
        peak = jnp.max(scores, axis=1, keepdims=True)
        weights = jnp.exp2((scores - peak) * (LOG2_E * HEAD_DIM ** (-0.5)))
        total = jnp.sum(weights, axis=1, keepdims=True)
        result = jnp.dot(
            weights.astype(jnp.bfloat16), value_all[:, columns], preferred_element_type=jnp.float32
        )
        out[:, columns] = (result / total).astype(out.dtype)


def multiply(shards, weight, weight_c, held):
    zh, zl = bits()
    core = lax.axis_index("head")
    for m in range(3):
        held[m] = shards[m][...]
    held[3] = jnp.where(zh == zl, shards[4][...], shards[3][...])
    total = None
    for other, block in enumerate((weight, weight_c)):
        high = 2 * jnp.where(flip(core, other) == zh, 0, 1)
        left = jnp.concatenate([held[high + zl], held[high + 1 - zl]], axis=1)
        term = jnp.dot(left, block[...], preferred_element_type=jnp.float32)
        total = term if total is None else total + term
    return total


def sent_kernel(*refs):
    shards, (weight, weight_c, out, held) = refs[:5], refs[5:]
    out[...] = multiply(shards, weight, weight_c, held).astype(out.dtype)


def kept_kernel(*refs):
    shards, (weight, weight_c, arrived, out0, out1, held) = refs[:5], refs[5:]
    total = multiply(shards, weight, weight_c, held) + arrived[...].astype(jnp.float32)
    half = out0.shape[0]
    x = lax.axis_index("wt")
    for low in range(2):
        part = total[low * half : (low + 1) * half].astype(out0.dtype)

        @pl.when(x == low)
        def _():
            out0[...] = part

        @pl.when(x != low)
        def _():
            out1[...] = part


def gather(shard, *ahead):
    near = lax.ppermute(shard, "seq", [(0, 1), (1, 0), (2, 3), (3, 2)])
    two = lax.ppermute(shard, "seq", [(0, 2), (2, 0), (1, 3), (3, 1)])
    late_shard, late_two = lax.optimization_barrier((shard, two, near) + ahead)[:2]
    middle = lax.ppermute(late_shard, "seq", [(1, 2), (2, 1)])
    ends = lax.ppermute(late_two, "seq", [(1, 0), (2, 3)])
    return [shard, near, two, middle, ends]


def call(kernel, args, outs, scratch=(), far_in=False, flops=0, vmem=VMEM_BYTES):
    place = pl.ANY if far_in else pltpu.VMEM
    return pl.pallas_call(
        kernel,
        in_specs=[pl.BlockSpec(memory_space=place)] * len(args),
        out_specs=[pl.BlockSpec(memory_space=pltpu.VMEM)] * len(outs),
        out_shape=[jax.ShapeDtypeStruct(shape, dtype) for shape, dtype in outs],
        scratch_shapes=list(scratch),
        compiler_params=pltpu.CompilerParams(vmem_limit_bytes=vmem),
        cost_estimate=pl.CostEstimate(flops=flops, bytes_accessed=0, transcendentals=0),
    )(*args)


def local_heads(
    queries,
    key_vectors,
    value_vectors,
    out_weight,
    gate_values,
    hidden_state,
    cached_deltas,
    skip_flags,
):
    rows, features = queries.shape
    width = features // 2
    depth, columns = out_weight.shape
    swap = [(0, 1), (1, 0)]
    bf16 = jnp.bfloat16

    half = rows // 2
    zl = lax.axis_index("seq") % 2

    weight_c = lax.ppermute(out_weight, "head", swap)

    packed = call(
        pack_kernel,
        (queries, key_vectors, value_vectors),
        [((2 * rows, width), bf16)] * 2 + [((rows, width), bf16)] * 2,
        [pltpu.SemaphoreType.DMA((10,))],
        far_in=True,
        vmem=PACK_BYTES,
    )
    moved = []
    for k in range(4):
        k1, k0 = k // 2, k % 2
        pairs = []
        for zz in range(4):
            for cc in range(2):
                to_z = 2 * cc + ((zz % 2) ^ k0)
                pairs.append((zz * 2 + cc, to_z * 2 + ((zz // 2) ^ k1)))
        moved.append(lax.ppermute(packed[k], ("seq", "head"), pairs))
    (joined,) = call(join_kernel, moved, [((4 * rows, width), bf16)])
    sibling = lax.ppermute(joined, "head", swap)
    parts = []
    for part in range(2):
        parts += call(
            functools.partial(attention_kernel, part),
            moved + [sibling],
            [((rows, width), bf16)],
            [
                pltpu.VMEM((4 * rows, width), bf16),
                pltpu.VMEM((4 * rows, width), bf16),
                pltpu.VMEM((rows, width), bf16),
            ],
            flops=4 * rows * (4 * rows) * width,
        )

    flops = 4 * rows * depth * columns
    held = [pltpu.VMEM((4, rows, width), bf16)]
    first, _ = lax.optimization_barrier((parts[0], weight_c))
    shards = gather(first, parts[1])
    (send,) = call(
        sent_kernel, shards + [out_weight, weight_c], [((rows, columns), bf16)], held, flops=flops
    )
    arrived = lax.ppermute(send, "wt", swap)
    second, _ = lax.optimization_barrier((parts[1], send))
    shards = gather(second)
    sums = call(
        kept_kernel,
        shards + [out_weight, weight_c, arrived],
        [((half, columns), bf16)] * 2,
        held,
        flops=flops,
    )

    owned = []
    for p, part in enumerate(sums):
        pairs = []
        for zz in range(4):
            for xx in range(2):
                for cc in range(2):
                    to = ((2 * cc + (p ^ xx)) * 2 + zz // 2) * 2 + zz % 2
                    pairs.append(((zz * 2 + xx) * 2 + cc, to))
        owned.append(lax.ppermute(part, ("seq", "wt", "head"), pairs))
    head_total = jnp.concatenate(
        [
            jnp.where(zl == 0, owned[0], owned[1]),
            jnp.where(zl == 0, owned[1], owned[0]),
        ],
        axis=0,
    ).astype(jnp.float32)
    kept_deltas = jnp.sum(skip_flags.astype(jnp.float32)[:, None, None] * cached_deltas, axis=0)
    resting = hidden_state + kept_deltas
    fresh_delta = head_total * gate_values[None, :]
    mixed_state = resting + fresh_delta
    return (mixed_state, fresh_delta)


def solution(mesh):
    placed = (
        P(("groups", "seq"), ("wt", "head")),
        P(("groups", "seq"), ("wt", "head")),
        P(("groups", "seq"), ("wt", "head")),
        P(("wt", "head"), "seq"),
        P(("groups", "wt", "head")),
        P(("groups", "seq"), ("wt", "head")),
        P(None, ("groups", "seq"), ("wt", "head")),
        P("groups"),
    )

    def local(*args):
        sizes = tuple(mesh.shape[name] for name in ("seq", "wt", "head"))
        rows, features = args[0].shape
        if sizes == (4, 2, 2) and rows % 32 == 0 and features % (2 * HEAD_DIM) == 0:
            return local_heads(*args)
        return local_general(*args)

    return jax.shard_map(
        local,
        mesh=mesh,
        in_specs=placed,
        out_specs=(P(("groups", "seq"), ("wt", "head")), P(("groups", "seq"), ("wt", "head"))),
        check_vma=False,
    )
```

```python
import jax
import jax.numpy as jnp
from jax import lax
from jax.experimental import pallas as pl
from jax.experimental.pallas import tpu as pltpu
from jax.sharding import PartitionSpec as P

HEAD_DIM = 128
VMEM_BYTES = 48 * 1024 * 1024
PACK_BYTES = 59 * 1024 * 1024 + 400 * 1024
LOG2_E = 1.4426950408889634


def attend(state_in, key_rows, value_rows, query_heads, score_scale):
    key_count = key_rows.shape[0]
    head_count = query_heads.shape[1]
    blocks = -(-key_count // 1024)
    while key_count % blocks:
        blocks = blocks + 1
    block_size = key_count // blocks

    def one_block(block_index, state_now):
        row_peak, row_total, weighted = state_now
        start_row = block_index * block_size
        key_block = lax.dynamic_slice_in_dim(key_rows, start_row, block_size, 0)
        value_block = lax.dynamic_slice_in_dim(value_rows, start_row, block_size, 0)
        key_heads = key_block.reshape(block_size, head_count, HEAD_DIM)
        value_heads = value_block.reshape(block_size, head_count, HEAD_DIM)
        scores = (
            jnp.einsum("ihd,jhd->hij", query_heads, key_heads, preferred_element_type=jnp.float32)
            * score_scale
        )
        new_peak = jnp.maximum(row_peak, jnp.max(scores, axis=2))
        exp_scores = jnp.exp(scores - new_peak[:, :, None])
        rescale = jnp.exp(row_peak - new_peak)
        row_total = row_total * rescale + jnp.sum(exp_scores, axis=2)
        weighted = weighted * rescale[:, :, None] + jnp.einsum(
            "hij,jhd->hid",
            exp_scores.astype(jnp.bfloat16),
            value_heads,
            preferred_element_type=jnp.float32,
        )
        return (new_peak, row_total, weighted)

    return lax.fori_loop(0, blocks, one_block, state_in)


def finish(state_out, row_count):
    row_peak, row_total, weighted = state_out
    normed = weighted / row_total[:, :, None]
    return normed.transpose(1, 0, 2).reshape(row_count, -1).astype(jnp.bfloat16)


def local_general(
    queries,
    key_vectors,
    value_vectors,
    out_weight,
    gate_values,
    hidden_state,
    cached_deltas,
    skip_flags,
):
    row_count = queries.shape[0]
    head_count = queries.shape[1] // HEAD_DIM
    score_scale = HEAD_DIM ** (-0.5)
    query_heads = queries.reshape(row_count, head_count, HEAD_DIM)
    start_state = (
        jnp.full((head_count, row_count), -1e30, jnp.float32),
        jnp.zeros((head_count, row_count), jnp.float32),
        jnp.zeros((head_count, row_count, HEAD_DIM), jnp.float32),
    )
    gathered_keys, gathered_values, gathered_weight = (
        lax.all_gather(key_vectors, "seq", axis=0, tiled=True),
        lax.all_gather(value_vectors, "seq", axis=0, tiled=True),
        lax.all_gather(out_weight, "seq", axis=1, tiled=True),
    )
    final_state = attend(start_state, gathered_keys, gathered_values, query_heads, score_scale)
    attention_out = finish(final_state, row_count)
    partial_sums = jnp.dot(attention_out, gathered_weight, preferred_element_type=jnp.float32)
    head_total = lax.psum_scatter(
        partial_sums.astype(jnp.bfloat16), ("wt", "head"), scatter_dimension=1, tiled=True
    ).astype(jnp.float32)
    fresh_delta = head_total * gate_values[None, :]
    kept_deltas = jnp.sum(skip_flags.astype(jnp.float32)[:, None, None] * cached_deltas, axis=0)
    mixed_state = hidden_state + kept_deltas + fresh_delta
    return (mixed_state, fresh_delta)


def bits():
    z = lax.axis_index("seq")
    return lax.div(z, 2), lax.rem(z, 2)


def flip(bit, value):
    return 1 - bit if value else bit


def pack_kernel(queries, keys, values, *refs):
    outs, sems = refs[:4], refs[4]
    rows, width = queries.shape[0], outs[0].shape[1]
    half = rows // 2
    zh, zl = bits()
    copies = []
    for k in range(4):
        part = pl.ds(pl.multiple_of(flip(zh, k // 2) * half, 16), half)
        columns = pl.ds(pl.multiple_of(flip(zl, k % 2) * width, 128), width)
        moves = [
            (keys.at[part, columns], outs[k].at[pl.ds(0, half), :]),
            (values.at[part, columns], outs[k].at[pl.ds(half, half), :]),
        ]
        if k < 2:
            moves.append((queries.at[:, columns], outs[k].at[pl.ds(rows, rows), :]))
        for start, end in moves:
            copies.append(pltpu.make_async_copy(start, end, sems.at[len(copies)]))
    for copy in copies:
        copy.start()
    for copy in copies:
        copy.wait()


def join_kernel(*refs):
    blocks, joined = refs[:4], refs[4]
    rows = joined.shape[0] // 4
    for k, block in enumerate(blocks):
        joined[k * rows : (k + 1) * rows, :] = block[:rows, :]


def attention_kernel(*refs):
    blocks, sibling = refs[:4], refs[4]
    sent, kept, key_all, value_all, query_all = refs[5:]
    rows = sent.shape[0]
    half = rows // 2
    for k in range(4):
        here, there = slice(k * half, (k + 1) * half), slice((4 + k) * half, (5 + k) * half)
        key_all[here, :] = blocks[k][:half, :]
        value_all[here, :] = blocks[k][half:rows, :]
        key_all[there, :] = sibling[k * rows : k * rows + half, :]
        value_all[there, :] = sibling[k * rows + half : (k + 1) * rows, :]
    _, zl = bits()
    x = lax.axis_index("wt")
    for k in range(2):
        for part in range(2):
            at = rows + flip(x, part == 0) * half
            to = (part * 2 + flip(zl, k)) * half
            query_all[pl.ds(pl.multiple_of(to, 16), half), :] = blocks[k][
                pl.ds(pl.multiple_of(at, 16), half), :
            ]
    for h in range(sent.shape[1] // HEAD_DIM):
        columns = slice(h * HEAD_DIM, (h + 1) * HEAD_DIM)
        scores = lax.dot_general(
            query_all[:, columns],
            key_all[:, columns],
            (((1,), (1,)), ((), ())),
            preferred_element_type=jnp.float32,
        )
        peak = jnp.max(scores, axis=1, keepdims=True)
        weights = jnp.exp2((scores - peak) * (LOG2_E * HEAD_DIM ** (-0.5)))
        total = jnp.sum(weights, axis=1, keepdims=True)
        result = jnp.dot(
            weights.astype(jnp.bfloat16), value_all[:, columns], preferred_element_type=jnp.float32
        )
        result = (result / total).astype(sent.dtype)
        sent[:, columns] = result[:rows]
        kept[:, columns] = result[rows:]


def multiply(shards, weight, weight_c, held):
    rows = shards[0].shape[0]
    zh, zl = bits()
    core = lax.axis_index("head")
    for m, shard in enumerate(shards):
        held[m * rows : (m + 1) * rows, :] = shard[...]
    total = None
    for other, block in enumerate((weight, weight_c)):
        high = 2 * lax.rem(flip(core, other) + zh, 2)
        left = jnp.concatenate(
            [
                held[pl.ds(pl.multiple_of((high + flip(zl, low)) * rows, 16), rows), :]
                for low in range(2)
            ],
            axis=1,
        )
        term = jnp.dot(left, block[...], preferred_element_type=jnp.float32)
        total = term if total is None else total + term
    return total


def sent_kernel(*refs):
    shards, (weight, weight_c, out, held) = refs[:4], refs[4:]
    out[...] = multiply(shards, weight, weight_c, held).astype(out.dtype)


def kept_kernel(*refs):
    arrived, shards, (weight, weight_c, out0, out1, held) = refs[0], refs[1:5], refs[5:]
    total = multiply(shards, weight, weight_c, held) + arrived[...].astype(jnp.float32)
    half = out0.shape[0]
    x = lax.axis_index("wt")
    for low in range(2):
        part = total[low * half : (low + 1) * half].astype(out0.dtype)

        @pl.when(x == low)
        def _():
            out0[...] = part

        @pl.when(x != low)
        def _():
            out1[...] = part


def along(shard, m):
    return lax.ppermute(shard, "seq", [(z, z ^ m) for z in range(4)])


def call(kernel, args, outs, scratch=(), far_in=False, flops=0, vmem=VMEM_BYTES):
    place = pl.ANY if far_in else pltpu.VMEM
    return pl.pallas_call(
        kernel,
        in_specs=[pl.BlockSpec(memory_space=place)] * len(args),
        out_specs=[pl.BlockSpec(memory_space=pltpu.VMEM)] * len(outs),
        out_shape=[jax.ShapeDtypeStruct(shape, dtype) for shape, dtype in outs],
        scratch_shapes=list(scratch),
        compiler_params=pltpu.CompilerParams(vmem_limit_bytes=vmem),
        cost_estimate=pl.CostEstimate(flops=flops, bytes_accessed=0, transcendentals=0),
    )(*args)


def local_heads(
    queries,
    key_vectors,
    value_vectors,
    out_weight,
    gate_values,
    hidden_state,
    cached_deltas,
    skip_flags,
):
    rows, features = queries.shape
    width = features // 2
    depth, columns = out_weight.shape
    swap = [(0, 1), (1, 0)]
    bf16 = jnp.bfloat16

    half = rows // 2
    zl = lax.axis_index("seq") % 2

    weight_c = lax.ppermute(out_weight, "head", swap)

    packed = call(
        pack_kernel,
        (queries, key_vectors, value_vectors),
        [((2 * rows, width), bf16)] * 2 + [((rows, width), bf16)] * 2,
        [pltpu.SemaphoreType.DMA((10,))],
        far_in=True,
        vmem=PACK_BYTES,
    )
    moved = []
    for k in range(4):
        k1, k0 = k // 2, k % 2
        pairs = []
        for zz in range(4):
            for cc in range(2):
                to_z = 2 * cc + ((zz % 2) ^ k0)
                pairs.append((zz * 2 + cc, to_z * 2 + ((zz // 2) ^ k1)))
        moved.append(lax.ppermute(packed[k], ("seq", "head"), pairs))
    (joined,) = call(join_kernel, moved, [((4 * rows, width), bf16)])
    sibling = lax.ppermute(joined, "head", swap)
    parts = call(
        attention_kernel,
        moved + [sibling],
        [((rows, width), bf16)] * 2,
        [
            pltpu.VMEM((4 * rows, width), bf16),
            pltpu.VMEM((4 * rows, width), bf16),
            pltpu.VMEM((2 * rows, width), bf16),
        ],
        flops=4 * (2 * rows) * (4 * rows) * width,
    )

    flops = 4 * rows * depth * columns
    held = [pltpu.VMEM((4 * rows, width), bf16)]
    first, second, _ = lax.optimization_barrier((parts[0], parts[1], weight_c))
    shards = [first] + [along(first, m) for m in (1, 2, 3)]
    near = along(second, 1)
    shards[3], _ = lax.optimization_barrier((shards[3], near))
    (send,) = call(
        sent_kernel, shards + [out_weight, weight_c], [((rows, columns), bf16)], held, flops=flops
    )
    arrived = lax.ppermute(send, "wt", swap)
    shards = [parts[1], near] + [along(parts[1], m) for m in (2, 3)]
    sums = call(
        kept_kernel,
        [arrived] + shards + [out_weight, weight_c],
        [((half, columns), bf16)] * 2,
        held,
        flops=flops,
    )

    owned = []
    for p, part in enumerate(sums):
        pairs = []
        for zz in range(4):
            for xx in range(2):
                for cc in range(2):
                    to = ((2 * cc + (p ^ xx)) * 2 + zz // 2) * 2 + zz % 2
                    pairs.append(((zz * 2 + xx) * 2 + cc, to))
        owned.append(lax.ppermute(part, ("seq", "wt", "head"), pairs))
    head_total = jnp.concatenate(
        [
            jnp.where(zl == 0, owned[0], owned[1]),
            jnp.where(zl == 0, owned[1], owned[0]),
        ],
        axis=0,
    ).astype(jnp.float32)
    kept_deltas = jnp.sum(skip_flags.astype(jnp.float32)[:, None, None] * cached_deltas, axis=0)
    resting = hidden_state + kept_deltas
    fresh_delta = head_total * gate_values[None, :]
    mixed_state = resting + fresh_delta
    return (mixed_state, fresh_delta)


def solution(mesh):
    placed = (
        P(("groups", "seq"), ("wt", "head")),
        P(("groups", "seq"), ("wt", "head")),
        P(("groups", "seq"), ("wt", "head")),
        P(("wt", "head"), "seq"),
        P(("groups", "wt", "head")),
        P(("groups", "seq"), ("wt", "head")),
        P(None, ("groups", "seq"), ("wt", "head")),
        P("groups"),
    )

    def local(*args):
        sizes = tuple(mesh.shape[name] for name in ("seq", "wt", "head"))
        rows, features = args[0].shape
        if sizes == (4, 2, 2) and rows % 32 == 0 and features % (2 * HEAD_DIM) == 0:
            return local_heads(*args)
        return local_general(*args)

    return jax.shard_map(
        local,
        mesh=mesh,
        in_specs=placed,
        out_specs=(P(("groups", "seq"), ("wt", "head")), P(("groups", "seq"), ("wt", "head"))),
        check_vma=False,
    )
```

```python
import jax
import jax.numpy as jnp
from jax import lax
from jax.experimental import pallas as pl
from jax.experimental.pallas import tpu as pltpu
from jax.sharding import PartitionSpec as P

HEAD_DIM = 128
VMEM_BYTES = 48 * 1024 * 1024
PACK_BYTES = 59 * 1024 * 1024 + 400 * 1024
LOG2_E = 1.4426950408889634


def attend(state_in, key_rows, value_rows, query_heads, score_scale):
    key_count = key_rows.shape[0]
    head_count = query_heads.shape[1]
    blocks = -(-key_count // 1024)
    while key_count % blocks:
        blocks = blocks + 1
    block_size = key_count // blocks

    def one_block(block_index, state_now):
        row_peak, row_total, weighted = state_now
        start_row = block_index * block_size
        key_block = lax.dynamic_slice_in_dim(key_rows, start_row, block_size, 0)
        value_block = lax.dynamic_slice_in_dim(value_rows, start_row, block_size, 0)
        key_heads = key_block.reshape(block_size, head_count, HEAD_DIM)
        value_heads = value_block.reshape(block_size, head_count, HEAD_DIM)
        scores = (
            jnp.einsum("ihd,jhd->hij", query_heads, key_heads, preferred_element_type=jnp.float32)
            * score_scale
        )
        new_peak = jnp.maximum(row_peak, jnp.max(scores, axis=2))
        exp_scores = jnp.exp(scores - new_peak[:, :, None])
        rescale = jnp.exp(row_peak - new_peak)
        row_total = row_total * rescale + jnp.sum(exp_scores, axis=2)
        weighted = weighted * rescale[:, :, None] + jnp.einsum(
            "hij,jhd->hid",
            exp_scores.astype(jnp.bfloat16),
            value_heads,
            preferred_element_type=jnp.float32,
        )
        return (new_peak, row_total, weighted)

    return lax.fori_loop(0, blocks, one_block, state_in)


def finish(state_out, row_count):
    row_peak, row_total, weighted = state_out
    normed = weighted / row_total[:, :, None]
    return normed.transpose(1, 0, 2).reshape(row_count, -1).astype(jnp.bfloat16)


def local_general(
    queries,
    key_vectors,
    value_vectors,
    out_weight,
    gate_values,
    hidden_state,
    cached_deltas,
    skip_flags,
):
    row_count = queries.shape[0]
    head_count = queries.shape[1] // HEAD_DIM
    score_scale = HEAD_DIM ** (-0.5)
    query_heads = queries.reshape(row_count, head_count, HEAD_DIM)
    start_state = (
        jnp.full((head_count, row_count), -1e30, jnp.float32),
        jnp.zeros((head_count, row_count), jnp.float32),
        jnp.zeros((head_count, row_count, HEAD_DIM), jnp.float32),
    )
    gathered_keys, gathered_values, gathered_weight = (
        lax.all_gather(key_vectors, "seq", axis=0, tiled=True),
        lax.all_gather(value_vectors, "seq", axis=0, tiled=True),
        lax.all_gather(out_weight, "seq", axis=1, tiled=True),
    )
    final_state = attend(start_state, gathered_keys, gathered_values, query_heads, score_scale)
    attention_out = finish(final_state, row_count)
    partial_sums = jnp.dot(attention_out, gathered_weight, preferred_element_type=jnp.float32)
    head_total = lax.psum_scatter(
        partial_sums.astype(jnp.bfloat16), ("wt", "head"), scatter_dimension=1, tiled=True
    ).astype(jnp.float32)
    fresh_delta = head_total * gate_values[None, :]
    kept_deltas = jnp.sum(skip_flags.astype(jnp.float32)[:, None, None] * cached_deltas, axis=0)
    mixed_state = hidden_state + kept_deltas + fresh_delta
    return (mixed_state, fresh_delta)


def bits():
    z = lax.axis_index("seq")
    return lax.div(z, 2), lax.rem(z, 2)


def flip(bit, value):
    return 1 - bit if value else bit


def pack_kernel(queries, keys, values, *refs):
    outs, sems = refs[:4], refs[4]
    rows, width = queries.shape[0], outs[0].shape[1]
    half = rows // 2
    zh, zl = bits()
    copies = []
    for k in range(4):
        part = pl.ds(pl.multiple_of(flip(zh, k // 2) * half, 16), half)
        columns = pl.ds(pl.multiple_of(flip(zl, k % 2) * width, 128), width)
        moves = [
            (keys.at[part, columns], outs[k].at[pl.ds(0, half), :]),
            (values.at[part, columns], outs[k].at[pl.ds(half, half), :]),
        ]
        if k < 2:
            moves.append((queries.at[:, columns], outs[k].at[pl.ds(rows, rows), :]))
        for start, end in moves:
            copies.append(pltpu.make_async_copy(start, end, sems.at[len(copies)]))
    for copy in copies:
        copy.start()
    for copy in copies:
        copy.wait()


def join_kernel(*refs):
    blocks, joined = refs[:4], refs[4]
    rows = joined.shape[0] // 4
    for k, block in enumerate(blocks):
        joined[k * rows : (k + 1) * rows, :] = block[:rows, :]


def attention_kernel(*refs):
    blocks, sibling = refs[:4], refs[4]
    sent, kept, key_all, value_all, query_all = refs[5:]
    rows = sent.shape[0]
    half = rows // 2
    for k in range(4):
        here, there = slice(k * half, (k + 1) * half), slice((4 + k) * half, (5 + k) * half)
        key_all[here, :] = blocks[k][:half, :]
        value_all[here, :] = blocks[k][half:rows, :]
        key_all[there, :] = sibling[k * rows : k * rows + half, :]
        value_all[there, :] = sibling[k * rows + half : (k + 1) * rows, :]
    _, zl = bits()
    x = lax.axis_index("wt")
    for k in range(2):
        for part in range(2):
            at = rows + flip(x, part == 0) * half
            to = (part * 2 + flip(zl, k)) * half
            query_all[pl.ds(pl.multiple_of(to, 16), half), :] = blocks[k][
                pl.ds(pl.multiple_of(at, 16), half), :
            ]
    for h in range(sent.shape[1] // HEAD_DIM):
        columns = slice(h * HEAD_DIM, (h + 1) * HEAD_DIM)
        scores = lax.dot_general(
            query_all[:, columns],
            key_all[:, columns],
            (((1,), (1,)), ((), ())),
            preferred_element_type=jnp.float32,
        )
        peak = jnp.max(scores, axis=1, keepdims=True)
        weights = jnp.exp2((scores - peak) * (LOG2_E * HEAD_DIM ** (-0.5)))
        total = jnp.sum(weights, axis=1, keepdims=True)
        result = jnp.dot(
            weights.astype(jnp.bfloat16), value_all[:, columns], preferred_element_type=jnp.float32
        )
        result = (result / total).astype(sent.dtype)
        sent[:, columns] = result[:rows]
        kept[:, columns] = result[rows:]


def multiply(shards, weight, weight_c, held):
    rows = shards[0].shape[0]
    zh, zl = bits()
    core = lax.axis_index("head")
    for m, shard in enumerate(shards):
        held[m * rows : (m + 1) * rows, :] = shard[...]
    total = None
    for other, block in enumerate((weight, weight_c)):
        high = 2 * lax.rem(flip(core, other) + zh, 2)
        left = jnp.concatenate(
            [
                held[pl.ds(pl.multiple_of((high + flip(zl, low)) * rows, 16), rows), :]
                for low in range(2)
            ],
            axis=1,
        )
        term = jnp.dot(left, block[...], preferred_element_type=jnp.float32)
        total = term if total is None else total + term
    return total


def sent_kernel(*refs):
    shards, (weight, weight_c, out, held) = refs[:4], refs[4:]
    out[...] = multiply(shards, weight, weight_c, held).astype(out.dtype)


def kept_kernel(*refs):
    shards, (weight, weight_c, out, held) = refs[:4], refs[4:]
    out[...] = multiply(shards, weight, weight_c, held)


def add_kernel(kept, arrived, out0, out1):
    half = out0.shape[0]
    x = lax.axis_index("wt")
    for low in range(2):
        at = slice(low * half, (low + 1) * half)
        part = (kept[at, :] + arrived[at, :].astype(jnp.float32)).astype(out0.dtype)

        @pl.when(x == low)
        def _():
            out0[...] = part

        @pl.when(x != low)
        def _():
            out1[...] = part


def along(shard, m):
    return lax.ppermute(shard, "seq", [(z, z ^ m) for z in range(4)])


def call(kernel, args, outs, scratch=(), far_in=False, flops=0, vmem=VMEM_BYTES):
    place = pl.ANY if far_in else pltpu.VMEM
    return pl.pallas_call(
        kernel,
        in_specs=[pl.BlockSpec(memory_space=place)] * len(args),
        out_specs=[pl.BlockSpec(memory_space=pltpu.VMEM)] * len(outs),
        out_shape=[jax.ShapeDtypeStruct(shape, dtype) for shape, dtype in outs],
        scratch_shapes=list(scratch),
        compiler_params=pltpu.CompilerParams(vmem_limit_bytes=vmem),
        cost_estimate=pl.CostEstimate(flops=flops, bytes_accessed=0, transcendentals=0),
    )(*args)


def local_heads(
    queries,
    key_vectors,
    value_vectors,
    out_weight,
    gate_values,
    hidden_state,
    cached_deltas,
    skip_flags,
):
    rows, features = queries.shape
    width = features // 2
    depth, columns = out_weight.shape
    swap = [(0, 1), (1, 0)]
    bf16 = jnp.bfloat16

    half = rows // 2
    zl = lax.axis_index("seq") % 2

    packed = call(
        pack_kernel,
        (queries, key_vectors, value_vectors),
        [((2 * rows, width), bf16)] * 2 + [((rows, width), bf16)] * 2,
        [pltpu.SemaphoreType.DMA((10,))],
        far_in=True,
        vmem=PACK_BYTES,
    )
    late_weight, _ = lax.optimization_barrier((out_weight, packed[0]))
    weight_c = lax.ppermute(late_weight, "head", swap)
    moved = []
    for k in range(4):
        k1, k0 = k // 2, k % 2
        pairs = []
        for zz in range(4):
            for cc in range(2):
                to_z = 2 * cc + ((zz % 2) ^ k0)
                pairs.append((zz * 2 + cc, to_z * 2 + ((zz // 2) ^ k1)))
        moved.append(lax.ppermute(packed[k], ("seq", "head"), pairs))
    (joined,) = call(join_kernel, moved, [((4 * rows, width), bf16)])
    sibling = lax.ppermute(joined, "head", swap)
    parts = call(
        attention_kernel,
        moved + [sibling],
        [((rows, width), bf16)] * 2,
        [
            pltpu.VMEM((4 * rows, width), bf16),
            pltpu.VMEM((4 * rows, width), bf16),
            pltpu.VMEM((2 * rows, width), bf16),
        ],
        flops=4 * (2 * rows) * (4 * rows) * width,
    )

    flops = 4 * rows * depth * columns
    held = [pltpu.VMEM((4 * rows, width), bf16)]
    first, second, _ = lax.optimization_barrier((parts[0], parts[1], weight_c))
    shards = [first] + [along(first, m) for m in (1, 2, 3)]
    near = along(second, 1)
    shards[3], _ = lax.optimization_barrier((shards[3], near))
    (send,) = call(
        sent_kernel, shards + [out_weight, weight_c], [((rows, columns), bf16)], held, flops=flops
    )
    arrived = lax.ppermute(send, "wt", swap)
    shards = [parts[1], near] + [along(parts[1], m) for m in (2, 3)]
    (kept,) = call(
        kept_kernel,
        shards + [out_weight, weight_c],
        [((rows, columns), jnp.float32)],
        held,
        flops=8 * flops,
    )
    sums = call(add_kernel, (kept, arrived), [((half, columns), bf16)] * 2)

    owned = []
    for p, part in enumerate(sums):
        pairs = []
        for zz in range(4):
            for xx in range(2):
                for cc in range(2):
                    to = ((2 * cc + (p ^ xx)) * 2 + zz // 2) * 2 + zz % 2
                    pairs.append(((zz * 2 + xx) * 2 + cc, to))
        owned.append(lax.ppermute(part, ("seq", "wt", "head"), pairs))
    head_total = jnp.concatenate(
        [
            jnp.where(zl == 0, owned[0], owned[1]),
            jnp.where(zl == 0, owned[1], owned[0]),
        ],
        axis=0,
    ).astype(jnp.float32)
    kept_deltas = jnp.sum(skip_flags.astype(jnp.float32)[:, None, None] * cached_deltas, axis=0)
    resting = hidden_state + kept_deltas
    fresh_delta = head_total * gate_values[None, :]
    mixed_state = resting + fresh_delta
    return (mixed_state, fresh_delta)


def solution(mesh):
    placed = (
        P(("groups", "seq"), ("wt", "head")),
        P(("groups", "seq"), ("wt", "head")),
        P(("groups", "seq"), ("wt", "head")),
        P(("wt", "head"), "seq"),
        P(("groups", "wt", "head")),
        P(("groups", "seq"), ("wt", "head")),
        P(None, ("groups", "seq"), ("wt", "head")),
        P("groups"),
    )

    def local(*args):
        sizes = tuple(mesh.shape[name] for name in ("seq", "wt", "head"))
        rows, features = args[0].shape
        if sizes == (4, 2, 2) and rows % 32 == 0 and features % (2 * HEAD_DIM) == 0:
            return local_heads(*args)
        return local_general(*args)

    return jax.shard_map(
        local,
        mesh=mesh,
        in_specs=placed,
        out_specs=(P(("groups", "seq"), ("wt", "head")), P(("groups", "seq"), ("wt", "head"))),
        check_vma=False,
    )
```

```python
import jax
import jax.numpy as jnp
from jax import lax
from jax.experimental import pallas as pl
from jax.experimental.pallas import tpu as pltpu
from jax.sharding import PartitionSpec as P

HEAD_DIM = 128
VMEM_BYTES = 48 * 1024 * 1024
PACK_BYTES = 59 * 1024 * 1024 + 400 * 1024
LOG2_E = 1.4426950408889634


def attend(state_in, key_rows, value_rows, query_heads, score_scale):
    key_count = key_rows.shape[0]
    head_count = query_heads.shape[1]
    blocks = -(-key_count // 1024)
    while key_count % blocks:
        blocks = blocks + 1
    block_size = key_count // blocks

    def one_block(block_index, state_now):
        row_peak, row_total, weighted = state_now
        start_row = block_index * block_size
        key_block = lax.dynamic_slice_in_dim(key_rows, start_row, block_size, 0)
        value_block = lax.dynamic_slice_in_dim(value_rows, start_row, block_size, 0)
        key_heads = key_block.reshape(block_size, head_count, HEAD_DIM)
        value_heads = value_block.reshape(block_size, head_count, HEAD_DIM)
        scores = (
            jnp.einsum("ihd,jhd->hij", query_heads, key_heads, preferred_element_type=jnp.float32)
            * score_scale
        )
        new_peak = jnp.maximum(row_peak, jnp.max(scores, axis=2))
        exp_scores = jnp.exp(scores - new_peak[:, :, None])
        rescale = jnp.exp(row_peak - new_peak)
        row_total = row_total * rescale + jnp.sum(exp_scores, axis=2)
        weighted = weighted * rescale[:, :, None] + jnp.einsum(
            "hij,jhd->hid",
            exp_scores.astype(jnp.bfloat16),
            value_heads,
            preferred_element_type=jnp.float32,
        )
        return (new_peak, row_total, weighted)

    return lax.fori_loop(0, blocks, one_block, state_in)


def finish(state_out, row_count):
    row_peak, row_total, weighted = state_out
    normed = weighted / row_total[:, :, None]
    return normed.transpose(1, 0, 2).reshape(row_count, -1).astype(jnp.bfloat16)


def local_general(
    queries,
    key_vectors,
    value_vectors,
    out_weight,
    gate_values,
    hidden_state,
    cached_deltas,
    skip_flags,
):
    row_count = queries.shape[0]
    head_count = queries.shape[1] // HEAD_DIM
    score_scale = HEAD_DIM ** (-0.5)
    query_heads = queries.reshape(row_count, head_count, HEAD_DIM)
    start_state = (
        jnp.full((head_count, row_count), -1e30, jnp.float32),
        jnp.zeros((head_count, row_count), jnp.float32),
        jnp.zeros((head_count, row_count, HEAD_DIM), jnp.float32),
    )
    gathered_keys, gathered_values, gathered_weight = (
        lax.all_gather(key_vectors, "seq", axis=0, tiled=True),
        lax.all_gather(value_vectors, "seq", axis=0, tiled=True),
        lax.all_gather(out_weight, "seq", axis=1, tiled=True),
    )
    final_state = attend(start_state, gathered_keys, gathered_values, query_heads, score_scale)
    attention_out = finish(final_state, row_count)
    partial_sums = jnp.dot(attention_out, gathered_weight, preferred_element_type=jnp.float32)
    head_total = lax.psum_scatter(
        partial_sums.astype(jnp.bfloat16), ("wt", "head"), scatter_dimension=1, tiled=True
    ).astype(jnp.float32)
    fresh_delta = head_total * gate_values[None, :]
    kept_deltas = jnp.sum(skip_flags.astype(jnp.float32)[:, None, None] * cached_deltas, axis=0)
    mixed_state = hidden_state + kept_deltas + fresh_delta
    return (mixed_state, fresh_delta)


def bits():
    z = lax.axis_index("seq")
    return lax.div(z, 2), lax.rem(z, 2)


def flip(bit, value):
    return 1 - bit if value else bit


def pack_kernel(queries, keys, values, *refs):
    outs, sems = refs[:4], refs[4]
    rows, width = queries.shape[0], outs[0].shape[1]
    half = rows // 2
    zh, zl = bits()
    copies = []
    for k in range(4):
        part = pl.ds(pl.multiple_of(flip(zh, k // 2) * half, 16), half)
        columns = pl.ds(pl.multiple_of(flip(zl, k % 2) * width, 128), width)
        moves = [
            (keys.at[part, columns], outs[k].at[pl.ds(0, half), :]),
            (values.at[part, columns], outs[k].at[pl.ds(half, half), :]),
        ]
        if k < 2:
            moves.append((queries.at[:, columns], outs[k].at[pl.ds(rows, rows), :]))
        for start, end in moves:
            copies.append(pltpu.make_async_copy(start, end, sems.at[len(copies)]))
    for copy in copies:
        copy.start()
    for copy in copies:
        copy.wait()


def join_kernel(*refs):
    blocks, joined = refs[:4], refs[4]
    rows = joined.shape[0] // 4
    for k, block in enumerate(blocks):
        joined[k * rows : (k + 1) * rows, :] = block[:rows, :]


def attention_kernel(*refs):
    blocks, sibling = refs[:4], refs[4]
    outs, key_all, value_all, query_all = refs[5:7], refs[7], refs[8], refs[9]
    rows = outs[0].shape[0]
    half = rows // 2
    for k in range(4):
        here, there = slice(k * half, (k + 1) * half), slice((4 + k) * half, (5 + k) * half)
        key_all[here, :] = blocks[k][:half, :]
        value_all[here, :] = blocks[k][half:rows, :]
        key_all[there, :] = sibling[k * rows : k * rows + half, :]
        value_all[there, :] = sibling[k * rows + half : (k + 1) * rows, :]
    x = lax.axis_index("wt")
    for k in range(2):
        at = pl.ds(pl.multiple_of(flip(x, k) * rows, 16), rows)
        query_all[at, :] = blocks[k][rows:, :]
    for h in range(outs[0].shape[1] // HEAD_DIM):
        columns = slice(h * HEAD_DIM, (h + 1) * HEAD_DIM)
        scores = lax.dot_general(
            query_all[:, columns],
            key_all[:, columns],
            (((1,), (1,)), ((), ())),
            preferred_element_type=jnp.float32,
        )
        peak = jnp.max(scores, axis=1, keepdims=True)
        weights = jnp.exp2((scores - peak) * (LOG2_E * HEAD_DIM ** (-0.5)))
        total = jnp.sum(weights, axis=1, keepdims=True)
        result = jnp.dot(
            weights.astype(jnp.bfloat16), value_all[:, columns], preferred_element_type=jnp.float32
        )
        result = (result / total).astype(outs[0].dtype)
        for part, out in enumerate(outs):
            out[:, columns] = result[part * rows : (part + 1) * rows]


def multiply(shards, weight, weight_c, held):
    rows = shards[0].shape[0]
    zh, zl = bits()
    core = lax.axis_index("head")
    for m, shard in enumerate(shards):
        held[m * rows : (m + 1) * rows, :] = shard[...]
    total = None
    for other, block in enumerate((weight, weight_c)):
        high = 2 * lax.rem(flip(core, other) + zh, 2)
        left = jnp.concatenate(
            [
                held[pl.ds(pl.multiple_of((high + flip(zl, low)) * rows, 16), rows), :]
                for low in range(2)
            ],
            axis=1,
        )
        term = jnp.dot(left, block[...], preferred_element_type=jnp.float32)
        total = term if total is None else total + term
    return total


def sent_kernel(*refs):
    shards, (weight, weight_c, out, held) = refs[:4], refs[4:]
    out[...] = multiply(shards, weight, weight_c, held).astype(out.dtype)


def kept_kernel(*refs):
    shards, (weight, weight_c, out, held) = refs[:4], refs[4:]
    out[...] = multiply(shards, weight, weight_c, held)


def add_kernel(kept, arrived, out):
    out[...] = (kept[...] + arrived[...].astype(jnp.float32)).astype(out.dtype)


def rest_kernel(flags, hidden, cached, out):
    total = hidden[...]
    for layer in range(cached.shape[0]):
        total = total + flags[layer].astype(jnp.float32) * cached[layer]
    out[...] = total


def final_kernel(owned, gate, resting, mixed, fresh):
    delta = owned[...].astype(jnp.float32) * gate[...]
    fresh[...] = delta
    mixed[...] = resting[...] + delta


def along(shard, m):
    return lax.ppermute(shard, "seq", [(z, z ^ m) for z in range(4)])


def call(kernel, args, outs, scratch=(), space=pltpu.VMEM, flops=0, vmem=VMEM_BYTES):
    spaces = [pltpu.SMEM if arg.dtype == jnp.int32 else space for arg in args]
    return pl.pallas_call(
        kernel,
        in_specs=[pl.BlockSpec(memory_space=place) for place in spaces],
        out_specs=[pl.BlockSpec(memory_space=pltpu.VMEM)] * len(outs),
        out_shape=[jax.ShapeDtypeStruct(shape, dtype) for shape, dtype in outs],
        scratch_shapes=list(scratch),
        compiler_params=pltpu.CompilerParams(vmem_limit_bytes=vmem),
        cost_estimate=pl.CostEstimate(flops=flops, bytes_accessed=0, transcendentals=0),
    )(*args)


def local_heads(
    queries,
    key_vectors,
    value_vectors,
    out_weight,
    gate_values,
    hidden_state,
    cached_deltas,
    skip_flags,
):
    rows, features = queries.shape
    width = features // 2
    depth, columns = out_weight.shape
    swap = [(0, 1), (1, 0)]
    bf16 = jnp.bfloat16

    packed = call(
        pack_kernel,
        (queries, key_vectors, value_vectors),
        [((2 * rows, width), bf16)] * 2 + [((rows, width), bf16)] * 2,
        [pltpu.SemaphoreType.DMA((10,))],
        space=pl.ANY,
        vmem=PACK_BYTES,
    )
    late_weight, _ = lax.optimization_barrier((out_weight, packed[0]))
    weight_c = lax.ppermute(late_weight, "head", swap)
    moved = []
    for k in range(4):
        k1, k0 = k // 2, k % 2
        pairs = []
        for zz in range(4):
            for cc in range(2):
                to_z = 2 * cc + ((zz % 2) ^ k0)
                pairs.append((zz * 2 + cc, to_z * 2 + ((zz // 2) ^ k1)))
        moved.append(lax.ppermute(packed[k], ("seq", "head"), pairs))
    (joined,) = call(join_kernel, moved, [((4 * rows, width), bf16)])
    sibling = lax.ppermute(joined, "head", swap)
    sibling, _ = lax.optimization_barrier((sibling, weight_c))
    parts = call(
        attention_kernel,
        moved + [sibling],
        [((rows, width), bf16)] * 2,
        [
            pltpu.VMEM((4 * rows, width), bf16),
            pltpu.VMEM((4 * rows, width), bf16),
            pltpu.VMEM((2 * rows, width), bf16),
        ],
        flops=4 * (2 * rows) * (4 * rows) * width,
    )

    flops = 4 * rows * depth * columns
    held = [pltpu.VMEM((4 * rows, width), bf16)]
    gathers = []
    for kept in range(2):
        shards = [parts[1 - kept]]
        for m in range(1, 4):
            pairs = [(z, z ^ m) for z in range(4)]
            shards.append(lax.ppermute(parts[(1 - kept) ^ (m % 2)], "seq", pairs))
        gathers.append(shards)
    (send,) = call(
        sent_kernel,
        gathers[0] + [out_weight, weight_c],
        [((rows, columns), bf16)],
        held,
        flops=flops,
    )
    arrived = lax.ppermute(send, "wt", swap)
    (kept,) = call(
        kept_kernel,
        gathers[1] + [out_weight, weight_c],
        [((rows, columns), jnp.float32)],
        held,
        flops=8 * flops,
    )
    (summed,) = call(add_kernel, (kept, arrived), [((rows, columns), bf16)])

    pairs = []
    for zz in range(4):
        for xx in range(2):
            for cc in range(2):
                to = ((2 * cc + (xx ^ (zz % 2))) * 2 + zz // 2) * 2 + zz % 2
                pairs.append(((zz * 2 + xx) * 2 + cc, to))
    owned = lax.ppermute(summed, ("seq", "wt", "head"), pairs)
    (resting,) = call(
        rest_kernel, (skip_flags, hidden_state, cached_deltas), [((rows, columns), jnp.float32)]
    )
    return tuple(
        call(
            final_kernel,
            (owned, gate_values[None, :], resting),
            [((rows, columns), jnp.float32)] * 2,
        )
    )


def solution(mesh):
    placed = (
        P(("groups", "seq"), ("wt", "head")),
        P(("groups", "seq"), ("wt", "head")),
        P(("groups", "seq"), ("wt", "head")),
        P(("wt", "head"), "seq"),
        P(("groups", "wt", "head")),
        P(("groups", "seq"), ("wt", "head")),
        P(None, ("groups", "seq"), ("wt", "head")),
        P("groups"),
    )

    def local(*args):
        sizes = tuple(mesh.shape[name] for name in ("seq", "wt", "head"))
        rows, features = args[0].shape
        if sizes == (4, 2, 2) and rows % 32 == 0 and features % (2 * HEAD_DIM) == 0:
            return local_heads(*args)
        return local_general(*args)

    return jax.shard_map(
        local,
        mesh=mesh,
        in_specs=placed,
        out_specs=(P(("groups", "seq"), ("wt", "head")), P(("groups", "seq"), ("wt", "head"))),
        check_vma=False,
    )
```

```python
import jax
import jax.numpy as jnp
from jax import lax
from jax.experimental import pallas as pl
from jax.experimental.pallas import tpu as pltpu
from jax.sharding import PartitionSpec as P

HEAD_DIM = 128
VMEM_BYTES = 48 * 1024 * 1024
PACK_BYTES = 59 * 1024 * 1024 + 400 * 1024
LOG2_E = 1.4426950408889634


def attend(state_in, key_rows, value_rows, query_heads, score_scale):
    key_count = key_rows.shape[0]
    head_count = query_heads.shape[1]
    blocks = -(-key_count // 1024)
    while key_count % blocks:
        blocks = blocks + 1
    block_size = key_count // blocks

    def one_block(block_index, state_now):
        row_peak, row_total, weighted = state_now
        start_row = block_index * block_size
        key_block = lax.dynamic_slice_in_dim(key_rows, start_row, block_size, 0)
        value_block = lax.dynamic_slice_in_dim(value_rows, start_row, block_size, 0)
        key_heads = key_block.reshape(block_size, head_count, HEAD_DIM)
        value_heads = value_block.reshape(block_size, head_count, HEAD_DIM)
        scores = (
            jnp.einsum("ihd,jhd->hij", query_heads, key_heads, preferred_element_type=jnp.float32)
            * score_scale
        )
        new_peak = jnp.maximum(row_peak, jnp.max(scores, axis=2))
        exp_scores = jnp.exp(scores - new_peak[:, :, None])
        rescale = jnp.exp(row_peak - new_peak)
        row_total = row_total * rescale + jnp.sum(exp_scores, axis=2)
        weighted = weighted * rescale[:, :, None] + jnp.einsum(
            "hij,jhd->hid",
            exp_scores.astype(jnp.bfloat16),
            value_heads,
            preferred_element_type=jnp.float32,
        )
        return (new_peak, row_total, weighted)

    return lax.fori_loop(0, blocks, one_block, state_in)


def finish(state_out, row_count):
    row_peak, row_total, weighted = state_out
    normed = weighted / row_total[:, :, None]
    return normed.transpose(1, 0, 2).reshape(row_count, -1).astype(jnp.bfloat16)


def local_general(
    queries,
    key_vectors,
    value_vectors,
    out_weight,
    gate_values,
    hidden_state,
    cached_deltas,
    skip_flags,
):
    row_count = queries.shape[0]
    head_count = queries.shape[1] // HEAD_DIM
    score_scale = HEAD_DIM ** (-0.5)
    query_heads = queries.reshape(row_count, head_count, HEAD_DIM)
    start_state = (
        jnp.full((head_count, row_count), -1e30, jnp.float32),
        jnp.zeros((head_count, row_count), jnp.float32),
        jnp.zeros((head_count, row_count, HEAD_DIM), jnp.float32),
    )
    gathered_keys, gathered_values, gathered_weight = (
        lax.all_gather(key_vectors, "seq", axis=0, tiled=True),
        lax.all_gather(value_vectors, "seq", axis=0, tiled=True),
        lax.all_gather(out_weight, "seq", axis=1, tiled=True),
    )
    final_state = attend(start_state, gathered_keys, gathered_values, query_heads, score_scale)
    attention_out = finish(final_state, row_count)
    partial_sums = jnp.dot(attention_out, gathered_weight, preferred_element_type=jnp.float32)
    head_total = lax.psum_scatter(
        partial_sums.astype(jnp.bfloat16), ("wt", "head"), scatter_dimension=1, tiled=True
    ).astype(jnp.float32)
    fresh_delta = head_total * gate_values[None, :]
    kept_deltas = jnp.sum(skip_flags.astype(jnp.float32)[:, None, None] * cached_deltas, axis=0)
    mixed_state = hidden_state + kept_deltas + fresh_delta
    return (mixed_state, fresh_delta)


def bits():
    z = lax.axis_index("seq")
    return lax.div(z, 2), lax.rem(z, 2)


def flip(bit, value):
    return 1 - bit if value else bit


def pack_kernel(queries, keys, values, *refs):
    outs, stages, read_sems, write_sems = refs[:4], refs[4:8], refs[8], refs[9]
    rows, width = queries.shape[0], outs[0].shape[1]
    half = rows // 2
    zh, zl = bits()
    reads = []
    for k, stage in enumerate(stages):
        part = pl.ds(pl.multiple_of(flip(zh, k // 2) * half, 16), half)
        columns = pl.ds(pl.multiple_of(flip(zl, k % 2) * width, 128), width)
        moves = [
            (keys.at[part, columns], stage.at[pl.ds(0, half), :]),
            (values.at[part, columns], stage.at[pl.ds(half, half), :]),
        ]
        if k < 2:
            moves.append((queries.at[:, columns], stage.at[pl.ds(rows, rows), :]))
        reads.append(
            [
                pltpu.make_async_copy(start, end, read_sems.at[3 * k + i])
                for i, (start, end) in enumerate(moves)
            ]
        )
        for copy in reads[-1]:
            copy.start()
    writes = []
    for k, stage in enumerate(stages):
        for copy in reads[k]:
            copy.wait()
        writes.append(pltpu.make_async_copy(stage, outs[k], write_sems.at[k]))
        writes[-1].start()
    for copy in writes:
        copy.wait()


def join_kernel(*refs):
    blocks, joined = refs[:4], refs[4]
    rows = joined.shape[0] // 4
    for k, block in enumerate(blocks):
        joined[k * rows : (k + 1) * rows, :] = block[:rows, :]


def attention_kernel(*refs):
    blocks, sibling = refs[:4], refs[4]
    outs, key_all, value_all, query_all = refs[5:7], refs[7], refs[8], refs[9]
    rows = outs[0].shape[0]
    half = rows // 2
    for k in range(4):
        here, there = slice(k * half, (k + 1) * half), slice((4 + k) * half, (5 + k) * half)
        key_all[here, :] = blocks[k][:half, :]
        value_all[here, :] = blocks[k][half:rows, :]
        key_all[there, :] = sibling[k * rows : k * rows + half, :]
        value_all[there, :] = sibling[k * rows + half : (k + 1) * rows, :]
    x = lax.axis_index("wt")
    for k in range(2):
        at = pl.ds(pl.multiple_of(flip(x, k) * rows, 16), rows)
        query_all[at, :] = blocks[k][rows:, :]
    for h in range(outs[0].shape[1] // HEAD_DIM):
        columns = slice(h * HEAD_DIM, (h + 1) * HEAD_DIM)
        scores = lax.dot_general(
            query_all[:, columns],
            key_all[:, columns],
            (((1,), (1,)), ((), ())),
            preferred_element_type=jnp.float32,
        )
        peak = jnp.max(scores, axis=1, keepdims=True)
        weights = jnp.exp2((scores - peak) * (LOG2_E * HEAD_DIM ** (-0.5)))
        total = jnp.sum(weights, axis=1, keepdims=True)
        result = jnp.dot(
            weights.astype(jnp.bfloat16), value_all[:, columns], preferred_element_type=jnp.float32
        )
        result = (result / total).astype(outs[0].dtype)
        for part, out in enumerate(outs):
            out[:, columns] = result[part * rows : (part + 1) * rows]


def multiply(shards, weight, weight_c, held):
    rows = shards[0].shape[0]
    zh, zl = bits()
    core = lax.axis_index("head")
    for m, shard in enumerate(shards):
        held[m * rows : (m + 1) * rows, :] = shard[...]
    total = None
    for other, block in enumerate((weight, weight_c)):
        high = 2 * lax.rem(flip(core, other) + zh, 2)
        left = jnp.concatenate(
            [
                held[pl.ds(pl.multiple_of((high + flip(zl, low)) * rows, 16), rows), :]
                for low in range(2)
            ],
            axis=1,
        )
        term = jnp.dot(left, block[...], preferred_element_type=jnp.float32)
        total = term if total is None else total + term
    return total


def project_kernel(*refs):
    shards, (weight, weight_c, out0, out1, held) = refs[:4], refs[4:]
    total = multiply(shards, weight, weight_c, held)
    count = out0.shape[1]
    out0[...] = total[:, :count].astype(out0.dtype)
    out1[...] = total[:, count:].astype(out1.dtype)


def add_kernel(kept, arrived, out):
    out[...] = (kept[...] + arrived[...].astype(jnp.float32)).astype(out.dtype)


def rest_kernel(flags, hidden, cached, out):
    total = hidden[...]
    for layer in range(cached.shape[0]):
        total = total + flags[layer].astype(jnp.float32) * cached[layer]
    out[...] = total


def final_kernel(owned0, owned1, gate, resting, mixed, fresh):
    count = owned0.shape[1]
    for h, owned in enumerate((owned0, owned1)):
        columns = slice(h * count, (h + 1) * count)
        delta = owned[...].astype(jnp.float32) * gate[:, columns]
        fresh[:, columns] = delta
        mixed[:, columns] = resting[:, columns] + delta


def call(
    kernel,
    args,
    outs,
    scratch=(),
    space=pltpu.VMEM,
    out_space=pltpu.VMEM,
    flops=0,
    vmem=VMEM_BYTES,
):
    spaces = [pltpu.SMEM if arg.dtype == jnp.int32 else space for arg in args]
    return pl.pallas_call(
        kernel,
        in_specs=[pl.BlockSpec(memory_space=place) for place in spaces],
        out_specs=[pl.BlockSpec(memory_space=out_space)] * len(outs),
        out_shape=[jax.ShapeDtypeStruct(shape, dtype) for shape, dtype in outs],
        scratch_shapes=list(scratch),
        compiler_params=pltpu.CompilerParams(vmem_limit_bytes=vmem),
        cost_estimate=pl.CostEstimate(flops=flops, bytes_accessed=0, transcendentals=0),
    )(*args)


def local_heads(
    queries,
    key_vectors,
    value_vectors,
    out_weight,
    gate_values,
    hidden_state,
    cached_deltas,
    skip_flags,
):
    rows, features = queries.shape
    width = features // 2
    depth, columns = out_weight.shape
    swap = [(0, 1), (1, 0)]
    bf16 = jnp.bfloat16

    packed = call(
        pack_kernel,
        (queries, key_vectors, value_vectors),
        [((2 * rows, width), bf16)] * 2 + [((rows, width), bf16)] * 2,
        [pltpu.VMEM((2 * rows, width), bf16)] * 2
        + [pltpu.VMEM((rows, width), bf16)] * 2
        + [pltpu.SemaphoreType.DMA((12,)), pltpu.SemaphoreType.DMA((4,))],
        space=pl.ANY,
        out_space=pl.ANY,
        vmem=PACK_BYTES,
    )
    late_weight, _ = lax.optimization_barrier((out_weight, packed[0]))
    weight_c = lax.ppermute(late_weight, "head", swap)
    moved = []
    for k in range(4):
        k1, k0 = k // 2, k % 2
        pairs = []
        for zz in range(4):
            for cc in range(2):
                to_z = 2 * cc + ((zz % 2) ^ k0)
                pairs.append((zz * 2 + cc, to_z * 2 + ((zz // 2) ^ k1)))
        moved.append(lax.ppermute(packed[k], ("seq", "head"), pairs))
    (joined,) = call(join_kernel, moved, [((4 * rows, width), bf16)])
    sibling = lax.ppermute(joined, "head", swap)
    sibling, _ = lax.optimization_barrier((sibling, weight_c))
    parts = call(
        attention_kernel,
        moved + [sibling],
        [((rows, width), bf16)] * 2,
        [
            pltpu.VMEM((4 * rows, width), bf16),
            pltpu.VMEM((4 * rows, width), bf16),
            pltpu.VMEM((2 * rows, width), bf16),
        ],
        flops=4 * (2 * rows) * (4 * rows) * width,
    )

    flops = 4 * rows * depth * columns
    held = [pltpu.VMEM((4 * rows, width), bf16)]
    gathers = []
    for kept in range(2):
        shards = [parts[1 - kept]]
        for m in range(1, 4):
            pairs = [(z, z ^ m) for z in range(4)]
            shards.append(lax.ppermute(parts[(1 - kept) ^ (m % 2)], "seq", pairs))
        gathers.append(shards)
    count = columns // 2
    sent, kept = (
        call(
            project_kernel,
            shards + [out_weight, weight_c],
            [((rows, count), dtype)] * 2,
            held,
            flops=effort * flops,
        )
        for shards, dtype, effort in ((gathers[0], bf16, 1), (gathers[1], jnp.float32, 8))
    )

    pairs = []
    for zz in range(4):
        for xx in range(2):
            for cc in range(2):
                to = ((2 * cc + (xx ^ (zz % 2))) * 2 + zz // 2) * 2 + zz % 2
                pairs.append(((zz * 2 + xx) * 2 + cc, to))
    owned = []
    for part, total in zip(sent, kept):
        arrived = lax.ppermute(part, "wt", swap)
        (summed,) = call(add_kernel, (total, arrived), [((rows, count), bf16)])
        owned.append(lax.ppermute(summed, ("seq", "wt", "head"), pairs))
    (resting,) = call(
        rest_kernel, (skip_flags, hidden_state, cached_deltas), [((rows, columns), jnp.float32)]
    )
    return tuple(
        call(
            final_kernel,
            (*owned, gate_values[None, :], resting),
            [((rows, columns), jnp.float32)] * 2,
        )
    )


def solution(mesh):
    placed = (
        P(("groups", "seq"), ("wt", "head")),
        P(("groups", "seq"), ("wt", "head")),
        P(("groups", "seq"), ("wt", "head")),
        P(("wt", "head"), "seq"),
        P(("groups", "wt", "head")),
        P(("groups", "seq"), ("wt", "head")),
        P(None, ("groups", "seq"), ("wt", "head")),
        P("groups"),
    )

    def local(*args):
        sizes = tuple(mesh.shape[name] for name in ("seq", "wt", "head"))
        rows, features = args[0].shape
        if sizes == (4, 2, 2) and rows % 32 == 0 and features % (2 * HEAD_DIM) == 0 and args[3].shape[1] % 256 == 0:
            return local_heads(*args)
        return local_general(*args)

    return jax.shard_map(
        local,
        mesh=mesh,
        in_specs=placed,
        out_specs=(P(("groups", "seq"), ("wt", "head")), P(("groups", "seq"), ("wt", "head"))),
        check_vma=False,
    )
```

```python
import functools

import jax
import jax.numpy as jnp
from jax import lax
from jax.experimental import pallas as pl
from jax.experimental.pallas import tpu as pltpu
from jax.sharding import PartitionSpec as P

HEAD_DIM = 128
VMEM_BYTES = 48 * 1024 * 1024
PACK_BYTES = 59 * 1024 * 1024 + 400 * 1024
LOG2_E = 1.4426950408889634


def attend(state_in, key_rows, value_rows, query_heads, score_scale):
    key_count = key_rows.shape[0]
    head_count = query_heads.shape[1]
    blocks = -(-key_count // 1024)
    while key_count % blocks:
        blocks = blocks + 1
    block_size = key_count // blocks

    def one_block(block_index, state_now):
        row_peak, row_total, weighted = state_now
        start_row = block_index * block_size
        key_block = lax.dynamic_slice_in_dim(key_rows, start_row, block_size, 0)
        value_block = lax.dynamic_slice_in_dim(value_rows, start_row, block_size, 0)
        key_heads = key_block.reshape(block_size, head_count, HEAD_DIM)
        value_heads = value_block.reshape(block_size, head_count, HEAD_DIM)
        scores = (
            jnp.einsum("ihd,jhd->hij", query_heads, key_heads, preferred_element_type=jnp.float32)
            * score_scale
        )
        new_peak = jnp.maximum(row_peak, jnp.max(scores, axis=2))
        exp_scores = jnp.exp(scores - new_peak[:, :, None])
        rescale = jnp.exp(row_peak - new_peak)
        row_total = row_total * rescale + jnp.sum(exp_scores, axis=2)
        weighted = weighted * rescale[:, :, None] + jnp.einsum(
            "hij,jhd->hid",
            exp_scores.astype(jnp.bfloat16),
            value_heads,
            preferred_element_type=jnp.float32,
        )
        return (new_peak, row_total, weighted)

    return lax.fori_loop(0, blocks, one_block, state_in)


def finish(state_out, row_count):
    row_peak, row_total, weighted = state_out
    normed = weighted / row_total[:, :, None]
    return normed.transpose(1, 0, 2).reshape(row_count, -1).astype(jnp.bfloat16)


def local_general(
    queries,
    key_vectors,
    value_vectors,
    out_weight,
    gate_values,
    hidden_state,
    cached_deltas,
    skip_flags,
):
    row_count = queries.shape[0]
    head_count = queries.shape[1] // HEAD_DIM
    score_scale = HEAD_DIM ** (-0.5)
    query_heads = queries.reshape(row_count, head_count, HEAD_DIM)
    start_state = (
        jnp.full((head_count, row_count), -1e30, jnp.float32),
        jnp.zeros((head_count, row_count), jnp.float32),
        jnp.zeros((head_count, row_count, HEAD_DIM), jnp.float32),
    )
    gathered_keys, gathered_values, gathered_weight = (
        lax.all_gather(key_vectors, "seq", axis=0, tiled=True),
        lax.all_gather(value_vectors, "seq", axis=0, tiled=True),
        lax.all_gather(out_weight, "seq", axis=1, tiled=True),
    )
    final_state = attend(start_state, gathered_keys, gathered_values, query_heads, score_scale)
    attention_out = finish(final_state, row_count)
    partial_sums = jnp.dot(attention_out, gathered_weight, preferred_element_type=jnp.float32)
    head_total = lax.psum_scatter(
        partial_sums.astype(jnp.bfloat16), ("wt", "head"), scatter_dimension=1, tiled=True
    ).astype(jnp.float32)
    fresh_delta = head_total * gate_values[None, :]
    kept_deltas = jnp.sum(skip_flags.astype(jnp.float32)[:, None, None] * cached_deltas, axis=0)
    mixed_state = hidden_state + kept_deltas + fresh_delta
    return (mixed_state, fresh_delta)


def bits():
    z = lax.axis_index("seq")
    return lax.div(z, 2), lax.rem(z, 2)


def flip(bit, value):
    return 1 - bit if value else bit


def pack_kernel(queries, keys, values, *refs):
    outs, stages, read_sems, write_sems = refs[:4], refs[4:8], refs[8], refs[9]
    rows, width = queries.shape[0], outs[0].shape[1]
    half = rows // 2
    zh, zl = bits()
    reads = []
    for k, stage in enumerate(stages):
        part = pl.ds(pl.multiple_of(flip(zh, k // 2) * half, 16), half)
        columns = pl.ds(pl.multiple_of(flip(zl, k % 2) * width, 128), width)
        moves = [
            (keys.at[part, columns], stage.at[pl.ds(0, half), :]),
            (values.at[part, columns], stage.at[pl.ds(half, half), :]),
        ]
        if k < 2:
            moves.append((queries.at[:, columns], stage.at[pl.ds(rows, rows), :]))
        reads.append(
            [
                pltpu.make_async_copy(start, end, read_sems.at[3 * k + i])
                for i, (start, end) in enumerate(moves)
            ]
        )
        for copy in reads[-1]:
            copy.start()
    writes = []
    for k, stage in enumerate(stages):
        for copy in reads[k]:
            copy.wait()
        writes.append(pltpu.make_async_copy(stage, outs[k], write_sems.at[k]))
        writes[-1].start()
    for copy in writes:
        copy.wait()


def join_kernel(*refs):
    blocks, joined = refs[:4], refs[4]
    rows = joined.shape[0] // 4
    for k, block in enumerate(blocks):
        joined[k * rows : (k + 1) * rows, :] = block[:rows, :]


def attention_kernel(*refs):
    blocks, sibling = refs[:4], refs[4]
    sent, kept, key_all, value_all, query_all = refs[5:]
    rows = sent.shape[0]
    half = rows // 2
    for k in range(4):
        here, there = slice(k * half, (k + 1) * half), slice((4 + k) * half, (5 + k) * half)
        key_all[here, :] = blocks[k][:half, :]
        value_all[here, :] = blocks[k][half:rows, :]
        key_all[there, :] = sibling[k * rows : k * rows + half, :]
        value_all[there, :] = sibling[k * rows + half : (k + 1) * rows, :]
    _, zl = bits()
    x = lax.axis_index("wt")
    for k in range(2):
        for part in range(2):
            at = rows + flip(x, part == 0) * half
            to = (part * 2 + flip(zl, k)) * half
            query_all[pl.ds(pl.multiple_of(to, 16), half), :] = blocks[k][
                pl.ds(pl.multiple_of(at, 16), half), :
            ]
    for h in range(sent.shape[1] // HEAD_DIM):
        columns = slice(h * HEAD_DIM, (h + 1) * HEAD_DIM)
        scores = lax.dot_general(
            query_all[:, columns],
            key_all[:, columns],
            (((1,), (1,)), ((), ())),
            preferred_element_type=jnp.float32,
        )
        peak = jnp.max(scores, axis=1, keepdims=True)
        weights = jnp.exp2((scores - peak) * (LOG2_E * HEAD_DIM ** (-0.5)))
        total = jnp.sum(weights, axis=1, keepdims=True)
        result = jnp.dot(
            weights.astype(jnp.bfloat16), value_all[:, columns], preferred_element_type=jnp.float32
        )
        result = (result / total).astype(sent.dtype)
        sent[:, columns] = result[:rows]
        kept[:, columns] = result[rows:]


def multiply(shards, weight, weight_c, held):
    rows = shards[0].shape[0]
    zh, zl = bits()
    core = lax.axis_index("head")
    for m, shard in enumerate(shards):
        held[m * rows : (m + 1) * rows, :] = shard[...]
    total = None
    for other, block in enumerate((weight, weight_c)):
        high = 2 * lax.rem(flip(core, other) + zh, 2)
        left = jnp.concatenate(
            [
                held[pl.ds(pl.multiple_of((high + flip(zl, low)) * rows, 16), rows), :]
                for low in range(2)
            ],
            axis=1,
        )
        term = jnp.dot(left, block[...], preferred_element_type=jnp.float32)
        total = term if total is None else total + term
    return total


def project_kernel(kept, *refs):
    shards, (weight, weight_c, out0, out1, held) = refs[:4], refs[4:]
    total = multiply(shards, weight, weight_c, held)
    half = out0.shape[0]
    x = lax.axis_index("wt")
    for low in range(2):
        part = total[low * half : (low + 1) * half].astype(out0.dtype)
        first = flip(x, low) == 1 - kept

        @pl.when(first)
        def _():
            out0[...] = part

        @pl.when(jnp.logical_not(first))
        def _():
            out1[...] = part


def add_kernel(kept, arrived, out):
    out[...] = (kept[...] + arrived[...].astype(jnp.float32)).astype(out.dtype)


def rest_kernel(flags, hidden, cached, out):
    total = hidden[...]
    for layer in range(cached.shape[0]):
        total = total + flags[layer].astype(jnp.float32) * cached[layer]
    out[...] = total


def final_kernel(owned0, owned1, gate, resting, mixed, fresh):
    half = owned0.shape[0]
    _, zl = bits()
    for p, owned in enumerate((owned0, owned1)):
        rows = pl.ds(pl.multiple_of(flip(zl, p) * half, 16), half)
        delta = owned[...].astype(jnp.float32) * gate[...]
        fresh[rows, :] = delta
        mixed[rows, :] = resting[rows, :] + delta


def along(shard, m):
    return lax.ppermute(shard, "seq", [(z, z ^ m) for z in range(4)])


def call(
    kernel,
    args,
    outs,
    scratch=(),
    space=pltpu.VMEM,
    out_space=pltpu.VMEM,
    flops=0,
    vmem=VMEM_BYTES,
):
    spaces = [pltpu.SMEM if arg.dtype == jnp.int32 else space for arg in args]
    return pl.pallas_call(
        kernel,
        in_specs=[pl.BlockSpec(memory_space=place) for place in spaces],
        out_specs=[pl.BlockSpec(memory_space=out_space)] * len(outs),
        out_shape=[jax.ShapeDtypeStruct(shape, dtype) for shape, dtype in outs],
        scratch_shapes=list(scratch),
        compiler_params=pltpu.CompilerParams(vmem_limit_bytes=vmem),
        cost_estimate=pl.CostEstimate(flops=flops, bytes_accessed=0, transcendentals=0),
    )(*args)


def local_heads(
    queries,
    key_vectors,
    value_vectors,
    out_weight,
    gate_values,
    hidden_state,
    cached_deltas,
    skip_flags,
):
    rows, features = queries.shape
    width = features // 2
    depth, columns = out_weight.shape
    swap = [(0, 1), (1, 0)]
    bf16 = jnp.bfloat16

    packed = call(
        pack_kernel,
        (queries, key_vectors, value_vectors),
        [((2 * rows, width), bf16)] * 2 + [((rows, width), bf16)] * 2,
        [pltpu.VMEM((2 * rows, width), bf16)] * 2
        + [pltpu.VMEM((rows, width), bf16)] * 2
        + [pltpu.SemaphoreType.DMA((12,)), pltpu.SemaphoreType.DMA((4,))],
        space=pl.ANY,
        out_space=pl.ANY,
        vmem=PACK_BYTES,
    )
    moved = []
    for k in range(4):
        k1, k0 = k // 2, k % 2
        pairs = []
        for zz in range(4):
            for cc in range(2):
                to_z = 2 * cc + ((zz % 2) ^ k0)
                pairs.append((zz * 2 + cc, to_z * 2 + ((zz // 2) ^ k1)))
        moved.append(lax.ppermute(packed[k], ("seq", "head"), pairs))
    (joined,) = call(join_kernel, moved, [((4 * rows, width), bf16)])
    sibling = lax.ppermute(joined, "head", swap)
    late_weight, _ = lax.optimization_barrier((out_weight, sibling))
    weight_c = lax.ppermute(late_weight, "head", swap)
    parts = call(
        attention_kernel,
        moved + [sibling],
        [((rows, width), bf16)] * 2,
        [
            pltpu.VMEM((4 * rows, width), bf16),
            pltpu.VMEM((4 * rows, width), bf16),
            pltpu.VMEM((2 * rows, width), bf16),
        ],
        flops=4 * (2 * rows) * (4 * rows) * width,
    )

    flops = 4 * rows * depth * columns
    held = [pltpu.VMEM((4 * rows, width), bf16)]
    half = rows // 2
    gathers = []
    for part in parts:
        near = along(part, 1)
        two = along(part, 2)
        gathers.append([part, near, two, along(two, 1)])
    sent, kept = (
        call(
            functools.partial(project_kernel, i),
            gathers[i] + [out_weight, weight_c],
            [((half, columns), dtype)] * 2,
            held,
            flops=effort * flops,
        )
        for i, dtype, effort in ((0, bf16, 1), (1, jnp.float32, 8))
    )

    owned = []
    for p in range(2):
        arrived = lax.ppermute(sent[p], "wt", swap)
        (summed,) = call(add_kernel, (kept[p], arrived), [((half, columns), bf16)])
        pairs = []
        for zz in range(4):
            for xx in range(2):
                for cc in range(2):
                    to = ((2 * cc + (p ^ xx)) * 2 + zz // 2) * 2 + zz % 2
                    pairs.append(((zz * 2 + xx) * 2 + cc, to))
        owned.append(lax.ppermute(summed, ("seq", "wt", "head"), pairs))
    (resting,) = call(
        rest_kernel, (skip_flags, hidden_state, cached_deltas), [((rows, columns), jnp.float32)]
    )
    return tuple(
        call(
            final_kernel,
            (*owned, gate_values[None, :], resting),
            [((rows, columns), jnp.float32)] * 2,
        )
    )


def solution(mesh):
    placed = (
        P(("groups", "seq"), ("wt", "head")),
        P(("groups", "seq"), ("wt", "head")),
        P(("groups", "seq"), ("wt", "head")),
        P(("wt", "head"), "seq"),
        P(("groups", "wt", "head")),
        P(("groups", "seq"), ("wt", "head")),
        P(None, ("groups", "seq"), ("wt", "head")),
        P("groups"),
    )

    def local(*args):
        sizes = tuple(mesh.shape[name] for name in ("seq", "wt", "head"))
        rows, features = args[0].shape
        if sizes == (4, 2, 2) and rows % 32 == 0 and features % (2 * HEAD_DIM) == 0:
            return local_heads(*args)
        return local_general(*args)

    return jax.shard_map(
        local,
        mesh=mesh,
        in_specs=placed,
        out_specs=(P(("groups", "seq"), ("wt", "head")), P(("groups", "seq"), ("wt", "head"))),
        check_vma=False,
    )
```

```python
import functools

import jax
import jax.numpy as jnp
from jax import lax
from jax.experimental import pallas as pl
from jax.experimental.pallas import tpu as pltpu
from jax.sharding import PartitionSpec as P

HEAD_DIM = 128
VMEM_BYTES = 48 * 1024 * 1024
PACK_BYTES = 59 * 1024 * 1024 + 400 * 1024
LOG2_E = 1.4426950408889634


def attend(state_in, key_rows, value_rows, query_heads, score_scale):
    key_count = key_rows.shape[0]
    head_count = query_heads.shape[1]
    blocks = -(-key_count // 1024)
    while key_count % blocks:
        blocks = blocks + 1
    block_size = key_count // blocks

    def one_block(block_index, state_now):
        row_peak, row_total, weighted = state_now
        start_row = block_index * block_size
        key_block = lax.dynamic_slice_in_dim(key_rows, start_row, block_size, 0)
        value_block = lax.dynamic_slice_in_dim(value_rows, start_row, block_size, 0)
        key_heads = key_block.reshape(block_size, head_count, HEAD_DIM)
        value_heads = value_block.reshape(block_size, head_count, HEAD_DIM)
        scores = (
            jnp.einsum("ihd,jhd->hij", query_heads, key_heads, preferred_element_type=jnp.float32)
            * score_scale
        )
        new_peak = jnp.maximum(row_peak, jnp.max(scores, axis=2))
        exp_scores = jnp.exp(scores - new_peak[:, :, None])
        rescale = jnp.exp(row_peak - new_peak)
        row_total = row_total * rescale + jnp.sum(exp_scores, axis=2)
        weighted = weighted * rescale[:, :, None] + jnp.einsum(
            "hij,jhd->hid",
            exp_scores.astype(jnp.bfloat16),
            value_heads,
            preferred_element_type=jnp.float32,
        )
        return (new_peak, row_total, weighted)

    return lax.fori_loop(0, blocks, one_block, state_in)


def finish(state_out, row_count):
    row_peak, row_total, weighted = state_out
    normed = weighted / row_total[:, :, None]
    return normed.transpose(1, 0, 2).reshape(row_count, -1).astype(jnp.bfloat16)


def local_general(
    queries,
    key_vectors,
    value_vectors,
    out_weight,
    gate_values,
    hidden_state,
    cached_deltas,
    skip_flags,
):
    row_count = queries.shape[0]
    head_count = queries.shape[1] // HEAD_DIM
    score_scale = HEAD_DIM ** (-0.5)
    query_heads = queries.reshape(row_count, head_count, HEAD_DIM)
    start_state = (
        jnp.full((head_count, row_count), -1e30, jnp.float32),
        jnp.zeros((head_count, row_count), jnp.float32),
        jnp.zeros((head_count, row_count, HEAD_DIM), jnp.float32),
    )
    gathered_keys, gathered_values, gathered_weight = (
        lax.all_gather(key_vectors, "seq", axis=0, tiled=True),
        lax.all_gather(value_vectors, "seq", axis=0, tiled=True),
        lax.all_gather(out_weight, "seq", axis=1, tiled=True),
    )
    final_state = attend(start_state, gathered_keys, gathered_values, query_heads, score_scale)
    attention_out = finish(final_state, row_count)
    partial_sums = jnp.dot(attention_out, gathered_weight, preferred_element_type=jnp.float32)
    head_total = lax.psum_scatter(
        partial_sums.astype(jnp.bfloat16), ("wt", "head"), scatter_dimension=1, tiled=True
    ).astype(jnp.float32)
    fresh_delta = head_total * gate_values[None, :]
    kept_deltas = jnp.sum(skip_flags.astype(jnp.float32)[:, None, None] * cached_deltas, axis=0)
    mixed_state = hidden_state + kept_deltas + fresh_delta
    return (mixed_state, fresh_delta)


def bits():
    z = lax.axis_index("seq")
    return lax.div(z, 2), lax.rem(z, 2)


def flip(bit, value):
    return 1 - bit if value else bit


def pack_kernel(queries, keys, values, *refs):
    outs, stages, read_sems, write_sems = refs[:4], refs[4:8], refs[8], refs[9]
    rows, width = queries.shape[0], outs[0].shape[1]
    half = rows // 2
    zh, zl = bits()
    reads = []
    for k, stage in enumerate(stages):
        part = pl.ds(pl.multiple_of(flip(zh, k // 2) * half, 16), half)
        columns = pl.ds(pl.multiple_of(flip(zl, k % 2) * width, 128), width)
        moves = [
            (keys.at[part, columns], stage.at[pl.ds(0, half), :]),
            (values.at[part, columns], stage.at[pl.ds(half, half), :]),
        ]
        if k < 2:
            moves.append((queries.at[:, columns], stage.at[pl.ds(rows, rows), :]))
        reads.append(
            [
                pltpu.make_async_copy(start, end, read_sems.at[3 * k + i])
                for i, (start, end) in enumerate(moves)
            ]
        )
        for copy in reads[-1]:
            copy.start()
    writes = []
    for k, stage in enumerate(stages):
        for copy in reads[k]:
            copy.wait()
        writes.append(pltpu.make_async_copy(stage, outs[k], write_sems.at[k]))
        writes[-1].start()
    for copy in writes:
        copy.wait()


def join_kernel(*refs):
    blocks, joined = refs[:4], refs[4]
    rows = joined.shape[0] // 4
    for k, block in enumerate(blocks):
        joined[k * rows : (k + 1) * rows, :] = block[:rows, :]


def attention_kernel(*refs):
    blocks, sibling = refs[:4], refs[4]
    sent, kept, key_all, value_all, query_all = refs[5:]
    rows = sent.shape[0]
    half = rows // 2
    for k in range(4):
        here, there = slice(k * half, (k + 1) * half), slice((4 + k) * half, (5 + k) * half)
        key_all[here, :] = blocks[k][:half, :]
        value_all[here, :] = blocks[k][half:rows, :]
        key_all[there, :] = sibling[k * rows : k * rows + half, :]
        value_all[there, :] = sibling[k * rows + half : (k + 1) * rows, :]
    _, zl = bits()
    x = lax.axis_index("wt")
    for k in range(2):
        for part in range(2):
            at = rows + flip(x, part == 0) * half
            to = (part * 2 + flip(zl, k)) * half
            query_all[pl.ds(pl.multiple_of(to, 16), half), :] = blocks[k][
                pl.ds(pl.multiple_of(at, 16), half), :
            ]
    for h in range(sent.shape[1] // HEAD_DIM):
        columns = slice(h * HEAD_DIM, (h + 1) * HEAD_DIM)
        scores = lax.dot_general(
            query_all[:, columns],
            key_all[:, columns],
            (((1,), (1,)), ((), ())),
            preferred_element_type=jnp.float32,
        )
        peak = jnp.max(scores, axis=1, keepdims=True)
        weights = jnp.exp2((scores - peak) * (LOG2_E * HEAD_DIM ** (-0.5)))
        total = jnp.sum(weights, axis=1, keepdims=True)
        result = jnp.dot(
            weights.astype(jnp.bfloat16), value_all[:, columns], preferred_element_type=jnp.float32
        )
        result = (result / total).astype(sent.dtype)
        sent[:, columns] = result[:rows]
        kept[:, columns] = result[rows:]


def multiply(shards, weight, weight_c, held):
    rows = shards[0].shape[0]
    zh, zl = bits()
    core = lax.axis_index("head")
    for m, shard in enumerate(shards):
        held[m * rows : (m + 1) * rows, :] = shard[...]
    total = None
    for other, block in enumerate((weight, weight_c)):
        high = 2 * lax.rem(flip(core, other) + zh, 2)
        left = jnp.concatenate(
            [
                held[pl.ds(pl.multiple_of((high + flip(zl, low)) * rows, 16), rows), :]
                for low in range(2)
            ],
            axis=1,
        )
        term = jnp.dot(left, block[...], preferred_element_type=jnp.float32)
        total = term if total is None else total + term
    return total


def project_kernel(kept, *refs):
    shards, (weight, weight_c, out0, out1, held) = refs[:4], refs[4:]
    total = multiply(shards, weight, weight_c, held)
    half = out0.shape[0]
    x = lax.axis_index("wt")
    for low in range(2):
        part = total[low * half : (low + 1) * half].astype(out0.dtype)
        first = flip(x, low) == 1 - kept

        @pl.when(first)
        def _():
            out0[...] = part

        @pl.when(jnp.logical_not(first))
        def _():
            out1[...] = part


def add_kernel(kept, arrived, out):
    out[...] = (kept[...] + arrived[...].astype(jnp.float32)).astype(out.dtype)


def rest_kernel(flags, hidden, cached, out):
    total = hidden[...]
    for layer in range(cached.shape[0]):
        total = total + flags[layer].astype(jnp.float32) * cached[layer]
    out[...] = total


def final_kernel(owned0, owned1, gate, resting, mixed, fresh):
    half = owned0.shape[0]
    _, zl = bits()
    for p, owned in enumerate((owned0, owned1)):
        rows = pl.ds(pl.multiple_of(flip(zl, p) * half, 16), half)
        delta = owned[...].astype(jnp.float32) * gate[...]
        fresh[rows, :] = delta
        mixed[rows, :] = resting[rows, :] + delta


def along(shard, m):
    return lax.ppermute(shard, "seq", [(z, z ^ m) for z in range(4)])


def call(
    kernel,
    args,
    outs,
    scratch=(),
    space=pltpu.VMEM,
    out_space=pltpu.VMEM,
    flops=0,
    vmem=VMEM_BYTES,
):
    spaces = [pltpu.SMEM if arg.dtype == jnp.int32 else space for arg in args]
    return pl.pallas_call(
        kernel,
        in_specs=[pl.BlockSpec(memory_space=place) for place in spaces],
        out_specs=[pl.BlockSpec(memory_space=out_space)] * len(outs),
        out_shape=[jax.ShapeDtypeStruct(shape, dtype) for shape, dtype in outs],
        scratch_shapes=list(scratch),
        compiler_params=pltpu.CompilerParams(vmem_limit_bytes=vmem),
        cost_estimate=pl.CostEstimate(flops=flops, bytes_accessed=0, transcendentals=0),
    )(*args)


def local_heads(
    queries,
    key_vectors,
    value_vectors,
    out_weight,
    gate_values,
    hidden_state,
    cached_deltas,
    skip_flags,
):
    rows, features = queries.shape
    width = features // 2
    depth, columns = out_weight.shape
    swap = [(0, 1), (1, 0)]
    bf16 = jnp.bfloat16

    packed = call(
        pack_kernel,
        (queries, key_vectors, value_vectors),
        [((2 * rows, width), bf16)] * 2 + [((rows, width), bf16)] * 2,
        [pltpu.VMEM((2 * rows, width), bf16)] * 2
        + [pltpu.VMEM((rows, width), bf16)] * 2
        + [pltpu.SemaphoreType.DMA((12,)), pltpu.SemaphoreType.DMA((4,))],
        space=pl.ANY,
        out_space=pl.ANY,
        vmem=PACK_BYTES,
    )
    moved = []
    for k in range(4):
        k1, k0 = k // 2, k % 2
        pairs = []
        for zz in range(4):
            for cc in range(2):
                to_z = 2 * cc + ((zz % 2) ^ k0)
                pairs.append((zz * 2 + cc, to_z * 2 + ((zz // 2) ^ k1)))
        moved.append(lax.ppermute(packed[k], ("seq", "head"), pairs))
    (joined,) = call(join_kernel, moved, [((4 * rows, width), bf16)])
    sibling = lax.ppermute(joined, "head", swap)
    late_weight, _ = lax.optimization_barrier((out_weight, sibling))
    weight_c = lax.ppermute(late_weight, "head", swap)
    parts = call(
        attention_kernel,
        moved + [sibling],
        [((rows, width), bf16)] * 2,
        [
            pltpu.VMEM((4 * rows, width), bf16),
            pltpu.VMEM((4 * rows, width), bf16),
            pltpu.VMEM((2 * rows, width), bf16),
        ],
        flops=4 * (2 * rows) * (4 * rows) * width,
    )

    flops = 4 * rows * depth * columns
    held = [pltpu.VMEM((4 * rows, width), bf16)]
    half = rows // 2
    def projected(i, near, two, far, dtype, effort):
        return call(
            functools.partial(project_kernel, i),
            (parts[i], near, two, far, out_weight, weight_c),
            [((half, columns), dtype)] * 2,
            held,
            flops=effort * flops,
        )

    near = along(parts[0], 1)
    two = along(parts[0], 2)
    late_two, late_part, _ = lax.optimization_barrier((two, parts[1], near))
    sent = projected(0, near, two, along(late_two, 1), bf16, 1)
    near = along(late_part, 1)
    two = along(late_part, 2)
    late_two, _ = lax.optimization_barrier((two, sent[0]))
    kept = projected(1, near, two, along(late_two, 1), jnp.float32, 8)

    owned = []
    for p in range(2):
        arrived = lax.ppermute(sent[p], "wt", swap)
        (summed,) = call(add_kernel, (kept[p], arrived), [((half, columns), bf16)])
        pairs = []
        for zz in range(4):
            for xx in range(2):
                for cc in range(2):
                    to = ((2 * cc + (p ^ xx)) * 2 + zz // 2) * 2 + zz % 2
                    pairs.append(((zz * 2 + xx) * 2 + cc, to))
        owned.append(lax.ppermute(summed, ("seq", "wt", "head"), pairs))
    (resting,) = call(
        rest_kernel, (skip_flags, hidden_state, cached_deltas), [((rows, columns), jnp.float32)]
    )
    return tuple(
        call(
            final_kernel,
            (*owned, gate_values[None, :], resting),
            [((rows, columns), jnp.float32)] * 2,
        )
    )


def solution(mesh):
    placed = (
        P(("groups", "seq"), ("wt", "head")),
        P(("groups", "seq"), ("wt", "head")),
        P(("groups", "seq"), ("wt", "head")),
        P(("wt", "head"), "seq"),
        P(("groups", "wt", "head")),
        P(("groups", "seq"), ("wt", "head")),
        P(None, ("groups", "seq"), ("wt", "head")),
        P("groups"),
    )

    def local(*args):
        sizes = tuple(mesh.shape[name] for name in ("seq", "wt", "head"))
        rows, features = args[0].shape
        if sizes == (4, 2, 2) and rows % 32 == 0 and features % (2 * HEAD_DIM) == 0:
            return local_heads(*args)
        return local_general(*args)

    return jax.shard_map(
        local,
        mesh=mesh,
        in_specs=placed,
        out_specs=(P(("groups", "seq"), ("wt", "head")), P(("groups", "seq"), ("wt", "head"))),
        check_vma=False,
    )
```

```python
import functools

import jax
import jax.numpy as jnp
from jax import lax
from jax.experimental import pallas as pl
from jax.experimental.pallas import tpu as pltpu
from jax.sharding import PartitionSpec as P

HEAD_DIM = 128
VMEM_BYTES = 48 * 1024 * 1024
PACK_BYTES = 53 * 1024 * 1024 + 128 * 1024
LOG2_E = 1.4426950408889634


def attend(state_in, key_rows, value_rows, query_heads, score_scale):
    key_count = key_rows.shape[0]
    head_count = query_heads.shape[1]
    blocks = -(-key_count // 1024)
    while key_count % blocks:
        blocks = blocks + 1
    block_size = key_count // blocks

    def one_block(block_index, state_now):
        row_peak, row_total, weighted = state_now
        start_row = block_index * block_size
        key_block = lax.dynamic_slice_in_dim(key_rows, start_row, block_size, 0)
        value_block = lax.dynamic_slice_in_dim(value_rows, start_row, block_size, 0)
        key_heads = key_block.reshape(block_size, head_count, HEAD_DIM)
        value_heads = value_block.reshape(block_size, head_count, HEAD_DIM)
        scores = (
            jnp.einsum("ihd,jhd->hij", query_heads, key_heads, preferred_element_type=jnp.float32)
            * score_scale
        )
        new_peak = jnp.maximum(row_peak, jnp.max(scores, axis=2))
        exp_scores = jnp.exp(scores - new_peak[:, :, None])
        rescale = jnp.exp(row_peak - new_peak)
        row_total = row_total * rescale + jnp.sum(exp_scores, axis=2)
        weighted = weighted * rescale[:, :, None] + jnp.einsum(
            "hij,jhd->hid",
            exp_scores.astype(jnp.bfloat16),
            value_heads,
            preferred_element_type=jnp.float32,
        )
        return (new_peak, row_total, weighted)

    return lax.fori_loop(0, blocks, one_block, state_in)


def finish(state_out, row_count):
    row_peak, row_total, weighted = state_out
    normed = weighted / row_total[:, :, None]
    return normed.transpose(1, 0, 2).reshape(row_count, -1).astype(jnp.bfloat16)


def local_general(
    queries,
    key_vectors,
    value_vectors,
    out_weight,
    gate_values,
    hidden_state,
    cached_deltas,
    skip_flags,
):
    row_count = queries.shape[0]
    head_count = queries.shape[1] // HEAD_DIM
    score_scale = HEAD_DIM ** (-0.5)
    query_heads = queries.reshape(row_count, head_count, HEAD_DIM)
    start_state = (
        jnp.full((head_count, row_count), -1e30, jnp.float32),
        jnp.zeros((head_count, row_count), jnp.float32),
        jnp.zeros((head_count, row_count, HEAD_DIM), jnp.float32),
    )
    gathered_keys, gathered_values, gathered_weight = (
        lax.all_gather(key_vectors, "seq", axis=0, tiled=True),
        lax.all_gather(value_vectors, "seq", axis=0, tiled=True),
        lax.all_gather(out_weight, "seq", axis=1, tiled=True),
    )
    final_state = attend(start_state, gathered_keys, gathered_values, query_heads, score_scale)
    attention_out = finish(final_state, row_count)
    partial_sums = jnp.dot(attention_out, gathered_weight, preferred_element_type=jnp.float32)
    head_total = lax.psum_scatter(
        partial_sums.astype(jnp.bfloat16), ("wt", "head"), scatter_dimension=1, tiled=True
    ).astype(jnp.float32)
    fresh_delta = head_total * gate_values[None, :]
    kept_deltas = jnp.sum(skip_flags.astype(jnp.float32)[:, None, None] * cached_deltas, axis=0)
    mixed_state = hidden_state + kept_deltas + fresh_delta
    return (mixed_state, fresh_delta)


def bits():
    z = lax.axis_index("seq")
    return lax.div(z, 2), lax.rem(z, 2)


def flip(bit, value):
    return 1 - bit if value else bit


def pack_kernel(queries, keys, values, *refs):
    outs, sems = refs[:4], refs[4]
    rows, width = queries.shape[0], outs[0].shape[1]
    half = rows // 2
    zh, zl = bits()
    copies = []
    for k in range(4):
        part = pl.ds(pl.multiple_of(flip(zh, k // 2) * half, 16), half)
        columns = pl.ds(pl.multiple_of(flip(zl, k % 2) * width, 128), width)
        moves = [
            (keys.at[part, columns], outs[k].at[pl.ds(0, half), :]),
            (values.at[part, columns], outs[k].at[pl.ds(half, half), :]),
        ]
        if k < 2:
            moves.append((queries.at[:, columns], outs[k].at[pl.ds(rows, rows), :]))
        for start, end in moves:
            copies.append(pltpu.make_async_copy(start, end, sems.at[len(copies)]))
    for copy in copies:
        copy.start()
    for copy in copies:
        copy.wait()


def join_kernel(*refs):
    blocks, joined = refs[:4], refs[4]
    rows = joined.shape[0] // 4
    for k, block in enumerate(blocks):
        joined[k * rows : (k + 1) * rows, :] = block[:rows, :]


def attention_kernel(*refs):
    blocks, sibling = refs[:4], refs[4]
    outs, key_all, value_all, query_all = refs[5:7], refs[7], refs[8], refs[9]
    rows = outs[0].shape[0]
    half = rows // 2
    for k in range(4):
        here, there = slice(k * half, (k + 1) * half), slice((4 + k) * half, (5 + k) * half)
        key_all[here, :] = blocks[k][:half, :]
        value_all[here, :] = blocks[k][half:rows, :]
        key_all[there, :] = sibling[k * rows : k * rows + half, :]
        value_all[there, :] = sibling[k * rows + half : (k + 1) * rows, :]
    x = lax.axis_index("wt")
    for k in range(2):
        at = pl.ds(pl.multiple_of(flip(x, k) * rows, 16), rows)
        query_all[at, :] = blocks[k][rows:, :]
    for h in range(outs[0].shape[1] // HEAD_DIM):
        columns = slice(h * HEAD_DIM, (h + 1) * HEAD_DIM)
        scores = lax.dot_general(
            query_all[:, columns],
            key_all[:, columns],
            (((1,), (1,)), ((), ())),
            preferred_element_type=jnp.float32,
        )
        peak = jnp.max(scores, axis=1, keepdims=True)
        weights = jnp.exp2((scores - peak) * (LOG2_E * HEAD_DIM ** (-0.5)))
        total = jnp.sum(weights, axis=1, keepdims=True)
        result = jnp.dot(
            weights.astype(jnp.bfloat16), value_all[:, columns], preferred_element_type=jnp.float32
        )
        result = (result / total).astype(outs[0].dtype)
        for part, out in enumerate(outs):
            out[:, columns] = result[part * rows : (part + 1) * rows]


def multiply(shards, weight, weight_c, held):
    rows = shards[0].shape[0]
    zh, zl = bits()
    core = lax.axis_index("head")
    for m, shard in enumerate(shards):
        held[m * rows : (m + 1) * rows, :] = shard[...]
    total = None
    for other, block in enumerate((weight, weight_c)):
        high = 2 * lax.rem(flip(core, other) + zh, 2)
        left = jnp.concatenate(
            [
                held[pl.ds(pl.multiple_of((high + flip(zl, low)) * rows, 16), rows), :]
                for low in range(2)
            ],
            axis=1,
        )
        term = jnp.dot(left, block[...], preferred_element_type=jnp.float32)
        total = term if total is None else total + term
    return total


def project_kernel(*refs):
    shards, (weight, weight_c, out0, out1, held) = refs[:4], refs[4:]
    total = multiply(shards, weight, weight_c, held)
    count = out0.shape[1]
    out0[...] = total[:, :count].astype(out0.dtype)
    out1[...] = total[:, count:].astype(out1.dtype)


def add_kernel(kept, arrived, out):
    out[...] = (kept[...] + arrived[...].astype(jnp.float32)).astype(out.dtype)


def rest_kernel(flags, hidden, cached, out):
    total = hidden[...]
    for layer in range(cached.shape[0]):
        total = total + flags[layer].astype(jnp.float32) * cached[layer]
    out[...] = total


def final_kernel(first, owned, gate, resting, *refs):
    mixed, fresh, mixed_part, fresh_part, sems = refs[-5:]
    columns = pl.ds(first, owned.shape[1])
    delta = owned[...].astype(jnp.float32) * gate[:, columns]
    fresh_part[...] = delta
    copy_fresh = pltpu.make_async_copy(fresh_part, fresh.at[:, columns], sems.at[0])
    copy_fresh.start()
    mixed_part[...] = resting[:, columns] + delta
    copy_mixed = pltpu.make_async_copy(mixed_part, mixed.at[:, columns], sems.at[1])
    copy_mixed.start()
    copy_fresh.wait()
    copy_mixed.wait()


def call(
    kernel,
    args,
    outs,
    scratch=(),
    space=pltpu.VMEM,
    out_space=pltpu.VMEM,
    flops=0,
    vmem=VMEM_BYTES,
):
    spaces = [pltpu.SMEM if arg.dtype == jnp.int32 else space for arg in args]
    return pl.pallas_call(
        kernel,
        in_specs=[pl.BlockSpec(memory_space=place) for place in spaces],
        out_specs=[pl.BlockSpec(memory_space=out_space)] * len(outs),
        out_shape=[jax.ShapeDtypeStruct(shape, dtype) for shape, dtype in outs],
        scratch_shapes=list(scratch),
        compiler_params=pltpu.CompilerParams(vmem_limit_bytes=vmem),
        cost_estimate=pl.CostEstimate(flops=flops, bytes_accessed=0, transcendentals=0),
    )(*args)


def local_heads(
    queries,
    key_vectors,
    value_vectors,
    out_weight,
    gate_values,
    hidden_state,
    cached_deltas,
    skip_flags,
):
    rows, features = queries.shape
    width = features // 2
    depth, columns = out_weight.shape
    swap = [(0, 1), (1, 0)]
    bf16 = jnp.bfloat16

    packed = call(
        pack_kernel,
        (queries, key_vectors, value_vectors),
        [((2 * rows, width), bf16)] * 2 + [((rows, width), bf16)] * 2,
        [pltpu.SemaphoreType.DMA((10,))],
        space=pl.ANY,
        vmem=PACK_BYTES,
    )
    moved = []
    for k in range(4):
        k1, k0 = k // 2, k % 2
        pairs = []
        for zz in range(4):
            for cc in range(2):
                to_z = 2 * cc + ((zz % 2) ^ k0)
                pairs.append((zz * 2 + cc, to_z * 2 + ((zz // 2) ^ k1)))
        moved.append(lax.ppermute(packed[k], ("seq", "head"), pairs))
    (joined,) = call(join_kernel, moved, [((4 * rows, width), bf16)])
    sibling = lax.ppermute(joined, "head", swap)
    late_weight, _ = lax.optimization_barrier((out_weight, sibling))
    weight_c = lax.ppermute(late_weight, "head", swap)
    parts = call(
        attention_kernel,
        moved + [sibling],
        [((rows, width), bf16)] * 2,
        [
            pltpu.VMEM((4 * rows, width), bf16),
            pltpu.VMEM((4 * rows, width), bf16),
            pltpu.VMEM((2 * rows, width), bf16),
        ],
        flops=4 * (2 * rows) * (4 * rows) * width,
    )

    flops = 4 * rows * depth * columns
    held = [pltpu.VMEM((4 * rows, width), bf16)]
    gathers = []
    for kept in range(2):
        shards = [parts[1 - kept]]
        for m in range(1, 4):
            pairs = [(z, z ^ m) for z in range(4)]
            shards.append(lax.ppermute(parts[(1 - kept) ^ (m % 2)], "seq", pairs))
        gathers.append(shards)
    count = columns // 2
    sent, kept = (
        call(
            project_kernel,
            shards + [out_weight, weight_c],
            [((rows, count), dtype)] * 2,
            held,
            flops=effort * flops,
        )
        for shards, dtype, effort in ((gathers[0], bf16, 1), (gathers[1], jnp.float32, 8))
    )

    pairs = []
    for zz in range(4):
        for xx in range(2):
            for cc in range(2):
                to = ((2 * cc + (xx ^ (zz % 2))) * 2 + zz // 2) * 2 + zz % 2
                pairs.append(((zz * 2 + xx) * 2 + cc, to))
    owned = []
    for part, total in zip(sent, kept):
        arrived = lax.ppermute(part, "wt", swap)
        (summed,) = call(add_kernel, (total, arrived), [((rows, count), bf16)])
        owned.append(lax.ppermute(summed, ("seq", "wt", "head"), pairs))
    (resting,) = call(
        rest_kernel, (skip_flags, hidden_state, cached_deltas), [((rows, columns), jnp.float32)]
    )
    gate = gate_values[None, :]
    results = ()
    for h, part in enumerate(owned):
        results = pl.pallas_call(
            functools.partial(final_kernel, h * count),
            in_specs=[pl.BlockSpec(memory_space=pltpu.VMEM)] * 3
            + [pl.BlockSpec(memory_space=pl.ANY)] * len(results),
            out_specs=[pl.BlockSpec(memory_space=pl.ANY)] * 2,
            out_shape=[jax.ShapeDtypeStruct((rows, columns), jnp.float32)] * 2,
            scratch_shapes=[pltpu.VMEM((rows, count), jnp.float32)] * 2
            + [pltpu.SemaphoreType.DMA((2,))],
            input_output_aliases={3 + i: i for i in range(len(results))},
            compiler_params=pltpu.CompilerParams(vmem_limit_bytes=VMEM_BYTES),
            cost_estimate=pl.CostEstimate(flops=0, bytes_accessed=0, transcendentals=0),
        )(part, gate, resting, *results)
    return tuple(results)


def solution(mesh):
    placed = (
        P(("groups", "seq"), ("wt", "head")),
        P(("groups", "seq"), ("wt", "head")),
        P(("groups", "seq"), ("wt", "head")),
        P(("wt", "head"), "seq"),
        P(("groups", "wt", "head")),
        P(("groups", "seq"), ("wt", "head")),
        P(None, ("groups", "seq"), ("wt", "head")),
        P("groups"),
    )

    def local(*args):
        sizes = tuple(mesh.shape[name] for name in ("seq", "wt", "head"))
        rows, features = args[0].shape
        if sizes == (4, 2, 2) and rows % 32 == 0 and features % (2 * HEAD_DIM) == 0 and args[3].shape[1] % 256 == 0:
            return local_heads(*args)
        return local_general(*args)

    return jax.shard_map(
        local,
        mesh=mesh,
        in_specs=placed,
        out_specs=(P(("groups", "seq"), ("wt", "head")), P(("groups", "seq"), ("wt", "head"))),
        check_vma=False,
    )
```

```python
import functools

import jax
import jax.numpy as jnp
from jax import lax
from jax.experimental import pallas as pl
from jax.experimental.pallas import tpu as pltpu
from jax.sharding import PartitionSpec as P

HEAD_DIM = 128
VMEM_BYTES = 48 * 1024 * 1024
PACK_BYTES = 53 * 1024 * 1024 + 128 * 1024
LOG2_E = 1.4426950408889634


def attend(state_in, key_rows, value_rows, query_heads, score_scale):
    key_count = key_rows.shape[0]
    head_count = query_heads.shape[1]
    blocks = -(-key_count // 1024)
    while key_count % blocks:
        blocks = blocks + 1
    block_size = key_count // blocks

    def one_block(block_index, state_now):
        row_peak, row_total, weighted = state_now
        start_row = block_index * block_size
        key_block = lax.dynamic_slice_in_dim(key_rows, start_row, block_size, 0)
        value_block = lax.dynamic_slice_in_dim(value_rows, start_row, block_size, 0)
        key_heads = key_block.reshape(block_size, head_count, HEAD_DIM)
        value_heads = value_block.reshape(block_size, head_count, HEAD_DIM)
        scores = (
            jnp.einsum("ihd,jhd->hij", query_heads, key_heads, preferred_element_type=jnp.float32)
            * score_scale
        )
        new_peak = jnp.maximum(row_peak, jnp.max(scores, axis=2))
        exp_scores = jnp.exp(scores - new_peak[:, :, None])
        rescale = jnp.exp(row_peak - new_peak)
        row_total = row_total * rescale + jnp.sum(exp_scores, axis=2)
        weighted = weighted * rescale[:, :, None] + jnp.einsum(
            "hij,jhd->hid",
            exp_scores.astype(jnp.bfloat16),
            value_heads,
            preferred_element_type=jnp.float32,
        )
        return (new_peak, row_total, weighted)

    return lax.fori_loop(0, blocks, one_block, state_in)


def finish(state_out, row_count):
    row_peak, row_total, weighted = state_out
    normed = weighted / row_total[:, :, None]
    return normed.transpose(1, 0, 2).reshape(row_count, -1).astype(jnp.bfloat16)


def local_general(
    queries,
    key_vectors,
    value_vectors,
    out_weight,
    gate_values,
    hidden_state,
    cached_deltas,
    skip_flags,
):
    row_count = queries.shape[0]
    head_count = queries.shape[1] // HEAD_DIM
    score_scale = HEAD_DIM ** (-0.5)
    query_heads = queries.reshape(row_count, head_count, HEAD_DIM)
    start_state = (
        jnp.full((head_count, row_count), -1e30, jnp.float32),
        jnp.zeros((head_count, row_count), jnp.float32),
        jnp.zeros((head_count, row_count, HEAD_DIM), jnp.float32),
    )
    gathered_keys, gathered_values, gathered_weight = (
        lax.all_gather(key_vectors, "seq", axis=0, tiled=True),
        lax.all_gather(value_vectors, "seq", axis=0, tiled=True),
        lax.all_gather(out_weight, "seq", axis=1, tiled=True),
    )
    final_state = attend(start_state, gathered_keys, gathered_values, query_heads, score_scale)
    attention_out = finish(final_state, row_count)
    partial_sums = jnp.dot(attention_out, gathered_weight, preferred_element_type=jnp.float32)
    head_total = lax.psum_scatter(
        partial_sums.astype(jnp.bfloat16), ("wt", "head"), scatter_dimension=1, tiled=True
    ).astype(jnp.float32)
    fresh_delta = head_total * gate_values[None, :]
    kept_deltas = jnp.sum(skip_flags.astype(jnp.float32)[:, None, None] * cached_deltas, axis=0)
    mixed_state = hidden_state + kept_deltas + fresh_delta
    return (mixed_state, fresh_delta)


def bits():
    z = lax.axis_index("seq")
    return lax.div(z, 2), lax.rem(z, 2)


def flip(bit, value):
    return 1 - bit if value else bit


def pack_kernel(queries, keys, values, *refs):
    outs, sems = refs[:4], refs[4]
    rows, width = queries.shape[0], outs[0].shape[1]
    half = rows // 2
    zh, zl = bits()
    copies = []
    for k in range(4):
        part = pl.ds(pl.multiple_of(flip(zh, k // 2) * half, 16), half)
        columns = pl.ds(pl.multiple_of(flip(zl, k % 2) * width, 128), width)
        moves = [
            (keys.at[part, columns], outs[k].at[pl.ds(0, half), :]),
            (values.at[part, columns], outs[k].at[pl.ds(half, half), :]),
        ]
        if k < 2:
            moves.append((queries.at[:, columns], outs[k].at[pl.ds(rows, rows), :]))
        for start, end in moves:
            copies.append(pltpu.make_async_copy(start, end, sems.at[len(copies)]))
    for copy in copies:
        copy.start()
    for copy in copies:
        copy.wait()


def join_kernel(*refs):
    blocks, joined = refs[:4], refs[4]
    rows = joined.shape[0] // 4
    for k, block in enumerate(blocks):
        joined[k * rows : (k + 1) * rows, :] = block[:rows, :]


def attention_kernel(*refs):
    blocks, sibling = refs[:4], refs[4]
    sent, kept, key_all, value_all, query_all = refs[5:]
    rows = sent.shape[0]
    half = rows // 2
    for k in range(4):
        here, there = slice(k * half, (k + 1) * half), slice((4 + k) * half, (5 + k) * half)
        key_all[here, :] = blocks[k][:half, :]
        value_all[here, :] = blocks[k][half:rows, :]
        key_all[there, :] = sibling[k * rows : k * rows + half, :]
        value_all[there, :] = sibling[k * rows + half : (k + 1) * rows, :]
    _, zl = bits()
    x = lax.axis_index("wt")
    for k in range(2):
        for part in range(2):
            at = rows + flip(x, part == 0) * half
            to = (part * 2 + flip(zl, k)) * half
            query_all[pl.ds(pl.multiple_of(to, 16), half), :] = blocks[k][
                pl.ds(pl.multiple_of(at, 16), half), :
            ]
    for h in range(sent.shape[1] // HEAD_DIM):
        columns = slice(h * HEAD_DIM, (h + 1) * HEAD_DIM)
        scores = lax.dot_general(
            query_all[:, columns],
            key_all[:, columns],
            (((1,), (1,)), ((), ())),
            preferred_element_type=jnp.float32,
        )
        peak = jnp.max(scores, axis=1, keepdims=True)
        weights = jnp.exp2((scores - peak) * (LOG2_E * HEAD_DIM ** (-0.5)))
        total = jnp.sum(weights, axis=1, keepdims=True)
        result = jnp.dot(
            weights.astype(jnp.bfloat16), value_all[:, columns], preferred_element_type=jnp.float32
        )
        result = (result / total).astype(sent.dtype)
        sent[:, columns] = result[:rows]
        kept[:, columns] = result[rows:]


def multiply(shards, weight, weight_c, held):
    rows = shards[0].shape[0]
    zh, zl = bits()
    core = lax.axis_index("head")
    for m, shard in enumerate(shards):
        held[m * rows : (m + 1) * rows, :] = shard[...]
    total = None
    for other, block in enumerate((weight, weight_c)):
        high = 2 * lax.rem(flip(core, other) + zh, 2)
        left = jnp.concatenate(
            [
                held[pl.ds(pl.multiple_of((high + flip(zl, low)) * rows, 16), rows), :]
                for low in range(2)
            ],
            axis=1,
        )
        term = jnp.dot(left, block[...], preferred_element_type=jnp.float32)
        total = term if total is None else total + term
    return total


def project_kernel(kept, *refs):
    shards, (weight, weight_c, out0, out1, held) = refs[:4], refs[4:]
    total = multiply(shards, weight, weight_c, held)
    half = out0.shape[0]
    x = lax.axis_index("wt")
    for low in range(2):
        part = total[low * half : (low + 1) * half].astype(out0.dtype)
        first = flip(x, low) == 1 - kept

        @pl.when(first)
        def _():
            out0[...] = part

        @pl.when(jnp.logical_not(first))
        def _():
            out1[...] = part


def add_kernel(kept, arrived, out):
    out[...] = (kept[...] + arrived[...].astype(jnp.float32)).astype(out.dtype)


def rest_kernel(flags, hidden, cached, out):
    total = hidden[...]
    for layer in range(cached.shape[0]):
        total = total + flags[layer].astype(jnp.float32) * cached[layer]
    out[...] = total


def final_kernel(piece, owned, gate, resting, *refs):
    mixed, fresh, mixed_part, fresh_part, sems = refs[-5:]
    half = owned.shape[0]
    _, zl = bits()
    rows = pl.ds(pl.multiple_of(flip(zl, piece) * half, 16), half)
    delta = owned[...].astype(jnp.float32) * gate[...]
    fresh_part[...] = delta
    copy_fresh = pltpu.make_async_copy(fresh_part, fresh.at[rows, :], sems.at[0])
    copy_fresh.start()
    mixed_part[...] = resting[rows, :] + delta
    copy_mixed = pltpu.make_async_copy(mixed_part, mixed.at[rows, :], sems.at[1])
    copy_mixed.start()
    copy_fresh.wait()
    copy_mixed.wait()


def along(shard, m):
    return lax.ppermute(shard, "seq", [(z, z ^ m) for z in range(4)])


def call(
    kernel,
    args,
    outs,
    scratch=(),
    space=pltpu.VMEM,
    out_space=pltpu.VMEM,
    flops=0,
    vmem=VMEM_BYTES,
):
    spaces = [pltpu.SMEM if arg.dtype == jnp.int32 else space for arg in args]
    return pl.pallas_call(
        kernel,
        in_specs=[pl.BlockSpec(memory_space=place) for place in spaces],
        out_specs=[pl.BlockSpec(memory_space=out_space)] * len(outs),
        out_shape=[jax.ShapeDtypeStruct(shape, dtype) for shape, dtype in outs],
        scratch_shapes=list(scratch),
        compiler_params=pltpu.CompilerParams(vmem_limit_bytes=vmem),
        cost_estimate=pl.CostEstimate(flops=flops, bytes_accessed=0, transcendentals=0),
    )(*args)


def local_heads(
    queries,
    key_vectors,
    value_vectors,
    out_weight,
    gate_values,
    hidden_state,
    cached_deltas,
    skip_flags,
):
    rows, features = queries.shape
    width = features // 2
    depth, columns = out_weight.shape
    swap = [(0, 1), (1, 0)]
    bf16 = jnp.bfloat16

    packed = call(
        pack_kernel,
        (queries, key_vectors, value_vectors),
        [((2 * rows, width), bf16)] * 2 + [((rows, width), bf16)] * 2,
        [pltpu.SemaphoreType.DMA((10,))],
        space=pl.ANY,
        vmem=PACK_BYTES,
    )
    late_weight, _ = lax.optimization_barrier((out_weight, packed[0]))
    weight_c = lax.ppermute(late_weight, "head", swap)
    moved = []
    for k in range(4):
        k1, k0 = k // 2, k % 2
        pairs = []
        for zz in range(4):
            for cc in range(2):
                to_z = 2 * cc + ((zz % 2) ^ k0)
                pairs.append((zz * 2 + cc, to_z * 2 + ((zz // 2) ^ k1)))
        moved.append(lax.ppermute(packed[k], ("seq", "head"), pairs))
    (joined,) = call(join_kernel, moved, [((4 * rows, width), bf16)])
    sibling = lax.ppermute(joined, "head", swap)
    sibling, _ = lax.optimization_barrier((sibling, weight_c))
    parts = call(
        attention_kernel,
        moved + [sibling],
        [((rows, width), bf16)] * 2,
        [
            pltpu.VMEM((4 * rows, width), bf16),
            pltpu.VMEM((4 * rows, width), bf16),
            pltpu.VMEM((2 * rows, width), bf16),
        ],
        flops=4 * (2 * rows) * (4 * rows) * width,
    )

    half = rows // 2
    flops = 4 * rows * depth * columns
    sent, kept = (
        call(
            functools.partial(project_kernel, i),
            [part] + [along(part, m) for m in (1, 2, 3)] + [out_weight, weight_c],
            [((half, columns), dtype)] * 2,
            [pltpu.VMEM((4 * rows, width), bf16)],
            flops=effort * flops,
        )
        for i, (part, dtype, effort) in enumerate(((parts[0], bf16, 1), (parts[1], jnp.float32, 8)))
    )

    owned = []
    for p in range(2):
        arrived = lax.ppermute(sent[p], "wt", swap)
        (summed,) = call(add_kernel, (kept[p], arrived), [((half, columns), bf16)])
        pairs = []
        for zz in range(4):
            for xx in range(2):
                for cc in range(2):
                    to = ((2 * cc + (p ^ xx)) * 2 + zz // 2) * 2 + zz % 2
                    pairs.append(((zz * 2 + xx) * 2 + cc, to))
        owned.append(lax.ppermute(summed, ("seq", "wt", "head"), pairs))
    (resting,) = call(
        rest_kernel, (skip_flags, hidden_state, cached_deltas), [((rows, columns), jnp.float32)]
    )
    gate = gate_values[None, :]
    results = ()
    for p, part in enumerate(owned):
        results = pl.pallas_call(
            functools.partial(final_kernel, p),
            in_specs=[pl.BlockSpec(memory_space=pltpu.VMEM)] * 3
            + [pl.BlockSpec(memory_space=pl.ANY)] * len(results),
            out_specs=[pl.BlockSpec(memory_space=pl.ANY)] * 2,
            out_shape=[jax.ShapeDtypeStruct((rows, columns), jnp.float32)] * 2,
            scratch_shapes=[pltpu.VMEM((half, columns), jnp.float32)] * 2
            + [pltpu.SemaphoreType.DMA((2,))],
            input_output_aliases={3 + i: i for i in range(len(results))},
            compiler_params=pltpu.CompilerParams(vmem_limit_bytes=VMEM_BYTES),
            cost_estimate=pl.CostEstimate(flops=0, bytes_accessed=0, transcendentals=0),
        )(part, gate, resting, *results)
    return tuple(results)


def solution(mesh):
    placed = (
        P(("groups", "seq"), ("wt", "head")),
        P(("groups", "seq"), ("wt", "head")),
        P(("groups", "seq"), ("wt", "head")),
        P(("wt", "head"), "seq"),
        P(("groups", "wt", "head")),
        P(("groups", "seq"), ("wt", "head")),
        P(None, ("groups", "seq"), ("wt", "head")),
        P("groups"),
    )

    def local(*args):
        sizes = tuple(mesh.shape[name] for name in ("seq", "wt", "head"))
        rows, features = args[0].shape
        if sizes == (4, 2, 2) and rows % 32 == 0 and features % (2 * HEAD_DIM) == 0:
            return local_heads(*args)
        return local_general(*args)

    return jax.shard_map(
        local,
        mesh=mesh,
        in_specs=placed,
        out_specs=(P(("groups", "seq"), ("wt", "head")), P(("groups", "seq"), ("wt", "head"))),
        check_vma=False,
    )
```

```python
import functools

import jax
import jax.numpy as jnp
from jax import lax
from jax.experimental import pallas as pl
from jax.experimental.pallas import tpu as pltpu
from jax.sharding import PartitionSpec as P

HEAD_DIM = 128
VMEM_BYTES = 48 * 1024 * 1024
PACK_BYTES = 53 * 1024 * 1024 + 128 * 1024
LOG2_E = 1.4426950408889634


def attend(state_in, key_rows, value_rows, query_heads, score_scale):
    key_count = key_rows.shape[0]
    head_count = query_heads.shape[1]
    blocks = -(-key_count // 1024)
    while key_count % blocks:
        blocks = blocks + 1
    block_size = key_count // blocks

    def one_block(block_index, state_now):
        row_peak, row_total, weighted = state_now
        start_row = block_index * block_size
        key_block = lax.dynamic_slice_in_dim(key_rows, start_row, block_size, 0)
        value_block = lax.dynamic_slice_in_dim(value_rows, start_row, block_size, 0)
        key_heads = key_block.reshape(block_size, head_count, HEAD_DIM)
        value_heads = value_block.reshape(block_size, head_count, HEAD_DIM)
        scores = (
            jnp.einsum("ihd,jhd->hij", query_heads, key_heads, preferred_element_type=jnp.float32)
            * score_scale
        )
        new_peak = jnp.maximum(row_peak, jnp.max(scores, axis=2))
        exp_scores = jnp.exp(scores - new_peak[:, :, None])
        rescale = jnp.exp(row_peak - new_peak)
        row_total = row_total * rescale + jnp.sum(exp_scores, axis=2)
        weighted = weighted * rescale[:, :, None] + jnp.einsum(
            "hij,jhd->hid",
            exp_scores.astype(jnp.bfloat16),
            value_heads,
            preferred_element_type=jnp.float32,
        )
        return (new_peak, row_total, weighted)

    return lax.fori_loop(0, blocks, one_block, state_in)


def finish(state_out, row_count):
    row_peak, row_total, weighted = state_out
    normed = weighted / row_total[:, :, None]
    return normed.transpose(1, 0, 2).reshape(row_count, -1).astype(jnp.bfloat16)


def local_general(
    queries,
    key_vectors,
    value_vectors,
    out_weight,
    gate_values,
    hidden_state,
    cached_deltas,
    skip_flags,
):
    row_count = queries.shape[0]
    head_count = queries.shape[1] // HEAD_DIM
    score_scale = HEAD_DIM ** (-0.5)
    query_heads = queries.reshape(row_count, head_count, HEAD_DIM)
    start_state = (
        jnp.full((head_count, row_count), -1e30, jnp.float32),
        jnp.zeros((head_count, row_count), jnp.float32),
        jnp.zeros((head_count, row_count, HEAD_DIM), jnp.float32),
    )
    gathered_keys, gathered_values, gathered_weight = (
        lax.all_gather(key_vectors, "seq", axis=0, tiled=True),
        lax.all_gather(value_vectors, "seq", axis=0, tiled=True),
        lax.all_gather(out_weight, "seq", axis=1, tiled=True),
    )
    final_state = attend(start_state, gathered_keys, gathered_values, query_heads, score_scale)
    attention_out = finish(final_state, row_count)
    partial_sums = jnp.dot(attention_out, gathered_weight, preferred_element_type=jnp.float32)
    head_total = lax.psum_scatter(
        partial_sums.astype(jnp.bfloat16), ("wt", "head"), scatter_dimension=1, tiled=True
    ).astype(jnp.float32)
    fresh_delta = head_total * gate_values[None, :]
    kept_deltas = jnp.sum(skip_flags.astype(jnp.float32)[:, None, None] * cached_deltas, axis=0)
    mixed_state = hidden_state + kept_deltas + fresh_delta
    return (mixed_state, fresh_delta)


def bits():
    z = lax.axis_index("seq")
    return lax.div(z, 2), lax.rem(z, 2)


def flip(bit, value):
    return 1 - bit if value else bit


def pack_kernel(queries, keys, values, *refs):
    outs, sems = refs[:4], refs[4]
    rows, width = queries.shape[0], outs[0].shape[1]
    half = rows // 2
    zh, zl = bits()
    copies = []
    for k in range(4):
        part = pl.ds(pl.multiple_of(flip(zh, k // 2) * half, 16), half)
        columns = pl.ds(pl.multiple_of(flip(zl, k % 2) * width, 128), width)
        moves = [
            (keys.at[part, columns], outs[k].at[pl.ds(0, half), :]),
            (values.at[part, columns], outs[k].at[pl.ds(half, half), :]),
        ]
        if k < 2:
            moves.append((queries.at[:, columns], outs[k].at[pl.ds(rows, rows), :]))
        for start, end in moves:
            copies.append(pltpu.make_async_copy(start, end, sems.at[len(copies)]))
    for copy in copies:
        copy.start()
    for copy in copies:
        copy.wait()


def join_kernel(*refs):
    blocks, joined = refs[:4], refs[4]
    rows = joined.shape[0] // 4
    for k, block in enumerate(blocks):
        joined[k * rows : (k + 1) * rows, :] = block[:rows, :]


def attention_kernel(*refs):
    blocks, sibling = refs[:4], refs[4]
    sent, kept, both, key_all, value_all, query_all = refs[5:]
    rows = sent.shape[0]
    half = rows // 2
    for k in range(4):
        here, there = slice(k * half, (k + 1) * half), slice((4 + k) * half, (5 + k) * half)
        key_all[here, :] = blocks[k][:half, :]
        value_all[here, :] = blocks[k][half:rows, :]
        key_all[there, :] = sibling[k * rows : k * rows + half, :]
        value_all[there, :] = sibling[k * rows + half : (k + 1) * rows, :]
    _, zl = bits()
    x = lax.axis_index("wt")
    for k in range(2):
        for part in range(2):
            at = rows + flip(x, part == 0) * half
            to = (part * 2 + flip(zl, k)) * half
            query_all[pl.ds(pl.multiple_of(to, 16), half), :] = blocks[k][
                pl.ds(pl.multiple_of(at, 16), half), :
            ]
    for h in range(sent.shape[1] // HEAD_DIM):
        columns = slice(h * HEAD_DIM, (h + 1) * HEAD_DIM)
        scores = lax.dot_general(
            query_all[:, columns],
            key_all[:, columns],
            (((1,), (1,)), ((), ())),
            preferred_element_type=jnp.float32,
        )
        peak = jnp.max(scores, axis=1, keepdims=True)
        weights = jnp.exp2((scores - peak) * (LOG2_E * HEAD_DIM ** (-0.5)))
        total = jnp.sum(weights, axis=1, keepdims=True)
        result = jnp.dot(
            weights.astype(jnp.bfloat16), value_all[:, columns], preferred_element_type=jnp.float32
        )
        result = (result / total).astype(sent.dtype)
        sent[:, columns] = result[:rows]
        kept[:, columns] = result[rows:]
        both[:, columns] = result


def multiply(shards, first, weight, weight_c, held):
    rows = shards[0].shape[0]
    zh, zl = bits()
    core = lax.axis_index("head")
    for m, shard in enumerate(shards):
        start = first if m == 1 else 0
        held[m * rows : (m + 1) * rows, :] = shard[start : start + rows, :]
    total = None
    for other, block in enumerate((weight, weight_c)):
        high = 2 * lax.rem(flip(core, other) + zh, 2)
        left = jnp.concatenate(
            [
                held[pl.ds(pl.multiple_of((high + flip(zl, low)) * rows, 16), rows), :]
                for low in range(2)
            ],
            axis=1,
        )
        term = jnp.dot(left, block[...], preferred_element_type=jnp.float32)
        total = term if total is None else total + term
    return total


def project_kernel(kept, *refs):
    shards, (weight, weight_c, out0, out1, held) = refs[:4], refs[4:]
    total = multiply(shards, kept * shards[0].shape[0], weight, weight_c, held)
    half = out0.shape[0]
    x = lax.axis_index("wt")
    for low in range(2):
        part = total[low * half : (low + 1) * half].astype(out0.dtype)
        first = flip(x, low) == 1 - kept

        @pl.when(first)
        def _():
            out0[...] = part

        @pl.when(jnp.logical_not(first))
        def _():
            out1[...] = part


def add_kernel(kept, arrived, out):
    out[...] = (kept[...] + arrived[...].astype(jnp.float32)).astype(out.dtype)


def rest_kernel(flags, hidden, cached, out):
    total = hidden[...]
    for layer in range(cached.shape[0]):
        total = total + flags[layer].astype(jnp.float32) * cached[layer]
    out[...] = total


def final_kernel(piece, owned, gate, resting, *refs):
    mixed, fresh, mixed_part, fresh_part, sems = refs[-5:]
    half = owned.shape[0]
    _, zl = bits()
    rows = pl.ds(pl.multiple_of(flip(zl, piece) * half, 16), half)
    delta = owned[...].astype(jnp.float32) * gate[...]
    fresh_part[...] = delta
    copy_fresh = pltpu.make_async_copy(fresh_part, fresh.at[rows, :], sems.at[0])
    copy_fresh.start()
    mixed_part[...] = resting[rows, :] + delta
    copy_mixed = pltpu.make_async_copy(mixed_part, mixed.at[rows, :], sems.at[1])
    copy_mixed.start()
    copy_fresh.wait()
    copy_mixed.wait()


def along(shard, m):
    return lax.ppermute(shard, "seq", [(z, z ^ m) for z in range(4)])


def call(
    kernel,
    args,
    outs,
    scratch=(),
    space=pltpu.VMEM,
    out_space=pltpu.VMEM,
    flops=0,
    vmem=VMEM_BYTES,
):
    spaces = [pltpu.SMEM if arg.dtype == jnp.int32 else space for arg in args]
    return pl.pallas_call(
        kernel,
        in_specs=[pl.BlockSpec(memory_space=place) for place in spaces],
        out_specs=[pl.BlockSpec(memory_space=out_space)] * len(outs),
        out_shape=[jax.ShapeDtypeStruct(shape, dtype) for shape, dtype in outs],
        scratch_shapes=list(scratch),
        compiler_params=pltpu.CompilerParams(vmem_limit_bytes=vmem),
        cost_estimate=pl.CostEstimate(flops=flops, bytes_accessed=0, transcendentals=0),
    )(*args)


def local_heads(
    queries,
    key_vectors,
    value_vectors,
    out_weight,
    gate_values,
    hidden_state,
    cached_deltas,
    skip_flags,
):
    rows, features = queries.shape
    width = features // 2
    depth, columns = out_weight.shape
    swap = [(0, 1), (1, 0)]
    bf16 = jnp.bfloat16

    packed = call(
        pack_kernel,
        (queries, key_vectors, value_vectors),
        [((2 * rows, width), bf16)] * 2 + [((rows, width), bf16)] * 2,
        [pltpu.SemaphoreType.DMA((10,))],
        space=pl.ANY,
        vmem=PACK_BYTES,
    )
    late_weight, _ = lax.optimization_barrier((out_weight, packed[0]))
    weight_c = lax.ppermute(late_weight, "head", swap)
    moved = []
    for k in range(4):
        k1, k0 = k // 2, k % 2
        pairs = []
        for zz in range(4):
            for cc in range(2):
                to_z = 2 * cc + ((zz % 2) ^ k0)
                pairs.append((zz * 2 + cc, to_z * 2 + ((zz // 2) ^ k1)))
        moved.append(lax.ppermute(packed[k], ("seq", "head"), pairs))
    (joined,) = call(join_kernel, moved, [((4 * rows, width), bf16)])
    sibling = lax.ppermute(joined, "head", swap)
    sibling, _ = lax.optimization_barrier((sibling, weight_c))
    parts = call(
        attention_kernel,
        moved + [sibling],
        [((rows, width), bf16)] * 2 + [((2 * rows, width), bf16)],
        [
            pltpu.VMEM((4 * rows, width), bf16),
            pltpu.VMEM((4 * rows, width), bf16),
            pltpu.VMEM((2 * rows, width), bf16),
        ],
        flops=4 * (2 * rows) * (4 * rows) * width,
    )

    half = rows // 2
    flops = 4 * rows * depth * columns
    near = along(parts[2], 1)
    sent, kept = (
        call(
            functools.partial(project_kernel, i),
            [part, near, along(part, 2), along(part, 3), out_weight, weight_c],
            [((half, columns), dtype)] * 2,
            [pltpu.VMEM((4 * rows, width), bf16)],
            flops=effort * flops,
        )
        for i, (part, dtype, effort) in enumerate(((parts[0], bf16, 1), (parts[1], jnp.float32, 8)))
    )

    owned = []
    for p in range(2):
        arrived = lax.ppermute(sent[p], "wt", swap)
        (summed,) = call(add_kernel, (kept[p], arrived), [((half, columns), bf16)])
        pairs = []
        for zz in range(4):
            for xx in range(2):
                for cc in range(2):
                    to = ((2 * cc + (p ^ xx)) * 2 + zz // 2) * 2 + zz % 2
                    pairs.append(((zz * 2 + xx) * 2 + cc, to))
        owned.append(lax.ppermute(summed, ("seq", "wt", "head"), pairs))
    (resting,) = call(
        rest_kernel, (skip_flags, hidden_state, cached_deltas), [((rows, columns), jnp.float32)]
    )
    gate = gate_values[None, :]
    results = ()
    for p, part in enumerate(owned):
        results = pl.pallas_call(
            functools.partial(final_kernel, p),
            in_specs=[pl.BlockSpec(memory_space=pltpu.VMEM)] * 3
            + [pl.BlockSpec(memory_space=pl.ANY)] * len(results),
            out_specs=[pl.BlockSpec(memory_space=pl.ANY)] * 2,
            out_shape=[jax.ShapeDtypeStruct((rows, columns), jnp.float32)] * 2,
            scratch_shapes=[pltpu.VMEM((half, columns), jnp.float32)] * 2
            + [pltpu.SemaphoreType.DMA((2,))],
            input_output_aliases={3 + i: i for i in range(len(results))},
            compiler_params=pltpu.CompilerParams(vmem_limit_bytes=VMEM_BYTES),
            cost_estimate=pl.CostEstimate(flops=0, bytes_accessed=0, transcendentals=0),
        )(part, gate, resting, *results)
    return tuple(results)


def solution(mesh):
    placed = (
        P(("groups", "seq"), ("wt", "head")),
        P(("groups", "seq"), ("wt", "head")),
        P(("groups", "seq"), ("wt", "head")),
        P(("wt", "head"), "seq"),
        P(("groups", "wt", "head")),
        P(("groups", "seq"), ("wt", "head")),
        P(None, ("groups", "seq"), ("wt", "head")),
        P("groups"),
    )

    def local(*args):
        sizes = tuple(mesh.shape[name] for name in ("seq", "wt", "head"))
        rows, features = args[0].shape
        if sizes == (4, 2, 2) and rows % 32 == 0 and features % (2 * HEAD_DIM) == 0:
            return local_heads(*args)
        return local_general(*args)

    return jax.shard_map(
        local,
        mesh=mesh,
        in_specs=placed,
        out_specs=(P(("groups", "seq"), ("wt", "head")), P(("groups", "seq"), ("wt", "head"))),
        check_vma=False,
    )
```

```python
import functools

import jax
import jax.numpy as jnp
from jax import lax
from jax.experimental import pallas as pl
from jax.experimental.pallas import tpu as pltpu
from jax.sharding import PartitionSpec as P

HEAD_DIM = 128
VMEM_BYTES = 48 * 1024 * 1024
PACK_BYTES = 53 * 1024 * 1024 + 128 * 1024
LOG2_E = 1.4426950408889634


def attend(state_in, key_rows, value_rows, query_heads, score_scale):
    key_count = key_rows.shape[0]
    head_count = query_heads.shape[1]
    blocks = -(-key_count // 1024)
    while key_count % blocks:
        blocks = blocks + 1
    block_size = key_count // blocks

    def one_block(block_index, state_now):
        row_peak, row_total, weighted = state_now
        start_row = block_index * block_size
        key_block = lax.dynamic_slice_in_dim(key_rows, start_row, block_size, 0)
        value_block = lax.dynamic_slice_in_dim(value_rows, start_row, block_size, 0)
        key_heads = key_block.reshape(block_size, head_count, HEAD_DIM)
        value_heads = value_block.reshape(block_size, head_count, HEAD_DIM)
        scores = (
            jnp.einsum("ihd,jhd->hij", query_heads, key_heads, preferred_element_type=jnp.float32)
            * score_scale
        )
        new_peak = jnp.maximum(row_peak, jnp.max(scores, axis=2))
        exp_scores = jnp.exp(scores - new_peak[:, :, None])
        rescale = jnp.exp(row_peak - new_peak)
        row_total = row_total * rescale + jnp.sum(exp_scores, axis=2)
        weighted = weighted * rescale[:, :, None] + jnp.einsum(
            "hij,jhd->hid",
            exp_scores.astype(jnp.bfloat16),
            value_heads,
            preferred_element_type=jnp.float32,
        )
        return (new_peak, row_total, weighted)

    return lax.fori_loop(0, blocks, one_block, state_in)


def finish(state_out, row_count):
    row_peak, row_total, weighted = state_out
    normed = weighted / row_total[:, :, None]
    return normed.transpose(1, 0, 2).reshape(row_count, -1).astype(jnp.bfloat16)


def local_general(
    queries,
    key_vectors,
    value_vectors,
    out_weight,
    gate_values,
    hidden_state,
    cached_deltas,
    skip_flags,
):
    row_count = queries.shape[0]
    head_count = queries.shape[1] // HEAD_DIM
    score_scale = HEAD_DIM ** (-0.5)
    query_heads = queries.reshape(row_count, head_count, HEAD_DIM)
    start_state = (
        jnp.full((head_count, row_count), -1e30, jnp.float32),
        jnp.zeros((head_count, row_count), jnp.float32),
        jnp.zeros((head_count, row_count, HEAD_DIM), jnp.float32),
    )
    gathered_keys, gathered_values, gathered_weight = (
        lax.all_gather(key_vectors, "seq", axis=0, tiled=True),
        lax.all_gather(value_vectors, "seq", axis=0, tiled=True),
        lax.all_gather(out_weight, "seq", axis=1, tiled=True),
    )
    final_state = attend(start_state, gathered_keys, gathered_values, query_heads, score_scale)
    attention_out = finish(final_state, row_count)
    partial_sums = jnp.dot(attention_out, gathered_weight, preferred_element_type=jnp.float32)
    head_total = lax.psum_scatter(
        partial_sums.astype(jnp.bfloat16), ("wt", "head"), scatter_dimension=1, tiled=True
    ).astype(jnp.float32)
    fresh_delta = head_total * gate_values[None, :]
    kept_deltas = jnp.sum(skip_flags.astype(jnp.float32)[:, None, None] * cached_deltas, axis=0)
    mixed_state = hidden_state + kept_deltas + fresh_delta
    return (mixed_state, fresh_delta)


def bits():
    z = lax.axis_index("seq")
    return lax.div(z, 2), lax.rem(z, 2)


def flip(bit, value):
    return 1 - bit if value else bit


def pack_kernel(queries, keys, values, *refs):
    outs, sems = refs[:4], refs[4]
    rows, width = queries.shape[0], outs[0].shape[1]
    half = rows // 2
    zh, zl = bits()
    copies = []
    for k in range(4):
        part = pl.ds(pl.multiple_of(flip(zl, k // 2) * half, 16), half)
        columns = pl.ds(pl.multiple_of(flip(zh, k % 2) * width, 128), width)
        moves = [
            (keys.at[part, columns], outs[k].at[pl.ds(0, half), :]),
            (values.at[part, columns], outs[k].at[pl.ds(half, half), :]),
        ]
        if k < 2:
            moves.append((queries.at[:, columns], outs[k].at[pl.ds(rows, rows), :]))
        for start, end in moves:
            copies.append(pltpu.make_async_copy(start, end, sems.at[len(copies)]))
    for copy in copies:
        copy.start()
    for copy in copies:
        copy.wait()


def join_kernel(*refs):
    blocks, joined = refs[:4], refs[4]
    rows = joined.shape[0] // 4
    for k, block in enumerate(blocks):
        joined[k * rows : (k + 1) * rows, :] = block[:rows, :]


def attention_kernel(*refs):
    blocks, sibling = refs[:4], refs[4]
    sent, kept, key_all, value_all, query_all = refs[5:]
    rows = sent.shape[0]
    half = rows // 2
    for k in range(4):
        here, there = slice(k * half, (k + 1) * half), slice((4 + k) * half, (5 + k) * half)
        key_all[here, :] = blocks[k][:half, :]
        value_all[here, :] = blocks[k][half:rows, :]
        key_all[there, :] = sibling[k * rows : k * rows + half, :]
        value_all[there, :] = sibling[k * rows + half : (k + 1) * rows, :]
    zh, _ = bits()
    x = lax.axis_index("wt")
    for k in range(2):
        for part in range(2):
            at = rows + flip(x, part == 0) * half
            to = (part * 2 + flip(zh, k)) * half
            query_all[pl.ds(pl.multiple_of(to, 16), half), :] = blocks[k][
                pl.ds(pl.multiple_of(at, 16), half), :
            ]
    for h in range(sent.shape[1] // HEAD_DIM):
        columns = slice(h * HEAD_DIM, (h + 1) * HEAD_DIM)
        scores = lax.dot_general(
            query_all[:, columns],
            key_all[:, columns],
            (((1,), (1,)), ((), ())),
            preferred_element_type=jnp.float32,
        )
        peak = jnp.max(scores, axis=1, keepdims=True)
        weights = jnp.exp2((scores - peak) * (LOG2_E * HEAD_DIM ** (-0.5)))
        total = jnp.sum(weights, axis=1, keepdims=True)
        result = jnp.dot(
            weights.astype(jnp.bfloat16), value_all[:, columns], preferred_element_type=jnp.float32
        )
        result = (result / total).astype(sent.dtype)
        sent[:, columns] = result[:rows]
        kept[:, columns] = result[rows:]


def multiply(shards, weight, weight_c, held):
    rows = shards[0].shape[0]
    zh, zl = bits()
    core = lax.axis_index("head")
    for m, shard in enumerate(shards):
        held[m * rows : (m + 1) * rows, :] = shard[...]
    total = None
    for other, block in enumerate((weight, weight_c)):
        low = lax.rem(flip(core, other) + zl, 2)
        left = jnp.concatenate(
            [
                held[pl.ds(pl.multiple_of((2 * flip(zh, high) + low) * rows, 16), rows), :]
                for high in range(2)
            ],
            axis=1,
        )
        term = jnp.dot(left, block[...], preferred_element_type=jnp.float32)
        total = term if total is None else total + term
    return total


def project_kernel(kept, *refs):
    shards, (weight, weight_c, out0, out1, held) = refs[:4], refs[4:]
    total = multiply(shards, weight, weight_c, held)
    half = out0.shape[0]
    x = lax.axis_index("wt")
    for low in range(2):
        part = total[low * half : (low + 1) * half].astype(out0.dtype)
        first = flip(x, low) == 1 - kept

        @pl.when(first)
        def _():
            out0[...] = part

        @pl.when(jnp.logical_not(first))
        def _():
            out1[...] = part


def add_kernel(kept, arrived, out):
    out[...] = (kept[...] + arrived[...].astype(jnp.float32)).astype(out.dtype)


def rest_kernel(flags, hidden, cached, out):
    total = hidden[...]
    for layer in range(cached.shape[0]):
        total = total + flags[layer].astype(jnp.float32) * cached[layer]
    out[...] = total


def final_kernel(piece, owned, gate, resting, *refs):
    mixed, fresh, mixed_part, fresh_part, sems = refs[-5:]
    half = owned.shape[0]
    zh, _ = bits()
    rows = pl.ds(pl.multiple_of(flip(zh, piece) * half, 16), half)
    delta = owned[...].astype(jnp.float32) * gate[...]
    fresh_part[...] = delta
    copy_fresh = pltpu.make_async_copy(fresh_part, fresh.at[rows, :], sems.at[0])
    copy_fresh.start()
    mixed_part[...] = resting[rows, :] + delta
    copy_mixed = pltpu.make_async_copy(mixed_part, mixed.at[rows, :], sems.at[1])
    copy_mixed.start()
    copy_fresh.wait()
    copy_mixed.wait()


def along(shard, m):
    return lax.ppermute(shard, "seq", [(z, z ^ m) for z in range(4)])


def call(
    kernel,
    args,
    outs,
    scratch=(),
    space=pltpu.VMEM,
    out_space=pltpu.VMEM,
    flops=0,
    vmem=VMEM_BYTES,
):
    spaces = [pltpu.SMEM if arg.dtype == jnp.int32 else space for arg in args]
    return pl.pallas_call(
        kernel,
        in_specs=[pl.BlockSpec(memory_space=place) for place in spaces],
        out_specs=[pl.BlockSpec(memory_space=out_space)] * len(outs),
        out_shape=[jax.ShapeDtypeStruct(shape, dtype) for shape, dtype in outs],
        scratch_shapes=list(scratch),
        compiler_params=pltpu.CompilerParams(vmem_limit_bytes=vmem),
        cost_estimate=pl.CostEstimate(flops=flops, bytes_accessed=0, transcendentals=0),
    )(*args)


def local_heads(
    queries,
    key_vectors,
    value_vectors,
    out_weight,
    gate_values,
    hidden_state,
    cached_deltas,
    skip_flags,
):
    rows, features = queries.shape
    width = features // 2
    depth, columns = out_weight.shape
    swap = [(0, 1), (1, 0)]
    bf16 = jnp.bfloat16

    packed = call(
        pack_kernel,
        (queries, key_vectors, value_vectors),
        [((2 * rows, width), bf16)] * 2 + [((rows, width), bf16)] * 2,
        [pltpu.SemaphoreType.DMA((10,))],
        space=pl.ANY,
        vmem=PACK_BYTES,
    )
    late_weight, _ = lax.optimization_barrier((out_weight, packed[0]))
    weight_c = lax.ppermute(late_weight, "head", swap)
    moved = []
    for k in range(4):
        k1, k0 = k // 2, k % 2
        pairs = []
        for zz in range(4):
            for cc in range(2):
                to_z = 2 * ((zz // 2) ^ k0) + cc
                pairs.append((zz * 2 + cc, to_z * 2 + ((zz % 2) ^ k1)))
        moved.append(lax.ppermute(packed[k], ("seq", "head"), pairs))
    (joined,) = call(join_kernel, moved, [((4 * rows, width), bf16)])
    sibling = lax.ppermute(joined, "head", swap)
    sibling, _ = lax.optimization_barrier((sibling, weight_c))
    parts = call(
        attention_kernel,
        moved + [sibling],
        [((rows, width), bf16)] * 2,
        [
            pltpu.VMEM((4 * rows, width), bf16),
            pltpu.VMEM((4 * rows, width), bf16),
            pltpu.VMEM((2 * rows, width), bf16),
        ],
        flops=4 * (2 * rows) * (4 * rows) * width,
    )

    half = rows // 2
    flops = 4 * rows * depth * columns
    sent, kept = (
        call(
            functools.partial(project_kernel, i),
            [part] + [along(part, m) for m in (1, 2, 3)] + [out_weight, weight_c],
            [((half, columns), dtype)] * 2,
            [pltpu.VMEM((4 * rows, width), bf16)],
            flops=effort * flops,
        )
        for i, (part, dtype, effort) in enumerate(((parts[0], bf16, 1), (parts[1], jnp.float32, 8)))
    )

    owned = []
    for p in range(2):
        arrived = lax.ppermute(sent[p], "wt", swap)
        (summed,) = call(add_kernel, (kept[p], arrived), [((half, columns), bf16)])
        pairs = []
        for zz in range(4):
            for xx in range(2):
                for cc in range(2):
                    to = ((cc + 2 * (p ^ xx)) * 2 + zz // 2) * 2 + zz % 2
                    pairs.append(((zz * 2 + xx) * 2 + cc, to))
        owned.append(lax.ppermute(summed, ("seq", "wt", "head"), pairs))
    (resting,) = call(
        rest_kernel, (skip_flags, hidden_state, cached_deltas), [((rows, columns), jnp.float32)]
    )
    gate = gate_values[None, :]
    results = ()
    for p, part in enumerate(owned):
        results = pl.pallas_call(
            functools.partial(final_kernel, p),
            in_specs=[pl.BlockSpec(memory_space=pltpu.VMEM)] * 3
            + [pl.BlockSpec(memory_space=pl.ANY)] * len(results),
            out_specs=[pl.BlockSpec(memory_space=pl.ANY)] * 2,
            out_shape=[jax.ShapeDtypeStruct((rows, columns), jnp.float32)] * 2,
            scratch_shapes=[pltpu.VMEM((half, columns), jnp.float32)] * 2
            + [pltpu.SemaphoreType.DMA((2,))],
            input_output_aliases={3 + i: i for i in range(len(results))},
            compiler_params=pltpu.CompilerParams(vmem_limit_bytes=VMEM_BYTES),
            cost_estimate=pl.CostEstimate(flops=0, bytes_accessed=0, transcendentals=0),
        )(part, gate, resting, *results)
    return tuple(results)


def solution(mesh):
    placed = (
        P(("groups", "seq"), ("wt", "head")),
        P(("groups", "seq"), ("wt", "head")),
        P(("groups", "seq"), ("wt", "head")),
        P(("wt", "head"), "seq"),
        P(("groups", "wt", "head")),
        P(("groups", "seq"), ("wt", "head")),
        P(None, ("groups", "seq"), ("wt", "head")),
        P("groups"),
    )

    def local(*args):
        sizes = tuple(mesh.shape[name] for name in ("seq", "wt", "head"))
        rows, features = args[0].shape
        if sizes == (4, 2, 2) and rows % 32 == 0 and features % (2 * HEAD_DIM) == 0:
            return local_heads(*args)
        return local_general(*args)

    return jax.shard_map(
        local,
        mesh=mesh,
        in_specs=placed,
        out_specs=(P(("groups", "seq"), ("wt", "head")), P(("groups", "seq"), ("wt", "head"))),
        check_vma=False,
    )
```

```python
import functools

import jax
import jax.numpy as jnp
from jax import lax
from jax.experimental import pallas as pl
from jax.experimental.pallas import tpu as pltpu
from jax.sharding import PartitionSpec as P

HEAD_DIM = 128
VMEM_BYTES = 48 * 1024 * 1024
PACK_BYTES = 53 * 1024 * 1024 + 128 * 1024
LOG2_E = 1.4426950408889634


def attend(state_in, key_rows, value_rows, query_heads, score_scale):
    key_count = key_rows.shape[0]
    head_count = query_heads.shape[1]
    blocks = -(-key_count // 1024)
    while key_count % blocks:
        blocks = blocks + 1
    block_size = key_count // blocks

    def one_block(block_index, state_now):
        row_peak, row_total, weighted = state_now
        start_row = block_index * block_size
        key_block = lax.dynamic_slice_in_dim(key_rows, start_row, block_size, 0)
        value_block = lax.dynamic_slice_in_dim(value_rows, start_row, block_size, 0)
        key_heads = key_block.reshape(block_size, head_count, HEAD_DIM)
        value_heads = value_block.reshape(block_size, head_count, HEAD_DIM)
        scores = (
            jnp.einsum("ihd,jhd->hij", query_heads, key_heads, preferred_element_type=jnp.float32)
            * score_scale
        )
        new_peak = jnp.maximum(row_peak, jnp.max(scores, axis=2))
        exp_scores = jnp.exp(scores - new_peak[:, :, None])
        rescale = jnp.exp(row_peak - new_peak)
        row_total = row_total * rescale + jnp.sum(exp_scores, axis=2)
        weighted = weighted * rescale[:, :, None] + jnp.einsum(
            "hij,jhd->hid",
            exp_scores.astype(jnp.bfloat16),
            value_heads,
            preferred_element_type=jnp.float32,
        )
        return (new_peak, row_total, weighted)

    return lax.fori_loop(0, blocks, one_block, state_in)


def finish(state_out, row_count):
    row_peak, row_total, weighted = state_out
    normed = weighted / row_total[:, :, None]
    return normed.transpose(1, 0, 2).reshape(row_count, -1).astype(jnp.bfloat16)


def local_general(
    queries,
    key_vectors,
    value_vectors,
    out_weight,
    gate_values,
    hidden_state,
    cached_deltas,
    skip_flags,
):
    row_count = queries.shape[0]
    head_count = queries.shape[1] // HEAD_DIM
    score_scale = HEAD_DIM ** (-0.5)
    query_heads = queries.reshape(row_count, head_count, HEAD_DIM)
    start_state = (
        jnp.full((head_count, row_count), -1e30, jnp.float32),
        jnp.zeros((head_count, row_count), jnp.float32),
        jnp.zeros((head_count, row_count, HEAD_DIM), jnp.float32),
    )
    gathered_keys, gathered_values, gathered_weight = (
        lax.all_gather(key_vectors, "seq", axis=0, tiled=True),
        lax.all_gather(value_vectors, "seq", axis=0, tiled=True),
        lax.all_gather(out_weight, "seq", axis=1, tiled=True),
    )
    final_state = attend(start_state, gathered_keys, gathered_values, query_heads, score_scale)
    attention_out = finish(final_state, row_count)
    partial_sums = jnp.dot(attention_out, gathered_weight, preferred_element_type=jnp.float32)
    head_total = lax.psum_scatter(
        partial_sums.astype(jnp.bfloat16), ("wt", "head"), scatter_dimension=1, tiled=True
    ).astype(jnp.float32)
    fresh_delta = head_total * gate_values[None, :]
    kept_deltas = jnp.sum(skip_flags.astype(jnp.float32)[:, None, None] * cached_deltas, axis=0)
    mixed_state = hidden_state + kept_deltas + fresh_delta
    return (mixed_state, fresh_delta)


def bits():
    z = lax.axis_index("seq")
    return lax.div(z, 2), lax.rem(z, 2)


def flip(bit, value):
    return 1 - bit if value else bit


def pack_kernel(queries, keys, values, *refs):
    outs, sems = refs[:4], refs[4]
    rows, width = queries.shape[0], outs[0].shape[1]
    half = rows // 2
    zh, zl = bits()
    copies = []
    for k in range(4):
        part = pl.ds(pl.multiple_of(flip(zl, k // 2) * half, 16), half)
        columns = pl.ds(pl.multiple_of(flip(zh, k % 2) * width, 128), width)
        moves = [
            (keys.at[part, columns], outs[k].at[pl.ds(0, half), :]),
            (values.at[part, columns], outs[k].at[pl.ds(half, half), :]),
        ]
        if k < 2:
            moves.append((queries.at[:, columns], outs[k].at[pl.ds(rows, rows), :]))
        for start, end in moves:
            copies.append(pltpu.make_async_copy(start, end, sems.at[len(copies)]))
    for copy in copies:
        copy.start()
    for copy in copies:
        copy.wait()


def join_kernel(*refs):
    blocks, joined = refs[:4], refs[4]
    rows = joined.shape[0] // 4
    for k, block in enumerate(blocks):
        joined[k * rows : (k + 1) * rows, :] = block[:rows, :]


def attention_kernel(*refs):
    blocks, sibling = refs[:4], refs[4]
    sent, kept, key_all, value_all, query_all = refs[5:]
    rows = sent.shape[0]
    half = rows // 2
    for k in range(4):
        here, there = slice(k * half, (k + 1) * half), slice((4 + k) * half, (5 + k) * half)
        key_all[here, :] = blocks[k][:half, :]
        value_all[here, :] = blocks[k][half:rows, :]
        key_all[there, :] = sibling[k * rows : k * rows + half, :]
        value_all[there, :] = sibling[k * rows + half : (k + 1) * rows, :]
    zh, _ = bits()
    x = lax.axis_index("wt")
    for k in range(2):
        for part in range(2):
            at = rows + flip(x, part == 0) * half
            to = (part * 2 + flip(zh, k)) * half
            query_all[pl.ds(pl.multiple_of(to, 16), half), :] = blocks[k][
                pl.ds(pl.multiple_of(at, 16), half), :
            ]
    for h in range(sent.shape[1] // HEAD_DIM):
        columns = slice(h * HEAD_DIM, (h + 1) * HEAD_DIM)
        scores = lax.dot_general(
            query_all[:, columns],
            key_all[:, columns],
            (((1,), (1,)), ((), ())),
            preferred_element_type=jnp.float32,
        )
        peak = jnp.max(scores, axis=1, keepdims=True)
        weights = jnp.exp2((scores - peak) * (LOG2_E * HEAD_DIM ** (-0.5)))
        total = jnp.sum(weights, axis=1, keepdims=True)
        result = jnp.dot(
            weights.astype(jnp.bfloat16), value_all[:, columns], preferred_element_type=jnp.float32
        )
        result = (result / total).astype(sent.dtype)
        sent[:, columns] = result[:rows]
        kept[:, columns] = result[rows:]


def multiply(shards, weight, weight_c, held):
    rows = shards[0].shape[0]
    zh, zl = bits()
    core = lax.axis_index("head")
    for m, shard in enumerate(shards):
        held[m * rows : (m + 1) * rows, :] = shard[...]
    total = None
    for other, block in enumerate((weight, weight_c)):
        low = lax.rem(flip(core, other) + zl, 2)
        left = jnp.concatenate(
            [
                held[pl.ds(pl.multiple_of((2 * flip(zh, high) + low) * rows, 16), rows), :]
                for high in range(2)
            ],
            axis=1,
        )
        term = jnp.dot(left, block[...], preferred_element_type=jnp.float32)
        total = term if total is None else total + term
    return total


def project_kernel(kept, *refs):
    shards, (weight, weight_c, out0, out1, held) = refs[:4], refs[4:]
    total = multiply(shards, weight, weight_c, held)
    half = out0.shape[0]
    side = lax.rem(lax.axis_index("wt") + lax.axis_index("head"), 2)
    for high in range(2):
        part = total[high * half : (high + 1) * half].astype(out0.dtype)
        first = flip(side, high) == 1 - kept

        @pl.when(first)
        def _():
            out0[...] = part

        @pl.when(jnp.logical_not(first))
        def _():
            out1[...] = part


def add_kernel(kept, arrived, out):
    out[...] = (kept[...] + arrived[...].astype(jnp.float32)).astype(out.dtype)


def rest_kernel(flags, hidden, cached, out):
    total = hidden[...]
    for layer in range(cached.shape[0]):
        total = total + flags[layer].astype(jnp.float32) * cached[layer]
    out[...] = total


def final_kernel(piece, owned, gate, resting, *refs):
    mixed, fresh, mixed_part, fresh_part, sems = refs[-5:]
    half = owned.shape[0]
    zh, zl = bits()
    rows = pl.ds(pl.multiple_of(flip(lax.rem(zh + zl, 2), piece) * half, 16), half)
    delta = owned[...].astype(jnp.float32) * gate[...]
    fresh_part[...] = delta
    copy_fresh = pltpu.make_async_copy(fresh_part, fresh.at[rows, :], sems.at[0])
    copy_fresh.start()
    mixed_part[...] = resting[rows, :] + delta
    copy_mixed = pltpu.make_async_copy(mixed_part, mixed.at[rows, :], sems.at[1])
    copy_mixed.start()
    copy_fresh.wait()
    copy_mixed.wait()


def along(shard, m):
    return lax.ppermute(shard, "seq", [(z, z ^ m) for z in range(4)])


def call(
    kernel,
    args,
    outs,
    scratch=(),
    space=pltpu.VMEM,
    out_space=pltpu.VMEM,
    flops=0,
    vmem=VMEM_BYTES,
):
    spaces = [pltpu.SMEM if arg.dtype == jnp.int32 else space for arg in args]
    return pl.pallas_call(
        kernel,
        in_specs=[pl.BlockSpec(memory_space=place) for place in spaces],
        out_specs=[pl.BlockSpec(memory_space=out_space)] * len(outs),
        out_shape=[jax.ShapeDtypeStruct(shape, dtype) for shape, dtype in outs],
        scratch_shapes=list(scratch),
        compiler_params=pltpu.CompilerParams(vmem_limit_bytes=vmem),
        cost_estimate=pl.CostEstimate(flops=flops, bytes_accessed=0, transcendentals=0),
    )(*args)


def local_heads(
    queries,
    key_vectors,
    value_vectors,
    out_weight,
    gate_values,
    hidden_state,
    cached_deltas,
    skip_flags,
):
    rows, features = queries.shape
    width = features // 2
    depth, columns = out_weight.shape
    swap = [(0, 1), (1, 0)]
    bf16 = jnp.bfloat16

    packed = call(
        pack_kernel,
        (queries, key_vectors, value_vectors),
        [((2 * rows, width), bf16)] * 2 + [((rows, width), bf16)] * 2,
        [pltpu.SemaphoreType.DMA((10,))],
        space=pl.ANY,
        vmem=PACK_BYTES,
    )
    late_weight, _ = lax.optimization_barrier((out_weight, packed[0]))
    weight_c = lax.ppermute(late_weight, "head", swap)
    moved = []
    for k in range(4):
        k1, k0 = k // 2, k % 2
        pairs = []
        for zz in range(4):
            for cc in range(2):
                to_z = 2 * ((zz // 2) ^ k0) + cc
                pairs.append((zz * 2 + cc, to_z * 2 + ((zz % 2) ^ k1)))
        moved.append(lax.ppermute(packed[k], ("seq", "head"), pairs))
    (joined,) = call(join_kernel, moved, [((4 * rows, width), bf16)])
    sibling = lax.ppermute(joined, "head", swap)
    sibling, _ = lax.optimization_barrier((sibling, weight_c))
    parts = call(
        attention_kernel,
        moved + [sibling],
        [((rows, width), bf16)] * 2,
        [
            pltpu.VMEM((4 * rows, width), bf16),
            pltpu.VMEM((4 * rows, width), bf16),
            pltpu.VMEM((2 * rows, width), bf16),
        ],
        flops=4 * (2 * rows) * (4 * rows) * width,
    )

    half = rows // 2
    flops = 4 * rows * depth * columns
    sent, kept = (
        call(
            functools.partial(project_kernel, i),
            [part] + [along(part, m) for m in (1, 2, 3)] + [out_weight, weight_c],
            [((half, columns), dtype)] * 2,
            [pltpu.VMEM((4 * rows, width), bf16)],
            flops=effort * flops,
        )
        for i, (part, dtype, effort) in enumerate(((parts[0], bf16, 1), (parts[1], jnp.float32, 8)))
    )

    owned = []
    for p in range(2):
        arrived = lax.ppermute(sent[p], "wt", swap)
        (summed,) = call(add_kernel, (kept[p], arrived), [((half, columns), bf16)])
        pairs = []
        for zz in range(4):
            for xx in range(2):
                for cc in range(2):
                    to = ((cc + 2 * (p ^ xx ^ cc)) * 2 + zz // 2) * 2 + zz % 2
                    pairs.append(((zz * 2 + xx) * 2 + cc, to))
        owned.append(lax.ppermute(summed, ("seq", "wt", "head"), pairs))
    (resting,) = call(
        rest_kernel, (skip_flags, hidden_state, cached_deltas), [((rows, columns), jnp.float32)]
    )
    gate = gate_values[None, :]
    results = ()
    for p, part in enumerate(owned):
        results = pl.pallas_call(
            functools.partial(final_kernel, p),
            in_specs=[pl.BlockSpec(memory_space=pltpu.VMEM)] * 3
            + [pl.BlockSpec(memory_space=pl.ANY)] * len(results),
            out_specs=[pl.BlockSpec(memory_space=pl.ANY)] * 2,
            out_shape=[jax.ShapeDtypeStruct((rows, columns), jnp.float32)] * 2,
            scratch_shapes=[pltpu.VMEM((half, columns), jnp.float32)] * 2
            + [pltpu.SemaphoreType.DMA((2,))],
            input_output_aliases={3 + i: i for i in range(len(results))},
            compiler_params=pltpu.CompilerParams(vmem_limit_bytes=VMEM_BYTES),
            cost_estimate=pl.CostEstimate(flops=0, bytes_accessed=0, transcendentals=0),
        )(part, gate, resting, *results)
    return tuple(results)


def solution(mesh):
    placed = (
        P(("groups", "seq"), ("wt", "head")),
        P(("groups", "seq"), ("wt", "head")),
        P(("groups", "seq"), ("wt", "head")),
        P(("wt", "head"), "seq"),
        P(("groups", "wt", "head")),
        P(("groups", "seq"), ("wt", "head")),
        P(None, ("groups", "seq"), ("wt", "head")),
        P("groups"),
    )

    def local(*args):
        sizes = tuple(mesh.shape[name] for name in ("seq", "wt", "head"))
        rows, features = args[0].shape
        if sizes == (4, 2, 2) and rows % 32 == 0 and features % (2 * HEAD_DIM) == 0:
            return local_heads(*args)
        return local_general(*args)

    return jax.shard_map(
        local,
        mesh=mesh,
        in_specs=placed,
        out_specs=(P(("groups", "seq"), ("wt", "head")), P(("groups", "seq"), ("wt", "head"))),
        check_vma=False,
    )
```

```python
import functools

import jax
import jax.numpy as jnp
from jax import lax
from jax.experimental import pallas as pl
from jax.experimental.pallas import tpu as pltpu
from jax.sharding import PartitionSpec as P

HEAD_DIM = 128
VMEM_BYTES = 48 * 1024 * 1024
PACK_BYTES = 53 * 1024 * 1024 + 128 * 1024
LOG2_E = 1.4426950408889634
ORDERS = ((2, 3, 1), (1, 2, 3))


def attend(state_in, key_rows, value_rows, query_heads, score_scale):
    key_count = key_rows.shape[0]
    head_count = query_heads.shape[1]
    blocks = -(-key_count // 1024)
    while key_count % blocks:
        blocks = blocks + 1
    block_size = key_count // blocks

    def one_block(block_index, state_now):
        row_peak, row_total, weighted = state_now
        start_row = block_index * block_size
        key_block = lax.dynamic_slice_in_dim(key_rows, start_row, block_size, 0)
        value_block = lax.dynamic_slice_in_dim(value_rows, start_row, block_size, 0)
        key_heads = key_block.reshape(block_size, head_count, HEAD_DIM)
        value_heads = value_block.reshape(block_size, head_count, HEAD_DIM)
        scores = (
            jnp.einsum("ihd,jhd->hij", query_heads, key_heads, preferred_element_type=jnp.float32)
            * score_scale
        )
        new_peak = jnp.maximum(row_peak, jnp.max(scores, axis=2))
        exp_scores = jnp.exp(scores - new_peak[:, :, None])
        rescale = jnp.exp(row_peak - new_peak)
        row_total = row_total * rescale + jnp.sum(exp_scores, axis=2)
        weighted = weighted * rescale[:, :, None] + jnp.einsum(
            "hij,jhd->hid",
            exp_scores.astype(jnp.bfloat16),
            value_heads,
            preferred_element_type=jnp.float32,
        )
        return (new_peak, row_total, weighted)

    return lax.fori_loop(0, blocks, one_block, state_in)


def finish(state_out, row_count):
    row_peak, row_total, weighted = state_out
    normed = weighted / row_total[:, :, None]
    return normed.transpose(1, 0, 2).reshape(row_count, -1).astype(jnp.bfloat16)


def local_general(
    queries,
    key_vectors,
    value_vectors,
    out_weight,
    gate_values,
    hidden_state,
    cached_deltas,
    skip_flags,
):
    row_count = queries.shape[0]
    head_count = queries.shape[1] // HEAD_DIM
    score_scale = HEAD_DIM ** (-0.5)
    query_heads = queries.reshape(row_count, head_count, HEAD_DIM)
    start_state = (
        jnp.full((head_count, row_count), -1e30, jnp.float32),
        jnp.zeros((head_count, row_count), jnp.float32),
        jnp.zeros((head_count, row_count, HEAD_DIM), jnp.float32),
    )
    gathered_keys, gathered_values, gathered_weight = (
        lax.all_gather(key_vectors, "seq", axis=0, tiled=True),
        lax.all_gather(value_vectors, "seq", axis=0, tiled=True),
        lax.all_gather(out_weight, "seq", axis=1, tiled=True),
    )
    final_state = attend(start_state, gathered_keys, gathered_values, query_heads, score_scale)
    attention_out = finish(final_state, row_count)
    partial_sums = jnp.dot(attention_out, gathered_weight, preferred_element_type=jnp.float32)
    head_total = lax.psum_scatter(
        partial_sums.astype(jnp.bfloat16), ("wt", "head"), scatter_dimension=1, tiled=True
    ).astype(jnp.float32)
    fresh_delta = head_total * gate_values[None, :]
    kept_deltas = jnp.sum(skip_flags.astype(jnp.float32)[:, None, None] * cached_deltas, axis=0)
    mixed_state = hidden_state + kept_deltas + fresh_delta
    return (mixed_state, fresh_delta)


def bits():
    z = lax.axis_index("seq")
    return lax.div(z, 2), lax.rem(z, 2)


def flip(bit, value):
    return 1 - bit if value else bit


def pack_kernel(queries, keys, values, *refs):
    outs, sems = refs[:4], refs[4]
    rows, width = queries.shape[0], outs[0].shape[1]
    half = rows // 2
    zh, zl = bits()
    copies = []
    for k in range(4):
        part = pl.ds(pl.multiple_of(flip(zl, k // 2) * half, 16), half)
        columns = pl.ds(pl.multiple_of(flip(zh, k % 2) * width, 128), width)
        moves = [
            (keys.at[part, columns], outs[k].at[pl.ds(0, half), :]),
            (values.at[part, columns], outs[k].at[pl.ds(half, half), :]),
        ]
        if k < 2:
            moves.append((queries.at[:, columns], outs[k].at[pl.ds(rows, rows), :]))
        for start, end in moves:
            copies.append(pltpu.make_async_copy(start, end, sems.at[len(copies)]))
    for copy in copies:
        copy.start()
    for copy in copies:
        copy.wait()


def join_kernel(*refs):
    blocks, joined = refs[:4], refs[4]
    rows = joined.shape[0] // 4
    for k, block in enumerate(blocks):
        joined[k * rows : (k + 1) * rows, :] = block[:rows, :]


def exp_scaled(scores):
    return jnp.exp2(scores * (LOG2_E * HEAD_DIM ** (-0.5)))


def dot_keys(queries, keys):
    return lax.dot_general(
        queries, keys, (((1,), (1,)), ((), ())), preferred_element_type=jnp.float32
    )


def near_attention_kernel(*refs):
    blocks, (query_all, weighted, peaks, totals, key_all, value_all) = refs[:4], refs[4:]
    half = query_all.shape[0] // 4
    rows = 2 * half
    for k in range(4):
        here = slice(k * half, (k + 1) * half)
        key_all[here, :] = blocks[k][:half, :]
        value_all[here, :] = blocks[k][half:rows, :]
    zh, _ = bits()
    x = lax.axis_index("wt")
    for k in range(2):
        for part in range(2):
            at = rows + flip(x, part == 0) * half
            to = (part * 2 + flip(zh, k)) * half
            query_all[pl.ds(pl.multiple_of(to, 16), half), :] = blocks[k][
                pl.ds(pl.multiple_of(at, 16), half), :
            ]
    for h in range(query_all.shape[1] // HEAD_DIM):
        columns = slice(h * HEAD_DIM, (h + 1) * HEAD_DIM)
        scores = dot_keys(query_all[:, columns], key_all[:, columns])
        peak = jnp.max(scores, axis=1, keepdims=True)
        weights = exp_scaled(scores - peak)
        weighted[:, columns] = jnp.dot(
            weights.astype(jnp.bfloat16), value_all[:, columns], preferred_element_type=jnp.float32
        )
        shape = (scores.shape[0], HEAD_DIM)
        peaks[:, columns] = jnp.broadcast_to(peak, shape)
        totals[:, columns] = jnp.broadcast_to(jnp.sum(weights, axis=1, keepdims=True), shape)


def attention_kernel(query_all, weighted, peaks, totals, sibling, *refs):
    sent, kept, key_all, value_all = refs
    rows = sent.shape[0]
    half = rows // 2
    for k in range(4):
        there = slice(k * half, (k + 1) * half)
        key_all[there, :] = sibling[k * rows : k * rows + half, :]
        value_all[there, :] = sibling[k * rows + half : (k + 1) * rows, :]
    for h in range(sent.shape[1] // HEAD_DIM):
        columns = slice(h * HEAD_DIM, (h + 1) * HEAD_DIM)
        scores = dot_keys(query_all[:, columns], key_all[:, columns])
        first_peak = peaks[:, columns]
        peak = jnp.maximum(first_peak, jnp.max(scores, axis=1, keepdims=True))
        rescale = exp_scaled(first_peak - peak)
        weights = exp_scaled(scores - peak[:, :1])
        total = totals[:, columns] * rescale + jnp.sum(weights, axis=1, keepdims=True)
        result = weighted[:, columns] * rescale + jnp.dot(
            weights.astype(jnp.bfloat16), value_all[:, columns], preferred_element_type=jnp.float32
        )
        result = (result / total).astype(sent.dtype)
        sent[:, columns] = result[:rows]
        kept[:, columns] = result[rows:]


def multiply(shards, order, weight, weight_c, held):
    rows = shards[0].shape[0]
    zh, zl = bits()
    core = lax.axis_index("head")
    for m, shard in zip((0,) + order, shards):
        held[m * rows : (m + 1) * rows, :] = shard[...]
    total = None
    for other, block in enumerate((weight, weight_c)):
        low = lax.rem(flip(core, other) + zl, 2)
        left = jnp.concatenate(
            [
                held[pl.ds(pl.multiple_of((2 * flip(zh, high) + low) * rows, 16), rows), :]
                for high in range(2)
            ],
            axis=1,
        )
        term = jnp.dot(left, block[...], preferred_element_type=jnp.float32)
        total = term if total is None else total + term
    return total


def project_kernel(kept, *refs):
    shards, (weight, weight_c, out0, out1, held) = refs[:4], refs[4:]
    total = multiply(shards, ORDERS[kept], weight, weight_c, held)
    half = out0.shape[0]
    x = lax.axis_index("wt")
    for low in range(2):
        part = total[low * half : (low + 1) * half].astype(out0.dtype)
        first = flip(x, low) == 1 - kept

        @pl.when(first)
        def _():
            out0[...] = part

        @pl.when(jnp.logical_not(first))
        def _():
            out1[...] = part


def add_kernel(kept, arrived, out):
    out[...] = (kept[...] + arrived[...].astype(jnp.float32)).astype(out.dtype)


def rest_kernel(flags, hidden, cached, out):
    total = hidden[...]
    for layer in range(cached.shape[0]):
        total = total + flags[layer].astype(jnp.float32) * cached[layer]
    out[...] = total


def final_kernel(owned0, owned1, gate, resting, mixed, fresh, mixed_part, fresh_part, sems):
    half, count = owned0.shape[0], owned0.shape[1] // 2
    zh, _ = bits()
    copies = []
    for p, owned in enumerate((owned0, owned1)):
        rows = pl.ds(pl.multiple_of(flip(zh, p) * half, 16), half)
        for h in range(2):
            columns = slice(h * count, (h + 1) * count)
            delta = owned[:, columns].astype(jnp.float32) * gate[:, columns]
            fresh_part[rows, columns] = delta
            mixed_part[rows, columns] = resting[rows, columns] + delta
            for part, out in ((fresh_part, fresh), (mixed_part, mixed)):
                copies.append(
                    pltpu.make_async_copy(
                        part.at[rows, columns], out.at[rows, columns], sems.at[len(copies)]
                    )
                )
                copies[-1].start()
    for copy in copies:
        copy.wait()


def along(shard, m):
    return lax.ppermute(shard, "seq", [(z, z ^ m) for z in range(4)])


def call(
    kernel,
    args,
    outs,
    scratch=(),
    space=pltpu.VMEM,
    out_space=pltpu.VMEM,
    flops=0,
    vmem=VMEM_BYTES,
):
    spaces = [pltpu.SMEM if arg.dtype == jnp.int32 else space for arg in args]
    return pl.pallas_call(
        kernel,
        in_specs=[pl.BlockSpec(memory_space=place) for place in spaces],
        out_specs=[pl.BlockSpec(memory_space=out_space)] * len(outs),
        out_shape=[jax.ShapeDtypeStruct(shape, dtype) for shape, dtype in outs],
        scratch_shapes=list(scratch),
        compiler_params=pltpu.CompilerParams(vmem_limit_bytes=vmem),
        cost_estimate=pl.CostEstimate(flops=flops, bytes_accessed=0, transcendentals=0),
    )(*args)


def local_heads(
    queries,
    key_vectors,
    value_vectors,
    out_weight,
    gate_values,
    hidden_state,
    cached_deltas,
    skip_flags,
):
    rows, features = queries.shape
    width = features // 2
    depth, columns = out_weight.shape
    swap = [(0, 1), (1, 0)]
    bf16 = jnp.bfloat16

    packed = call(
        pack_kernel,
        (queries, key_vectors, value_vectors),
        [((2 * rows, width), bf16)] * 2 + [((rows, width), bf16)] * 2,
        [pltpu.SemaphoreType.DMA((10,))],
        space=pl.ANY,
        vmem=PACK_BYTES,
    )
    late_weight, _ = lax.optimization_barrier((out_weight, packed[0]))
    weight_c = lax.ppermute(late_weight, "head", swap)
    moved = []
    for k in range(4):
        k1, k0 = k // 2, k % 2
        pairs = []
        for zz in range(4):
            for cc in range(2):
                to_z = 2 * ((zz // 2) ^ k0) + cc
                pairs.append((zz * 2 + cc, to_z * 2 + ((zz % 2) ^ k1)))
        moved.append(lax.ppermute(packed[k], ("seq", "head"), pairs))
    (joined,) = call(join_kernel, moved, [((4 * rows, width), bf16)])
    sibling = lax.ppermute(joined, "head", swap)
    sibling, _ = lax.optimization_barrier((sibling, weight_c))
    flops = 4 * (2 * rows) * (2 * rows) * width
    half_keys = [pltpu.VMEM((2 * rows, width), bf16)] * 2
    near = call(
        near_attention_kernel,
        moved,
        [((2 * rows, width), bf16)] + [((2 * rows, width), jnp.float32)] * 3,
        half_keys,
        flops=flops,
    )
    parts = call(
        attention_kernel,
        list(near) + [sibling],
        [((rows, width), bf16)] * 2,
        half_keys,
        flops=flops,
    )

    half = rows // 2
    flops = 4 * rows * depth * columns
    sent, kept = (
        call(
            functools.partial(project_kernel, i),
            [part] + [along(part, m) for m in ORDERS[i]] + [out_weight, weight_c],
            [((half, columns), dtype)] * 2,
            [pltpu.VMEM((4 * rows, width), bf16)],
            flops=effort * flops,
        )
        for i, (part, dtype, effort) in enumerate(((parts[0], bf16, 1), (parts[1], jnp.float32, 8)))
    )

    owned = []
    for p in range(2):
        arrived = lax.ppermute(sent[p], "wt", swap)
        (summed,) = call(add_kernel, (kept[p], arrived), [((half, columns), bf16)])
        pairs = []
        for zz in range(4):
            for xx in range(2):
                for cc in range(2):
                    to = ((cc + 2 * (p ^ xx)) * 2 + zz // 2) * 2 + zz % 2
                    pairs.append(((zz * 2 + xx) * 2 + cc, to))
        owned.append(lax.ppermute(summed, ("seq", "wt", "head"), pairs))
    (resting,) = call(
        rest_kernel, (skip_flags, hidden_state, cached_deltas), [((rows, columns), jnp.float32)]
    )
    return tuple(
        call(
            final_kernel,
            (*owned, gate_values[None, :], resting),
            [((rows, columns), jnp.float32)] * 2,
            [pltpu.VMEM((rows, columns), jnp.float32)] * 2 + [pltpu.SemaphoreType.DMA((8,))],
            out_space=pl.ANY,
        )
    )


def solution(mesh):
    placed = (
        P(("groups", "seq"), ("wt", "head")),
        P(("groups", "seq"), ("wt", "head")),
        P(("groups", "seq"), ("wt", "head")),
        P(("wt", "head"), "seq"),
        P(("groups", "wt", "head")),
        P(("groups", "seq"), ("wt", "head")),
        P(None, ("groups", "seq"), ("wt", "head")),
        P("groups"),
    )

    def local(*args):
        sizes = tuple(mesh.shape[name] for name in ("seq", "wt", "head"))
        rows, features = args[0].shape
        if sizes == (4, 2, 2) and rows % 32 == 0 and features % (2 * HEAD_DIM) == 0 and args[3].shape[1] % 256 == 0:
            return local_heads(*args)
        return local_general(*args)

    return jax.shard_map(
        local,
        mesh=mesh,
        in_specs=placed,
        out_specs=(P(("groups", "seq"), ("wt", "head")), P(("groups", "seq"), ("wt", "head"))),
        check_vma=False,
    )
```

```python
import functools

import jax
import jax.numpy as jnp
from jax import lax
from jax.experimental import pallas as pl
from jax.experimental.pallas import tpu as pltpu
from jax.sharding import PartitionSpec as P

HEAD_DIM = 128
VMEM_BYTES = 48 * 1024 * 1024
PACK_BYTES = 53 * 1024 * 1024 + 128 * 1024
LOG2_E = 1.4426950408889634


def attend(state_in, key_rows, value_rows, query_heads, score_scale):
    key_count = key_rows.shape[0]
    head_count = query_heads.shape[1]
    blocks = -(-key_count // 1024)
    while key_count % blocks:
        blocks = blocks + 1
    block_size = key_count // blocks

    def one_block(block_index, state_now):
        row_peak, row_total, weighted = state_now
        start_row = block_index * block_size
        key_block = lax.dynamic_slice_in_dim(key_rows, start_row, block_size, 0)
        value_block = lax.dynamic_slice_in_dim(value_rows, start_row, block_size, 0)
        key_heads = key_block.reshape(block_size, head_count, HEAD_DIM)
        value_heads = value_block.reshape(block_size, head_count, HEAD_DIM)
        scores = (
            jnp.einsum("ihd,jhd->hij", query_heads, key_heads, preferred_element_type=jnp.float32)
            * score_scale
        )
        new_peak = jnp.maximum(row_peak, jnp.max(scores, axis=2))
        exp_scores = jnp.exp(scores - new_peak[:, :, None])
        rescale = jnp.exp(row_peak - new_peak)
        row_total = row_total * rescale + jnp.sum(exp_scores, axis=2)
        weighted = weighted * rescale[:, :, None] + jnp.einsum(
            "hij,jhd->hid",
            exp_scores.astype(jnp.bfloat16),
            value_heads,
            preferred_element_type=jnp.float32,
        )
        return (new_peak, row_total, weighted)

    return lax.fori_loop(0, blocks, one_block, state_in)


def finish(state_out, row_count):
    row_peak, row_total, weighted = state_out
    normed = weighted / row_total[:, :, None]
    return normed.transpose(1, 0, 2).reshape(row_count, -1).astype(jnp.bfloat16)


def local_general(
    queries,
    key_vectors,
    value_vectors,
    out_weight,
    gate_values,
    hidden_state,
    cached_deltas,
    skip_flags,
):
    row_count = queries.shape[0]
    head_count = queries.shape[1] // HEAD_DIM
    score_scale = HEAD_DIM ** (-0.5)
    query_heads = queries.reshape(row_count, head_count, HEAD_DIM)
    start_state = (
        jnp.full((head_count, row_count), -1e30, jnp.float32),
        jnp.zeros((head_count, row_count), jnp.float32),
        jnp.zeros((head_count, row_count, HEAD_DIM), jnp.float32),
    )
    gathered_keys, gathered_values, gathered_weight = (
        lax.all_gather(key_vectors, "seq", axis=0, tiled=True),
        lax.all_gather(value_vectors, "seq", axis=0, tiled=True),
        lax.all_gather(out_weight, "seq", axis=1, tiled=True),
    )
    final_state = attend(start_state, gathered_keys, gathered_values, query_heads, score_scale)
    attention_out = finish(final_state, row_count)
    partial_sums = jnp.dot(attention_out, gathered_weight, preferred_element_type=jnp.float32)
    head_total = lax.psum_scatter(
        partial_sums.astype(jnp.bfloat16), ("wt", "head"), scatter_dimension=1, tiled=True
    ).astype(jnp.float32)
    fresh_delta = head_total * gate_values[None, :]
    kept_deltas = jnp.sum(skip_flags.astype(jnp.float32)[:, None, None] * cached_deltas, axis=0)
    mixed_state = hidden_state + kept_deltas + fresh_delta
    return (mixed_state, fresh_delta)


def bits():
    z = lax.axis_index("seq")
    return lax.div(z, 2), lax.rem(z, 2)


def flip(bit, value):
    return 1 - bit if value else bit


def pack_kernel(queries, keys, values, *refs):
    outs, sems = refs[:4], refs[4]
    rows, width = queries.shape[0], outs[0].shape[1]
    half = rows // 2
    zh, zl = bits()
    copies = []
    for k in range(4):
        part = pl.ds(pl.multiple_of(flip(zl, k // 2) * half, 16), half)
        columns = pl.ds(pl.multiple_of(flip(zh, k % 2) * width, 128), width)
        moves = [
            (keys.at[part, columns], outs[k].at[pl.ds(0, half), :]),
            (values.at[part, columns], outs[k].at[pl.ds(half, half), :]),
        ]
        if k < 2:
            moves.append((queries.at[:, columns], outs[k].at[pl.ds(rows, rows), :]))
        for start, end in moves:
            copies.append(pltpu.make_async_copy(start, end, sems.at[len(copies)]))
    for copy in copies:
        copy.start()
    for copy in copies:
        copy.wait()


def join_kernel(*refs):
    blocks, joined = refs[:4], refs[4]
    rows = joined.shape[0] // 4
    for k, block in enumerate(blocks):
        joined[k * rows : (k + 1) * rows, :] = block[:rows, :]


def attention_kernel(*refs):
    blocks, sibling = refs[:4], refs[4]
    sent, kept0, kept1, key_all, value_all, query_all = refs[5:]
    rows = sent.shape[0]
    half = rows // 2
    for k in range(4):
        here, there = slice(k * half, (k + 1) * half), slice((4 + k) * half, (5 + k) * half)
        key_all[here, :] = blocks[k][:half, :]
        value_all[here, :] = blocks[k][half:rows, :]
        key_all[there, :] = sibling[k * rows : k * rows + half, :]
        value_all[there, :] = sibling[k * rows + half : (k + 1) * rows, :]
    zh, _ = bits()
    x = lax.axis_index("wt")
    for k in range(2):
        high = flip(zh, k)
        for at, to in ((1 - x, high), (x, 2 + lax.rem(high + x, 2))):
            at, to = rows + at * half, to * half
            query_all[pl.ds(pl.multiple_of(to, 16), half), :] = blocks[k][
                pl.ds(pl.multiple_of(at, 16), half), :
            ]
    for h in range(sent.shape[1] // HEAD_DIM):
        columns = slice(h * HEAD_DIM, (h + 1) * HEAD_DIM)
        scores = lax.dot_general(
            query_all[:, columns],
            key_all[:, columns],
            (((1,), (1,)), ((), ())),
            preferred_element_type=jnp.float32,
        )
        peak = jnp.max(scores, axis=1, keepdims=True)
        weights = jnp.exp2((scores - peak) * (LOG2_E * HEAD_DIM ** (-0.5)))
        total = jnp.sum(weights, axis=1, keepdims=True)
        result = jnp.dot(
            weights.astype(jnp.bfloat16), value_all[:, columns], preferred_element_type=jnp.float32
        )
        result = (result / total).astype(sent.dtype)
        sent[:, columns] = result[:rows]
        kept0[:, columns] = result[rows : rows + half]
        kept1[:, columns] = result[rows + half :]


def multiply(shards, weight, weight_c, held):
    rows = shards[0].shape[0]
    zh, zl = bits()
    core = lax.axis_index("head")
    for m, shard in enumerate(shards):
        held[m * rows : (m + 1) * rows, :] = shard[...]
    total = None
    for other, block in enumerate((weight, weight_c)):
        low = lax.rem(flip(core, other) + zl, 2)
        left = jnp.concatenate(
            [
                held[pl.ds(pl.multiple_of((2 * flip(zh, high) + low) * rows, 16), rows), :]
                for high in range(2)
            ],
            axis=1,
        )
        term = jnp.dot(left, block[...], preferred_element_type=jnp.float32)
        total = term if total is None else total + term
    return total


def sent_kernel(*refs):
    shards, (weight, weight_c, out0, out1, held) = refs[:4], refs[4:]
    total = multiply(shards, weight, weight_c, held)
    half = out0.shape[0]
    x = lax.axis_index("wt")
    for high in range(2):
        part = total[high * half : (high + 1) * half].astype(out0.dtype)

        @pl.when(x != high)
        def _():
            out0[...] = part

        @pl.when(x == high)
        def _():
            out1[...] = part


def kept_kernel(*refs):
    shards, (weight, weight_c, out, held) = refs[:4], refs[4:]
    out[...] = multiply(shards, weight, weight_c, held)


def add_kernel(kept, arrived, out):
    out[...] = (kept[...] + arrived[...].astype(jnp.float32)).astype(out.dtype)


def rest_kernel(flags, hidden, cached, out):
    total = hidden[...]
    for layer in range(cached.shape[0]):
        total = total + flags[layer].astype(jnp.float32) * cached[layer]
    out[...] = total


def final_kernel(piece, owned, gate, resting, *refs):
    mixed, fresh, mixed_part, fresh_part, sems = refs[-5:]
    half = owned.shape[0]
    zh, _ = bits()
    rows = pl.ds(pl.multiple_of(flip(zh, piece) * half, 16), half)
    delta = owned[...].astype(jnp.float32) * gate[...]
    fresh_part[...] = delta
    copy_fresh = pltpu.make_async_copy(fresh_part, fresh.at[rows, :], sems.at[0])
    copy_fresh.start()
    mixed_part[...] = resting[rows, :] + delta
    copy_mixed = pltpu.make_async_copy(mixed_part, mixed.at[rows, :], sems.at[1])
    copy_mixed.start()
    copy_fresh.wait()
    copy_mixed.wait()


def along(shard, m):
    return lax.ppermute(shard, "seq", [(z, z ^ m) for z in range(4)])


def call(
    kernel,
    args,
    outs,
    scratch=(),
    space=pltpu.VMEM,
    out_space=pltpu.VMEM,
    flops=0,
    vmem=VMEM_BYTES,
):
    spaces = [pltpu.SMEM if arg.dtype == jnp.int32 else space for arg in args]
    return pl.pallas_call(
        kernel,
        in_specs=[pl.BlockSpec(memory_space=place) for place in spaces],
        out_specs=[pl.BlockSpec(memory_space=out_space)] * len(outs),
        out_shape=[jax.ShapeDtypeStruct(shape, dtype) for shape, dtype in outs],
        scratch_shapes=list(scratch),
        compiler_params=pltpu.CompilerParams(vmem_limit_bytes=vmem),
        cost_estimate=pl.CostEstimate(flops=flops, bytes_accessed=0, transcendentals=0),
    )(*args)


def local_heads(
    queries,
    key_vectors,
    value_vectors,
    out_weight,
    gate_values,
    hidden_state,
    cached_deltas,
    skip_flags,
):
    rows, features = queries.shape
    width = features // 2
    depth, columns = out_weight.shape
    swap = [(0, 1), (1, 0)]
    bf16 = jnp.bfloat16

    packed = call(
        pack_kernel,
        (queries, key_vectors, value_vectors),
        [((2 * rows, width), bf16)] * 2 + [((rows, width), bf16)] * 2,
        [pltpu.SemaphoreType.DMA((10,))],
        space=pl.ANY,
        vmem=PACK_BYTES,
    )
    late_weight, _ = lax.optimization_barrier((out_weight, packed[0]))
    weight_c = lax.ppermute(late_weight, "head", swap)
    moved = []
    for k in range(4):
        k1, k0 = k // 2, k % 2
        pairs = []
        for zz in range(4):
            for cc in range(2):
                to_z = 2 * ((zz // 2) ^ k0) + cc
                pairs.append((zz * 2 + cc, to_z * 2 + ((zz % 2) ^ k1)))
        moved.append(lax.ppermute(packed[k], ("seq", "head"), pairs))
    (joined,) = call(join_kernel, moved, [((4 * rows, width), bf16)])
    sibling = lax.ppermute(joined, "head", swap)
    sibling, _ = lax.optimization_barrier((sibling, weight_c))
    parts = call(
        attention_kernel,
        moved + [sibling],
        [((rows, width), bf16)] + [((rows // 2, width), bf16)] * 2,
        [
            pltpu.VMEM((4 * rows, width), bf16),
            pltpu.VMEM((4 * rows, width), bf16),
            pltpu.VMEM((2 * rows, width), bf16),
        ],
        flops=4 * (2 * rows) * (4 * rows) * width,
    )

    half = rows // 2
    flops = 4 * rows * depth * columns
    weights = [out_weight, weight_c]
    shards = [[part] + [along(part, m) for m in (1, 2, 3)] for part in parts[:2]]
    sent = call(
        sent_kernel,
        shards[0] + weights,
        [((half, columns), bf16)] * 2,
        [pltpu.VMEM((4 * rows, width), bf16)],
        flops=flops,
    )
    part, _ = lax.optimization_barrier((parts[2], sent[0]))
    shards.append([part] + [along(part, m) for m in (1, 2, 3)])

    owned = []
    for p in range(2):
        arrived = lax.ppermute(sent[p], "wt", swap)
        (kept,) = call(
            kept_kernel,
            shards[1 + p] + weights,
            [((half, columns), jnp.float32)],
            [pltpu.VMEM((4 * half, width), bf16)],
            flops=flops,
        )
        (summed,) = call(add_kernel, (kept, arrived), [((half, columns), bf16)])
        pairs = []
        for zz in range(4):
            for xx in range(2):
                for cc in range(2):
                    to = ((cc + 2 * (p ^ xx)) * 2 + zz // 2) * 2 + zz % 2
                    pairs.append(((zz * 2 + xx) * 2 + cc, to))
        owned.append(lax.ppermute(summed, ("seq", "wt", "head"), pairs))
    (resting,) = call(
        rest_kernel, (skip_flags, hidden_state, cached_deltas), [((rows, columns), jnp.float32)]
    )
    gate = gate_values[None, :]
    results = ()
    for p, part in enumerate(owned):
        results = pl.pallas_call(
            functools.partial(final_kernel, p),
            in_specs=[pl.BlockSpec(memory_space=pltpu.VMEM)] * 3
            + [pl.BlockSpec(memory_space=pl.ANY)] * len(results),
            out_specs=[pl.BlockSpec(memory_space=pl.ANY)] * 2,
            out_shape=[jax.ShapeDtypeStruct((rows, columns), jnp.float32)] * 2,
            scratch_shapes=[pltpu.VMEM((half, columns), jnp.float32)] * 2
            + [pltpu.SemaphoreType.DMA((2,))],
            input_output_aliases={3 + i: i for i in range(len(results))},
            compiler_params=pltpu.CompilerParams(vmem_limit_bytes=VMEM_BYTES),
            cost_estimate=pl.CostEstimate(flops=0, bytes_accessed=0, transcendentals=0),
        )(part, gate, resting, *results)
    return tuple(results)


def solution(mesh):
    placed = (
        P(("groups", "seq"), ("wt", "head")),
        P(("groups", "seq"), ("wt", "head")),
        P(("groups", "seq"), ("wt", "head")),
        P(("wt", "head"), "seq"),
        P(("groups", "wt", "head")),
        P(("groups", "seq"), ("wt", "head")),
        P(None, ("groups", "seq"), ("wt", "head")),
        P("groups"),
    )

    def local(*args):
        sizes = tuple(mesh.shape[name] for name in ("seq", "wt", "head"))
        rows, features = args[0].shape
        if sizes == (4, 2, 2) and rows % 32 == 0 and features % (2 * HEAD_DIM) == 0:
            return local_heads(*args)
        return local_general(*args)

    return jax.shard_map(
        local,
        mesh=mesh,
        in_specs=placed,
        out_specs=(P(("groups", "seq"), ("wt", "head")), P(("groups", "seq"), ("wt", "head"))),
        check_vma=False,
    )
```

```python
import functools

import jax
import jax.numpy as jnp
from jax import lax
from jax.experimental import pallas as pl
from jax.experimental.pallas import tpu as pltpu
from jax.sharding import PartitionSpec as P

HEAD_DIM = 128
VMEM_BYTES = 48 * 1024 * 1024
PACK_BYTES = 53 * 1024 * 1024 + 128 * 1024
LOG2_E = 1.4426950408889634


def attend(state_in, key_rows, value_rows, query_heads, score_scale):
    key_count = key_rows.shape[0]
    head_count = query_heads.shape[1]
    blocks = -(-key_count // 1024)
    while key_count % blocks:
        blocks = blocks + 1
    block_size = key_count // blocks

    def one_block(block_index, state_now):
        row_peak, row_total, weighted = state_now
        start_row = block_index * block_size
        key_block = lax.dynamic_slice_in_dim(key_rows, start_row, block_size, 0)
        value_block = lax.dynamic_slice_in_dim(value_rows, start_row, block_size, 0)
        key_heads = key_block.reshape(block_size, head_count, HEAD_DIM)
        value_heads = value_block.reshape(block_size, head_count, HEAD_DIM)
        scores = (
            jnp.einsum("ihd,jhd->hij", query_heads, key_heads, preferred_element_type=jnp.float32)
            * score_scale
        )
        new_peak = jnp.maximum(row_peak, jnp.max(scores, axis=2))
        exp_scores = jnp.exp(scores - new_peak[:, :, None])
        rescale = jnp.exp(row_peak - new_peak)
        row_total = row_total * rescale + jnp.sum(exp_scores, axis=2)
        weighted = weighted * rescale[:, :, None] + jnp.einsum(
            "hij,jhd->hid",
            exp_scores.astype(jnp.bfloat16),
            value_heads,
            preferred_element_type=jnp.float32,
        )
        return (new_peak, row_total, weighted)

    return lax.fori_loop(0, blocks, one_block, state_in)


def finish(state_out, row_count):
    row_peak, row_total, weighted = state_out
    normed = weighted / row_total[:, :, None]
    return normed.transpose(1, 0, 2).reshape(row_count, -1).astype(jnp.bfloat16)


def local_general(
    queries,
    key_vectors,
    value_vectors,
    out_weight,
    gate_values,
    hidden_state,
    cached_deltas,
    skip_flags,
):
    row_count = queries.shape[0]
    head_count = queries.shape[1] // HEAD_DIM
    score_scale = HEAD_DIM ** (-0.5)
    query_heads = queries.reshape(row_count, head_count, HEAD_DIM)
    start_state = (
        jnp.full((head_count, row_count), -1e30, jnp.float32),
        jnp.zeros((head_count, row_count), jnp.float32),
        jnp.zeros((head_count, row_count, HEAD_DIM), jnp.float32),
    )
    gathered_keys, gathered_values, gathered_weight = (
        lax.all_gather(key_vectors, "seq", axis=0, tiled=True),
        lax.all_gather(value_vectors, "seq", axis=0, tiled=True),
        lax.all_gather(out_weight, "seq", axis=1, tiled=True),
    )
    final_state = attend(start_state, gathered_keys, gathered_values, query_heads, score_scale)
    attention_out = finish(final_state, row_count)
    partial_sums = jnp.dot(attention_out, gathered_weight, preferred_element_type=jnp.float32)
    head_total = lax.psum_scatter(
        partial_sums.astype(jnp.bfloat16), ("wt", "head"), scatter_dimension=1, tiled=True
    ).astype(jnp.float32)
    fresh_delta = head_total * gate_values[None, :]
    kept_deltas = jnp.sum(skip_flags.astype(jnp.float32)[:, None, None] * cached_deltas, axis=0)
    mixed_state = hidden_state + kept_deltas + fresh_delta
    return (mixed_state, fresh_delta)


def bits():
    z = lax.axis_index("seq")
    return lax.div(z, 2), lax.rem(z, 2)


def flip(bit, value):
    return 1 - bit if value else bit


def pack_kernel(queries, keys, values, *refs):
    outs, sems = refs[:4], refs[4]
    rows, width = queries.shape[0], outs[0].shape[1]
    half = rows // 2
    zh, zl = bits()
    copies = []
    for k in range(4):
        part = pl.ds(pl.multiple_of(flip(zl, k // 2) * half, 16), half)
        columns = pl.ds(pl.multiple_of(flip(zh, 1 - k % 2) * width, 128), width)
        moves = [
            (keys.at[part, columns], outs[k].at[pl.ds(0, half), :]),
            (values.at[part, columns], outs[k].at[pl.ds(half, half), :]),
        ]
        if k < 2:
            moves.append((queries.at[:, columns], outs[k].at[pl.ds(rows, rows), :]))
        for start, end in moves:
            copies.append(pltpu.make_async_copy(start, end, sems.at[len(copies)]))
    for copy in copies:
        copy.start()
    for copy in copies:
        copy.wait()


def join_kernel(*refs):
    blocks, joined = refs[:4], refs[4]
    rows = joined.shape[0] // 4
    for k, block in enumerate(blocks):
        joined[k * rows : (k + 1) * rows, :] = block[:rows, :]


def attention_kernel(*refs):
    blocks, sibling = refs[:4], refs[4]
    sent, kept, key_all, value_all, query_all = refs[5:]
    rows = sent.shape[0]
    half = rows // 2
    for k in range(4):
        here, there = slice(k * half, (k + 1) * half), slice((4 + k) * half, (5 + k) * half)
        key_all[here, :] = blocks[k][:half, :]
        value_all[here, :] = blocks[k][half:rows, :]
        key_all[there, :] = sibling[k * rows : k * rows + half, :]
        value_all[there, :] = sibling[k * rows + half : (k + 1) * rows, :]
    zh, _ = bits()
    x = lax.axis_index("wt")
    for k in range(2):
        for part in range(2):
            at = rows + flip(x, part == 0) * half
            to = (part * 2 + flip(zh, 1 - k)) * half
            query_all[pl.ds(pl.multiple_of(to, 16), half), :] = blocks[k][
                pl.ds(pl.multiple_of(at, 16), half), :
            ]
    for h in range(sent.shape[1] // HEAD_DIM):
        columns = slice(h * HEAD_DIM, (h + 1) * HEAD_DIM)
        scores = lax.dot_general(
            query_all[:, columns],
            key_all[:, columns],
            (((1,), (1,)), ((), ())),
            preferred_element_type=jnp.float32,
        )
        peak = jnp.max(scores, axis=1, keepdims=True)
        weights = jnp.exp2((scores - peak) * (LOG2_E * HEAD_DIM ** (-0.5)))
        total = jnp.sum(weights, axis=1, keepdims=True)
        result = jnp.dot(
            weights.astype(jnp.bfloat16), value_all[:, columns], preferred_element_type=jnp.float32
        )
        result = (result / total).astype(sent.dtype)
        sent[:, columns] = result[:rows]
        kept[:, columns] = result[rows:]


def multiply(shards, weight, weight_c, held):
    rows = shards[0].shape[0]
    zh, zl = bits()
    core = lax.axis_index("head")
    for m, shard in enumerate(shards):
        held[m * rows : (m + 1) * rows, :] = shard[...]
    total = None
    for other, block in enumerate((weight, weight_c)):
        low = lax.rem(flip(core, other) + zl, 2)
        left = jnp.concatenate(
            [
                held[pl.ds(pl.multiple_of((2 * flip(zh, high) + low) * rows, 16), rows), :]
                for high in range(2)
            ],
            axis=1,
        )
        term = jnp.dot(left, block[...], preferred_element_type=jnp.float32)
        total = term if total is None else total + term
    return total


def project_kernel(kept, *refs):
    shards, (weight, weight_c, out0, out1, held) = refs[:4], refs[4:]
    total = multiply(shards, weight, weight_c, held)
    half = out0.shape[0]
    x = lax.axis_index("wt")
    for low in range(2):
        part = total[low * half : (low + 1) * half].astype(out0.dtype)
        first = flip(x, low) == 1 - kept

        @pl.when(first)
        def _():
            out0[...] = part

        @pl.when(jnp.logical_not(first))
        def _():
            out1[...] = part


def add_kernel(kept, arrived, out):
    out[...] = (kept[...] + arrived[...].astype(jnp.float32)).astype(out.dtype)


def rest_kernel(flags, hidden, cached, out):
    total = hidden[...]
    for layer in range(cached.shape[0]):
        total = total + flags[layer].astype(jnp.float32) * cached[layer]
    out[...] = total


def final_kernel(piece, owned, gate, resting, *refs):
    mixed, fresh, mixed_part, fresh_part, sems = refs[-5:]
    half = owned.shape[0]
    zh, _ = bits()
    rows = pl.ds(pl.multiple_of(flip(zh, piece) * half, 16), half)
    delta = owned[...].astype(jnp.float32) * gate[...]
    fresh_part[...] = delta
    copy_fresh = pltpu.make_async_copy(fresh_part, fresh.at[rows, :], sems.at[0])
    copy_fresh.start()
    mixed_part[...] = resting[rows, :] + delta
    copy_mixed = pltpu.make_async_copy(mixed_part, mixed.at[rows, :], sems.at[1])
    copy_mixed.start()
    copy_fresh.wait()
    copy_mixed.wait()


def along(shard, m):
    return lax.ppermute(shard, "seq", [(z, z ^ m) for z in range(4)])


def call(
    kernel,
    args,
    outs,
    scratch=(),
    space=pltpu.VMEM,
    out_space=pltpu.VMEM,
    flops=0,
    vmem=VMEM_BYTES,
):
    spaces = [pltpu.SMEM if arg.dtype == jnp.int32 else space for arg in args]
    return pl.pallas_call(
        kernel,
        in_specs=[pl.BlockSpec(memory_space=place) for place in spaces],
        out_specs=[pl.BlockSpec(memory_space=out_space)] * len(outs),
        out_shape=[jax.ShapeDtypeStruct(shape, dtype) for shape, dtype in outs],
        scratch_shapes=list(scratch),
        compiler_params=pltpu.CompilerParams(vmem_limit_bytes=vmem),
        cost_estimate=pl.CostEstimate(flops=flops, bytes_accessed=0, transcendentals=0),
    )(*args)


def local_heads(
    queries,
    key_vectors,
    value_vectors,
    out_weight,
    gate_values,
    hidden_state,
    cached_deltas,
    skip_flags,
):
    rows, features = queries.shape
    width = features // 2
    depth, columns = out_weight.shape
    swap = [(0, 1), (1, 0)]
    bf16 = jnp.bfloat16

    packed = call(
        pack_kernel,
        (queries, key_vectors, value_vectors),
        [((2 * rows, width), bf16)] * 2 + [((rows, width), bf16)] * 2,
        [pltpu.SemaphoreType.DMA((10,))],
        space=pl.ANY,
        vmem=PACK_BYTES,
    )
    late_weight, _ = lax.optimization_barrier((out_weight, packed[0]))
    weight_c = lax.ppermute(late_weight, "head", swap)
    moved = []
    for k in range(4):
        k1, k0 = k // 2, 1 - k % 2
        pairs = []
        for zz in range(4):
            for cc in range(2):
                to_z = 2 * ((zz // 2) ^ k0) + cc
                pairs.append((zz * 2 + cc, to_z * 2 + ((zz % 2) ^ k1)))
        moved.append(lax.ppermute(packed[k], ("seq", "head"), pairs))
    (joined,) = call(join_kernel, moved, [((4 * rows, width), bf16)])
    sibling = lax.ppermute(joined, "head", swap)
    sibling, _ = lax.optimization_barrier((sibling, weight_c))
    parts = call(
        attention_kernel,
        moved + [sibling],
        [((rows, width), bf16)] * 2,
        [
            pltpu.VMEM((4 * rows, width), bf16),
            pltpu.VMEM((4 * rows, width), bf16),
            pltpu.VMEM((2 * rows, width), bf16),
        ],
        flops=4 * (2 * rows) * (4 * rows) * width,
    )

    half = rows // 2
    flops = 4 * rows * depth * columns
    sent, kept = (
        call(
            functools.partial(project_kernel, i),
            [part] + [along(part, m) for m in (1, 2, 3)] + [out_weight, weight_c],
            [((half, columns), dtype)] * 2,
            [pltpu.VMEM((4 * rows, width), bf16)],
            flops=effort * flops,
        )
        for i, (part, dtype, effort) in enumerate(((parts[0], bf16, 1), (parts[1], jnp.float32, 8)))
    )

    owned = []
    for p in range(2):
        arrived = lax.ppermute(sent[p], "wt", swap)
        (summed,) = call(add_kernel, (kept[p], arrived), [((half, columns), bf16)])
        pairs = []
        for zz in range(4):
            for xx in range(2):
                for cc in range(2):
                    to = ((cc + 2 * (p ^ xx)) * 2 + zz // 2) * 2 + zz % 2
                    pairs.append(((zz * 2 + xx) * 2 + cc, to))
        owned.append(lax.ppermute(summed, ("seq", "wt", "head"), pairs))
    (resting,) = call(
        rest_kernel, (skip_flags, hidden_state, cached_deltas), [((rows, columns), jnp.float32)]
    )
    gate = gate_values[None, :]
    results = ()
    for p, part in enumerate(owned):
        results = pl.pallas_call(
            functools.partial(final_kernel, p),
            in_specs=[pl.BlockSpec(memory_space=pltpu.VMEM)] * 3
            + [pl.BlockSpec(memory_space=pl.ANY)] * len(results),
            out_specs=[pl.BlockSpec(memory_space=pl.ANY)] * 2,
            out_shape=[jax.ShapeDtypeStruct((rows, columns), jnp.float32)] * 2,
            scratch_shapes=[pltpu.VMEM((half, columns), jnp.float32)] * 2
            + [pltpu.SemaphoreType.DMA((2,))],
            input_output_aliases={3 + i: i for i in range(len(results))},
            compiler_params=pltpu.CompilerParams(vmem_limit_bytes=VMEM_BYTES),
            cost_estimate=pl.CostEstimate(flops=0, bytes_accessed=0, transcendentals=0),
        )(part, gate, resting, *results)
    return tuple(results)


def solution(mesh):
    placed = (
        P(("groups", "seq"), ("wt", "head")),
        P(("groups", "seq"), ("wt", "head")),
        P(("groups", "seq"), ("wt", "head")),
        P(("wt", "head"), "seq"),
        P(("groups", "wt", "head")),
        P(("groups", "seq"), ("wt", "head")),
        P(None, ("groups", "seq"), ("wt", "head")),
        P("groups"),
    )

    def local(*args):
        sizes = tuple(mesh.shape[name] for name in ("seq", "wt", "head"))
        rows, features = args[0].shape
        if sizes == (4, 2, 2) and rows % 32 == 0 and features % (2 * HEAD_DIM) == 0:
            return local_heads(*args)
        return local_general(*args)

    return jax.shard_map(
        local,
        mesh=mesh,
        in_specs=placed,
        out_specs=(P(("groups", "seq"), ("wt", "head")), P(("groups", "seq"), ("wt", "head"))),
        check_vma=False,
    )
```

```python
import functools

import jax
import jax.numpy as jnp
from jax import lax
from jax.experimental import pallas as pl
from jax.experimental.pallas import tpu as pltpu
from jax.sharding import PartitionSpec as P

HEAD_DIM = 128
VMEM_BYTES = 48 * 1024 * 1024
PACK_BYTES = 53 * 1024 * 1024 + 128 * 1024
LOG2_E = 1.4426950408889634


def attend(state_in, key_rows, value_rows, query_heads, score_scale):
    key_count = key_rows.shape[0]
    head_count = query_heads.shape[1]
    blocks = -(-key_count // 1024)
    while key_count % blocks:
        blocks = blocks + 1
    block_size = key_count // blocks

    def one_block(block_index, state_now):
        row_peak, row_total, weighted = state_now
        start_row = block_index * block_size
        key_block = lax.dynamic_slice_in_dim(key_rows, start_row, block_size, 0)
        value_block = lax.dynamic_slice_in_dim(value_rows, start_row, block_size, 0)
        key_heads = key_block.reshape(block_size, head_count, HEAD_DIM)
        value_heads = value_block.reshape(block_size, head_count, HEAD_DIM)
        scores = (
            jnp.einsum("ihd,jhd->hij", query_heads, key_heads, preferred_element_type=jnp.float32)
            * score_scale
        )
        new_peak = jnp.maximum(row_peak, jnp.max(scores, axis=2))
        exp_scores = jnp.exp(scores - new_peak[:, :, None])
        rescale = jnp.exp(row_peak - new_peak)
        row_total = row_total * rescale + jnp.sum(exp_scores, axis=2)
        weighted = weighted * rescale[:, :, None] + jnp.einsum(
            "hij,jhd->hid",
            exp_scores.astype(jnp.bfloat16),
            value_heads,
            preferred_element_type=jnp.float32,
        )
        return (new_peak, row_total, weighted)

    return lax.fori_loop(0, blocks, one_block, state_in)


def finish(state_out, row_count):
    row_peak, row_total, weighted = state_out
    normed = weighted / row_total[:, :, None]
    return normed.transpose(1, 0, 2).reshape(row_count, -1).astype(jnp.bfloat16)


def local_general(
    queries,
    key_vectors,
    value_vectors,
    out_weight,
    gate_values,
    hidden_state,
    cached_deltas,
    skip_flags,
):
    row_count = queries.shape[0]
    head_count = queries.shape[1] // HEAD_DIM
    score_scale = HEAD_DIM ** (-0.5)
    query_heads = queries.reshape(row_count, head_count, HEAD_DIM)
    start_state = (
        jnp.full((head_count, row_count), -1e30, jnp.float32),
        jnp.zeros((head_count, row_count), jnp.float32),
        jnp.zeros((head_count, row_count, HEAD_DIM), jnp.float32),
    )
    gathered_keys, gathered_values, gathered_weight = (
        lax.all_gather(key_vectors, "seq", axis=0, tiled=True),
        lax.all_gather(value_vectors, "seq", axis=0, tiled=True),
        lax.all_gather(out_weight, "seq", axis=1, tiled=True),
    )
    final_state = attend(start_state, gathered_keys, gathered_values, query_heads, score_scale)
    attention_out = finish(final_state, row_count)
    partial_sums = jnp.dot(attention_out, gathered_weight, preferred_element_type=jnp.float32)
    head_total = lax.psum_scatter(
        partial_sums.astype(jnp.bfloat16), ("wt", "head"), scatter_dimension=1, tiled=True
    ).astype(jnp.float32)
    fresh_delta = head_total * gate_values[None, :]
    kept_deltas = jnp.sum(skip_flags.astype(jnp.float32)[:, None, None] * cached_deltas, axis=0)
    mixed_state = hidden_state + kept_deltas + fresh_delta
    return (mixed_state, fresh_delta)


def bits():
    z = lax.axis_index("seq")
    return lax.div(z, 2), lax.rem(z, 2)


def flip(bit, value):
    return 1 - bit if value else bit


def pack_kernel(queries, keys, values, *refs):
    outs, sems = refs[:4], refs[4]
    rows, width = queries.shape[0], outs[0].shape[1]
    half = rows // 2
    zh, zl = bits()
    copies = []
    for k in range(4):
        part = pl.ds(pl.multiple_of(flip(zl, k // 2) * half, 16), half)
        columns = pl.ds(pl.multiple_of(flip(zh, 1 - k % 2) * width, 128), width)
        moves = [
            (keys.at[part, columns], outs[k].at[pl.ds(0, half), :]),
            (values.at[part, columns], outs[k].at[pl.ds(half, half), :]),
        ]
        if k < 2:
            moves.append((queries.at[:, columns], outs[k].at[pl.ds(rows, rows), :]))
        for start, end in moves:
            copies.append(pltpu.make_async_copy(start, end, sems.at[len(copies)]))
    for copy in copies:
        copy.start()
    for copy in copies:
        copy.wait()


def join_kernel(*refs):
    blocks, joined = refs[:4], refs[4]
    rows = joined.shape[0] // 4
    for k, block in enumerate(blocks):
        joined[k * rows : (k + 1) * rows, :] = block[:rows, :]


def attention_kernel(*refs):
    blocks, sibling = refs[:4], refs[4]
    sent, kept, key_all, value_all, query_all = refs[5:]
    rows = sent.shape[0]
    half = rows // 2
    for k in range(4):
        here, there = slice(k * half, (k + 1) * half), slice((4 + k) * half, (5 + k) * half)
        key_all[here, :] = blocks[k][:half, :]
        value_all[here, :] = blocks[k][half:rows, :]
        key_all[there, :] = sibling[k * rows : k * rows + half, :]
        value_all[there, :] = sibling[k * rows + half : (k + 1) * rows, :]
    zh, _ = bits()
    x = lax.axis_index("wt")
    for k in range(2):
        for part in range(2):
            at = rows + flip(x, part == 0) * half
            to = (part * 2 + flip(zh, 1 - k)) * half
            query_all[pl.ds(pl.multiple_of(to, 16), half), :] = blocks[k][
                pl.ds(pl.multiple_of(at, 16), half), :
            ]
    for h in range(sent.shape[1] // HEAD_DIM):
        columns = slice(h * HEAD_DIM, (h + 1) * HEAD_DIM)
        scores = lax.dot_general(
            query_all[:, columns],
            key_all[:, columns],
            (((1,), (1,)), ((), ())),
            preferred_element_type=jnp.float32,
        )
        peak = jnp.max(scores, axis=1, keepdims=True)
        weights = jnp.exp2((scores - peak) * (LOG2_E * HEAD_DIM ** (-0.5)))
        total = jnp.sum(weights, axis=1, keepdims=True)
        result = jnp.dot(
            weights.astype(jnp.bfloat16), value_all[:, columns], preferred_element_type=jnp.float32
        )
        result = (result / total).astype(sent.dtype)
        sent[:, columns] = result[:rows]
        kept[:, columns] = result[rows:]


def multiply(shards, weight, weight_c, held):
    rows = shards[0].shape[0]
    zh, zl = bits()
    core = lax.axis_index("head")
    for m, shard in enumerate(shards):
        held[m * rows : (m + 1) * rows, :] = shard[...]
    total = None
    for other, block in enumerate((weight, weight_c)):
        low = lax.rem(flip(core, other) + zl, 2)
        left = jnp.concatenate(
            [
                held[pl.ds(pl.multiple_of((2 * flip(zh, high) + low) * rows, 16), rows), :]
                for high in range(2)
            ],
            axis=1,
        )
        term = jnp.dot(left, block[...], preferred_element_type=jnp.float32)
        total = term if total is None else total + term
    return total


def project_kernel(kept, *refs):
    shards, (weight, weight_c, out0, out1, held) = refs[:4], refs[4:]
    total = multiply(shards, weight, weight_c, held)
    half = out0.shape[0]
    x = lax.axis_index("wt")
    for low in range(2):
        part = total[low * half : (low + 1) * half].astype(out0.dtype)
        first = flip(x, low) == 1 - kept

        @pl.when(first)
        def _():
            out0[...] = part

        @pl.when(jnp.logical_not(first))
        def _():
            out1[...] = part


def add_kernel(kept, arrived, out):
    out[...] = (kept[...] + arrived[...].astype(jnp.float32)).astype(out.dtype)


def rest_kernel(flags, hidden, cached, out):
    total = hidden[...]
    for layer in range(cached.shape[0]):
        total = total + flags[layer].astype(jnp.float32) * cached[layer]
    out[...] = total


def final_kernel(piece, owned, gate, resting, *refs):
    mixed, fresh, mixed_part, fresh_part, sems = refs[-5:]
    half = owned.shape[0]
    zh, _ = bits()
    rows = pl.ds(pl.multiple_of(flip(zh, piece) * half, 16), half)
    delta = owned[...].astype(jnp.float32) * gate[...]
    fresh_part[...] = delta
    copy_fresh = pltpu.make_async_copy(fresh_part, fresh.at[rows, :], sems.at[0])
    copy_fresh.start()
    mixed_part[...] = resting[rows, :] + delta
    copy_mixed = pltpu.make_async_copy(mixed_part, mixed.at[rows, :], sems.at[1])
    copy_mixed.start()
    copy_fresh.wait()
    copy_mixed.wait()


def along(shard, m):
    return lax.ppermute(shard, "seq", [(z, z ^ m) for z in range(4)])


def call(
    kernel,
    args,
    outs,
    scratch=(),
    space=pltpu.VMEM,
    out_space=pltpu.VMEM,
    flops=0,
    vmem=VMEM_BYTES,
):
    spaces = [pltpu.SMEM if arg.dtype == jnp.int32 else space for arg in args]
    return pl.pallas_call(
        kernel,
        in_specs=[pl.BlockSpec(memory_space=place) for place in spaces],
        out_specs=[pl.BlockSpec(memory_space=out_space)] * len(outs),
        out_shape=[jax.ShapeDtypeStruct(shape, dtype) for shape, dtype in outs],
        scratch_shapes=list(scratch),
        compiler_params=pltpu.CompilerParams(vmem_limit_bytes=vmem),
        cost_estimate=pl.CostEstimate(flops=flops, bytes_accessed=0, transcendentals=0),
    )(*args)


def local_heads(
    queries,
    key_vectors,
    value_vectors,
    out_weight,
    gate_values,
    hidden_state,
    cached_deltas,
    skip_flags,
):
    rows, features = queries.shape
    width = features // 2
    depth, columns = out_weight.shape
    swap = [(0, 1), (1, 0)]
    bf16 = jnp.bfloat16

    packed = call(
        pack_kernel,
        (queries, key_vectors, value_vectors),
        [((2 * rows, width), bf16)] * 2 + [((rows, width), bf16)] * 2,
        [pltpu.SemaphoreType.DMA((10,))],
        space=pl.ANY,
        vmem=PACK_BYTES,
    )
    late_weight, _ = lax.optimization_barrier((out_weight, packed[0]))
    weight_c = lax.ppermute(late_weight, "head", swap)
    packed = list(packed)
    packed[1], packed[3], _ = lax.optimization_barrier((packed[1], packed[3], weight_c))
    moved = []
    for k in range(4):
        k1, k0 = k // 2, 1 - k % 2
        pairs = []
        for zz in range(4):
            for cc in range(2):
                to_z = 2 * ((zz // 2) ^ k0) + cc
                pairs.append((zz * 2 + cc, to_z * 2 + ((zz % 2) ^ k1)))
        moved.append(lax.ppermute(packed[k], ("seq", "head"), pairs))
    (joined,) = call(join_kernel, moved, [((4 * rows, width), bf16)])
    sibling = lax.ppermute(joined, "head", swap)
    sibling, _ = lax.optimization_barrier((sibling, weight_c))
    parts = call(
        attention_kernel,
        moved + [sibling],
        [((rows, width), bf16)] * 2,
        [
            pltpu.VMEM((4 * rows, width), bf16),
            pltpu.VMEM((4 * rows, width), bf16),
            pltpu.VMEM((2 * rows, width), bf16),
        ],
        flops=4 * (2 * rows) * (4 * rows) * width,
    )

    half = rows // 2
    flops = 4 * rows * depth * columns
    sent, kept = (
        call(
            functools.partial(project_kernel, i),
            [part] + [along(part, m) for m in (1, 2, 3)] + [out_weight, weight_c],
            [((half, columns), dtype)] * 2,
            [pltpu.VMEM((4 * rows, width), bf16)],
            flops=effort * flops,
        )
        for i, (part, dtype, effort) in enumerate(((parts[0], bf16, 1), (parts[1], jnp.float32, 8)))
    )

    owned = []
    for p in range(2):
        arrived = lax.ppermute(sent[p], "wt", swap)
        (summed,) = call(add_kernel, (kept[p], arrived), [((half, columns), bf16)])
        pairs = []
        for zz in range(4):
            for xx in range(2):
                for cc in range(2):
                    to = ((cc + 2 * (p ^ xx)) * 2 + zz // 2) * 2 + zz % 2
                    pairs.append(((zz * 2 + xx) * 2 + cc, to))
        owned.append(lax.ppermute(summed, ("seq", "wt", "head"), pairs))
    (resting,) = call(
        rest_kernel, (skip_flags, hidden_state, cached_deltas), [((rows, columns), jnp.float32)]
    )
    gate = gate_values[None, :]
    results = ()
    for p, part in enumerate(owned):
        results = pl.pallas_call(
            functools.partial(final_kernel, p),
            in_specs=[pl.BlockSpec(memory_space=pltpu.VMEM)] * 3
            + [pl.BlockSpec(memory_space=pl.ANY)] * len(results),
            out_specs=[pl.BlockSpec(memory_space=pl.ANY)] * 2,
            out_shape=[jax.ShapeDtypeStruct((rows, columns), jnp.float32)] * 2,
            scratch_shapes=[pltpu.VMEM((half, columns), jnp.float32)] * 2
            + [pltpu.SemaphoreType.DMA((2,))],
            input_output_aliases={3 + i: i for i in range(len(results))},
            compiler_params=pltpu.CompilerParams(vmem_limit_bytes=VMEM_BYTES),
            cost_estimate=pl.CostEstimate(flops=0, bytes_accessed=0, transcendentals=0),
        )(part, gate, resting, *results)
    return tuple(results)


def solution(mesh):
    placed = (
        P(("groups", "seq"), ("wt", "head")),
        P(("groups", "seq"), ("wt", "head")),
        P(("groups", "seq"), ("wt", "head")),
        P(("wt", "head"), "seq"),
        P(("groups", "wt", "head")),
        P(("groups", "seq"), ("wt", "head")),
        P(None, ("groups", "seq"), ("wt", "head")),
        P("groups"),
    )

    def local(*args):
        sizes = tuple(mesh.shape[name] for name in ("seq", "wt", "head"))
        rows, features = args[0].shape
        if sizes == (4, 2, 2) and rows % 32 == 0 and features % (2 * HEAD_DIM) == 0:
            return local_heads(*args)
        return local_general(*args)

    return jax.shard_map(
        local,
        mesh=mesh,
        in_specs=placed,
        out_specs=(P(("groups", "seq"), ("wt", "head")), P(("groups", "seq"), ("wt", "head"))),
        check_vma=False,
    )
```

```python
import functools

import jax
import jax.numpy as jnp
from jax import lax
from jax.experimental import pallas as pl
from jax.experimental.pallas import tpu as pltpu
from jax.sharding import PartitionSpec as P

HEAD_DIM = 128
VMEM_BYTES = 48 * 1024 * 1024
PACK_BYTES = 53 * 1024 * 1024 + 128 * 1024
LOG2_E = 1.4426950408889634


def attend(state_in, key_rows, value_rows, query_heads, score_scale):
    key_count = key_rows.shape[0]
    head_count = query_heads.shape[1]
    blocks = -(-key_count // 1024)
    while key_count % blocks:
        blocks = blocks + 1
    block_size = key_count // blocks

    def one_block(block_index, state_now):
        row_peak, row_total, weighted = state_now
        start_row = block_index * block_size
        key_block = lax.dynamic_slice_in_dim(key_rows, start_row, block_size, 0)
        value_block = lax.dynamic_slice_in_dim(value_rows, start_row, block_size, 0)
        key_heads = key_block.reshape(block_size, head_count, HEAD_DIM)
        value_heads = value_block.reshape(block_size, head_count, HEAD_DIM)
        scores = (
            jnp.einsum("ihd,jhd->hij", query_heads, key_heads, preferred_element_type=jnp.float32)
            * score_scale
        )
        new_peak = jnp.maximum(row_peak, jnp.max(scores, axis=2))
        exp_scores = jnp.exp(scores - new_peak[:, :, None])
        rescale = jnp.exp(row_peak - new_peak)
        row_total = row_total * rescale + jnp.sum(exp_scores, axis=2)
        weighted = weighted * rescale[:, :, None] + jnp.einsum(
            "hij,jhd->hid",
            exp_scores.astype(jnp.bfloat16),
            value_heads,
            preferred_element_type=jnp.float32,
        )
        return (new_peak, row_total, weighted)

    return lax.fori_loop(0, blocks, one_block, state_in)


def finish(state_out, row_count):
    row_peak, row_total, weighted = state_out
    normed = weighted / row_total[:, :, None]
    return normed.transpose(1, 0, 2).reshape(row_count, -1).astype(jnp.bfloat16)


def local_general(
    queries,
    key_vectors,
    value_vectors,
    out_weight,
    gate_values,
    hidden_state,
    cached_deltas,
    skip_flags,
):
    row_count = queries.shape[0]
    head_count = queries.shape[1] // HEAD_DIM
    score_scale = HEAD_DIM ** (-0.5)
    query_heads = queries.reshape(row_count, head_count, HEAD_DIM)
    start_state = (
        jnp.full((head_count, row_count), -1e30, jnp.float32),
        jnp.zeros((head_count, row_count), jnp.float32),
        jnp.zeros((head_count, row_count, HEAD_DIM), jnp.float32),
    )
    gathered_keys, gathered_values, gathered_weight = (
        lax.all_gather(key_vectors, "seq", axis=0, tiled=True),
        lax.all_gather(value_vectors, "seq", axis=0, tiled=True),
        lax.all_gather(out_weight, "seq", axis=1, tiled=True),
    )
    final_state = attend(start_state, gathered_keys, gathered_values, query_heads, score_scale)
    attention_out = finish(final_state, row_count)
    partial_sums = jnp.dot(attention_out, gathered_weight, preferred_element_type=jnp.float32)
    head_total = lax.psum_scatter(
        partial_sums.astype(jnp.bfloat16), ("wt", "head"), scatter_dimension=1, tiled=True
    ).astype(jnp.float32)
    fresh_delta = head_total * gate_values[None, :]
    kept_deltas = jnp.sum(skip_flags.astype(jnp.float32)[:, None, None] * cached_deltas, axis=0)
    mixed_state = hidden_state + kept_deltas + fresh_delta
    return (mixed_state, fresh_delta)


def bits():
    z = lax.axis_index("seq")
    return lax.div(z, 2), lax.rem(z, 2)


def flip(bit, value):
    return 1 - bit if value else bit


def pack_kernel(queries, keys, values, *refs):
    outs, sems = refs[:4], refs[4]
    rows, width = queries.shape[0], outs[0].shape[1]
    half = rows // 2
    zh, zl = bits()
    copies = []
    for k in range(4):
        part = pl.ds(pl.multiple_of(flip(zl, k // 2) * half, 16), half)
        columns = pl.ds(pl.multiple_of(flip(zh, 1 - k % 2) * width, 128), width)
        moves = [
            (keys.at[part, columns], outs[k].at[pl.ds(0, half), :]),
            (values.at[part, columns], outs[k].at[pl.ds(half, half), :]),
        ]
        if k < 2:
            moves.append((queries.at[:, columns], outs[k].at[pl.ds(rows, rows), :]))
        for start, end in moves:
            copies.append(pltpu.make_async_copy(start, end, sems.at[len(copies)]))
    for copy in copies:
        copy.start()
    for copy in copies:
        copy.wait()


def join_kernel(*refs):
    blocks, joined = refs[:4], refs[4]
    rows = joined.shape[0] // 4
    for k, block in enumerate(blocks):
        joined[k * rows : (k + 1) * rows, :] = block[:rows, :]


def attention_kernel(*refs):
    blocks, sibling = refs[:4], refs[4]
    sent, kept, key_all, value_all, query_all = refs[5:]
    rows = sent.shape[0]
    half = rows // 2
    for k in range(4):
        here, there = slice(k * half, (k + 1) * half), slice((4 + k) * half, (5 + k) * half)
        key_all[here, :] = blocks[k][:half, :]
        value_all[here, :] = blocks[k][half:rows, :]
        key_all[there, :] = sibling[k * rows : k * rows + half, :]
        value_all[there, :] = sibling[k * rows + half : (k + 1) * rows, :]
    zh, _ = bits()
    x = lax.axis_index("wt")
    for k in range(2):
        for part in range(2):
            at = rows + flip(x, part == 0) * half
            to = (part * 2 + flip(zh, 1 - k)) * half
            query_all[pl.ds(pl.multiple_of(to, 16), half), :] = blocks[k][
                pl.ds(pl.multiple_of(at, 16), half), :
            ]
    for h in range(sent.shape[1] // HEAD_DIM):
        columns = slice(h * HEAD_DIM, (h + 1) * HEAD_DIM)
        scores = lax.dot_general(
            query_all[:, columns],
            key_all[:, columns],
            (((1,), (1,)), ((), ())),
            preferred_element_type=jnp.float32,
        )
        peak = jnp.max(scores, axis=1, keepdims=True)
        weights = jnp.exp2((scores - peak) * (LOG2_E * HEAD_DIM ** (-0.5)))
        total = jnp.sum(weights, axis=1, keepdims=True)
        result = jnp.dot(
            weights.astype(jnp.bfloat16), value_all[:, columns], preferred_element_type=jnp.float32
        )
        result = (result / total).astype(sent.dtype)
        sent[:, columns] = result[:rows]
        kept[:, columns] = result[rows:]


def multiply(shards, weight, weight_c, held):
    rows = shards[0].shape[0]
    zh, zl = bits()
    core = lax.axis_index("head")
    for m, shard in enumerate(shards):
        held[m * rows : (m + 1) * rows, :] = shard[...]
    total = None
    for other, block in enumerate((weight, weight_c)):
        low = lax.rem(flip(core, other) + zl, 2)
        left = jnp.concatenate(
            [
                held[pl.ds(pl.multiple_of((2 * flip(zh, high) + low) * rows, 16), rows), :]
                for high in range(2)
            ],
            axis=1,
        )
        term = jnp.dot(left, block[...], preferred_element_type=jnp.float32)
        total = term if total is None else total + term
    return total


def project_kernel(kept, *refs):
    shards, (weight, weight_c, out0, out1, held) = refs[:4], refs[4:]
    total = multiply(shards, weight, weight_c, held)
    half = out0.shape[0]
    _, zl = bits()
    side = lax.rem(lax.axis_index("wt") + zl, 2)
    for high in range(2):
        part = total[high * half : (high + 1) * half].astype(out0.dtype)
        first = flip(side, high) == 1 - kept

        @pl.when(first)
        def _():
            out0[...] = part

        @pl.when(jnp.logical_not(first))
        def _():
            out1[...] = part


def add_kernel(kept, arrived, out):
    out[...] = (kept[...] + arrived[...].astype(jnp.float32)).astype(out.dtype)


def rest_kernel(flags, hidden, cached, out):
    total = hidden[...]
    for layer in range(cached.shape[0]):
        total = total + flags[layer].astype(jnp.float32) * cached[layer]
    out[...] = total


def final_kernel(piece, owned, gate, resting, *refs):
    mixed, fresh, mixed_part, fresh_part, sems = refs[-5:]
    half = owned.shape[0]
    zh, _ = bits()
    side = lax.rem(zh + lax.axis_index("head"), 2)
    rows = pl.ds(pl.multiple_of(flip(side, piece) * half, 16), half)
    delta = owned[...].astype(jnp.float32) * gate[...]
    fresh_part[...] = delta
    copy_fresh = pltpu.make_async_copy(fresh_part, fresh.at[rows, :], sems.at[0])
    copy_fresh.start()
    mixed_part[...] = resting[rows, :] + delta
    copy_mixed = pltpu.make_async_copy(mixed_part, mixed.at[rows, :], sems.at[1])
    copy_mixed.start()
    copy_fresh.wait()
    copy_mixed.wait()


def along(shard, m):
    return lax.ppermute(shard, "seq", [(z, z ^ m) for z in range(4)])


def call(
    kernel,
    args,
    outs,
    scratch=(),
    space=pltpu.VMEM,
    out_space=pltpu.VMEM,
    flops=0,
    vmem=VMEM_BYTES,
):
    spaces = [pltpu.SMEM if arg.dtype == jnp.int32 else space for arg in args]
    return pl.pallas_call(
        kernel,
        in_specs=[pl.BlockSpec(memory_space=place) for place in spaces],
        out_specs=[pl.BlockSpec(memory_space=out_space)] * len(outs),
        out_shape=[jax.ShapeDtypeStruct(shape, dtype) for shape, dtype in outs],
        scratch_shapes=list(scratch),
        compiler_params=pltpu.CompilerParams(vmem_limit_bytes=vmem),
        cost_estimate=pl.CostEstimate(flops=flops, bytes_accessed=0, transcendentals=0),
    )(*args)


def local_heads(
    queries,
    key_vectors,
    value_vectors,
    out_weight,
    gate_values,
    hidden_state,
    cached_deltas,
    skip_flags,
):
    rows, features = queries.shape
    width = features // 2
    depth, columns = out_weight.shape
    swap = [(0, 1), (1, 0)]
    bf16 = jnp.bfloat16

    packed = call(
        pack_kernel,
        (queries, key_vectors, value_vectors),
        [((2 * rows, width), bf16)] * 2 + [((rows, width), bf16)] * 2,
        [pltpu.SemaphoreType.DMA((10,))],
        space=pl.ANY,
        vmem=PACK_BYTES,
    )
    late_weight, _ = lax.optimization_barrier((out_weight, packed[0]))
    weight_c = lax.ppermute(late_weight, "head", swap)
    moved = []
    for k in range(4):
        k1, k0 = k // 2, 1 - k % 2
        pairs = []
        for zz in range(4):
            for cc in range(2):
                to_z = 2 * ((zz // 2) ^ k0) + cc
                pairs.append((zz * 2 + cc, to_z * 2 + ((zz % 2) ^ k1)))
        moved.append(lax.ppermute(packed[k], ("seq", "head"), pairs))
    (joined,) = call(join_kernel, moved, [((4 * rows, width), bf16)])
    sibling = lax.ppermute(joined, "head", swap)
    sibling, _ = lax.optimization_barrier((sibling, weight_c))
    parts = call(
        attention_kernel,
        moved + [sibling],
        [((rows, width), bf16)] * 2,
        [
            pltpu.VMEM((4 * rows, width), bf16),
            pltpu.VMEM((4 * rows, width), bf16),
            pltpu.VMEM((2 * rows, width), bf16),
        ],
        flops=4 * (2 * rows) * (4 * rows) * width,
    )

    half = rows // 2
    flops = 4 * rows * depth * columns
    sent, kept = (
        call(
            functools.partial(project_kernel, i),
            [part] + [along(part, m) for m in (1, 2, 3)] + [out_weight, weight_c],
            [((half, columns), dtype)] * 2,
            [pltpu.VMEM((4 * rows, width), bf16)],
            flops=effort * flops,
        )
        for i, (part, dtype, effort) in enumerate(((parts[0], bf16, 1), (parts[1], jnp.float32, 8)))
    )

    owned = []
    for p in range(2):
        arrived = lax.ppermute(sent[p], "wt", swap)
        (summed,) = call(add_kernel, (kept[p], arrived), [((half, columns), bf16)])
        pairs = []
        for zz in range(4):
            for xx in range(2):
                for cc in range(2):
                    to = ((cc + 2 * (p ^ xx ^ (zz % 2))) * 2 + zz // 2) * 2 + zz % 2
                    pairs.append(((zz * 2 + xx) * 2 + cc, to))
        owned.append(lax.ppermute(summed, ("seq", "wt", "head"), pairs))
    (resting,) = call(
        rest_kernel, (skip_flags, hidden_state, cached_deltas), [((rows, columns), jnp.float32)]
    )
    gate = gate_values[None, :]
    results = ()
    for p, part in enumerate(owned):
        results = pl.pallas_call(
            functools.partial(final_kernel, p),
            in_specs=[pl.BlockSpec(memory_space=pltpu.VMEM)] * 3
            + [pl.BlockSpec(memory_space=pl.ANY)] * len(results),
            out_specs=[pl.BlockSpec(memory_space=pl.ANY)] * 2,
            out_shape=[jax.ShapeDtypeStruct((rows, columns), jnp.float32)] * 2,
            scratch_shapes=[pltpu.VMEM((half, columns), jnp.float32)] * 2
            + [pltpu.SemaphoreType.DMA((2,))],
            input_output_aliases={3 + i: i for i in range(len(results))},
            compiler_params=pltpu.CompilerParams(vmem_limit_bytes=VMEM_BYTES),
            cost_estimate=pl.CostEstimate(flops=0, bytes_accessed=0, transcendentals=0),
        )(part, gate, resting, *results)
    return tuple(results)


def solution(mesh):
    placed = (
        P(("groups", "seq"), ("wt", "head")),
        P(("groups", "seq"), ("wt", "head")),
        P(("groups", "seq"), ("wt", "head")),
        P(("wt", "head"), "seq"),
        P(("groups", "wt", "head")),
        P(("groups", "seq"), ("wt", "head")),
        P(None, ("groups", "seq"), ("wt", "head")),
        P("groups"),
    )

    def local(*args):
        sizes = tuple(mesh.shape[name] for name in ("seq", "wt", "head"))
        rows, features = args[0].shape
        if sizes == (4, 2, 2) and rows % 32 == 0 and features % (2 * HEAD_DIM) == 0:
            return local_heads(*args)
        return local_general(*args)

    return jax.shard_map(
        local,
        mesh=mesh,
        in_specs=placed,
        out_specs=(P(("groups", "seq"), ("wt", "head")), P(("groups", "seq"), ("wt", "head"))),
        check_vma=False,
    )
```

```python
import functools

import jax
import jax.numpy as jnp
from jax import lax
from jax.experimental import pallas as pl
from jax.experimental.pallas import tpu as pltpu
from jax.sharding import PartitionSpec as P

HEAD_DIM = 128
VMEM_BYTES = 48 * 1024 * 1024
PACK_BYTES = 53 * 1024 * 1024 + 128 * 1024
LOG2_E = 1.4426950408889634


def attend(state_in, key_rows, value_rows, query_heads, score_scale):
    key_count = key_rows.shape[0]
    head_count = query_heads.shape[1]
    blocks = -(-key_count // 1024)
    while key_count % blocks:
        blocks = blocks + 1
    block_size = key_count // blocks

    def one_block(block_index, state_now):
        row_peak, row_total, weighted = state_now
        start_row = block_index * block_size
        key_block = lax.dynamic_slice_in_dim(key_rows, start_row, block_size, 0)
        value_block = lax.dynamic_slice_in_dim(value_rows, start_row, block_size, 0)
        key_heads = key_block.reshape(block_size, head_count, HEAD_DIM)
        value_heads = value_block.reshape(block_size, head_count, HEAD_DIM)
        scores = (
            jnp.einsum("ihd,jhd->hij", query_heads, key_heads, preferred_element_type=jnp.float32)
            * score_scale
        )
        new_peak = jnp.maximum(row_peak, jnp.max(scores, axis=2))
        exp_scores = jnp.exp(scores - new_peak[:, :, None])
        rescale = jnp.exp(row_peak - new_peak)
        row_total = row_total * rescale + jnp.sum(exp_scores, axis=2)
        weighted = weighted * rescale[:, :, None] + jnp.einsum(
            "hij,jhd->hid",
            exp_scores.astype(jnp.bfloat16),
            value_heads,
            preferred_element_type=jnp.float32,
        )
        return (new_peak, row_total, weighted)

    return lax.fori_loop(0, blocks, one_block, state_in)


def finish(state_out, row_count):
    row_peak, row_total, weighted = state_out
    normed = weighted / row_total[:, :, None]
    return normed.transpose(1, 0, 2).reshape(row_count, -1).astype(jnp.bfloat16)


def local_general(
    queries,
    key_vectors,
    value_vectors,
    out_weight,
    gate_values,
    hidden_state,
    cached_deltas,
    skip_flags,
):
    row_count = queries.shape[0]
    head_count = queries.shape[1] // HEAD_DIM
    score_scale = HEAD_DIM ** (-0.5)
    query_heads = queries.reshape(row_count, head_count, HEAD_DIM)
    start_state = (
        jnp.full((head_count, row_count), -1e30, jnp.float32),
        jnp.zeros((head_count, row_count), jnp.float32),
        jnp.zeros((head_count, row_count, HEAD_DIM), jnp.float32),
    )
    gathered_keys, gathered_values, gathered_weight = (
        lax.all_gather(key_vectors, "seq", axis=0, tiled=True),
        lax.all_gather(value_vectors, "seq", axis=0, tiled=True),
        lax.all_gather(out_weight, "seq", axis=1, tiled=True),
    )
    final_state = attend(start_state, gathered_keys, gathered_values, query_heads, score_scale)
    attention_out = finish(final_state, row_count)
    partial_sums = jnp.dot(attention_out, gathered_weight, preferred_element_type=jnp.float32)
    head_total = lax.psum_scatter(
        partial_sums.astype(jnp.bfloat16), ("wt", "head"), scatter_dimension=1, tiled=True
    ).astype(jnp.float32)
    fresh_delta = head_total * gate_values[None, :]
    kept_deltas = jnp.sum(skip_flags.astype(jnp.float32)[:, None, None] * cached_deltas, axis=0)
    mixed_state = hidden_state + kept_deltas + fresh_delta
    return (mixed_state, fresh_delta)


def bits():
    z = lax.axis_index("seq")
    return lax.div(z, 2), lax.rem(z, 2)


def flip(bit, value):
    return 1 - bit if value else bit


def pack_kernel(queries, keys, values, *refs):
    outs, sems = refs[:4], refs[4]
    rows, width = queries.shape[0], outs[0].shape[1]
    half = rows // 2
    zh, zl = bits()
    copies = []
    for k in range(4):
        part = pl.ds(pl.multiple_of(flip(zl, k // 2) * half, 16), half)
        columns = pl.ds(pl.multiple_of(flip(zh, 1 - k % 2) * width, 128), width)
        moves = [
            (keys.at[part, columns], outs[k].at[pl.ds(0, half), :]),
            (values.at[part, columns], outs[k].at[pl.ds(half, half), :]),
        ]
        if k < 2:
            moves.append((queries.at[:, columns], outs[k].at[pl.ds(rows, rows), :]))
        for start, end in moves:
            copies.append(pltpu.make_async_copy(start, end, sems.at[len(copies)]))
    for copy in copies:
        copy.start()
    for copy in copies:
        copy.wait()


def join_kernel(*refs):
    blocks, joined = refs[:4], refs[4]
    rows = joined.shape[0] // 4
    for k, block in enumerate(blocks):
        joined[k * rows : (k + 1) * rows, :] = block[:rows, :]


def attention_kernel(*refs):
    blocks, sibling = refs[:4], refs[4]
    sent, kept, key_all, value_all, query_all = refs[5:]
    rows = sent.shape[0]
    half = rows // 2
    for k in range(4):
        here, there = slice(k * half, (k + 1) * half), slice((4 + k) * half, (5 + k) * half)
        key_all[here, :] = blocks[k][:half, :]
        value_all[here, :] = blocks[k][half:rows, :]
        key_all[there, :] = sibling[k * rows : k * rows + half, :]
        value_all[there, :] = sibling[k * rows + half : (k + 1) * rows, :]
    zh, _ = bits()
    x = lax.axis_index("wt")
    for k in range(2):
        for part in range(2):
            at = rows + flip(x, part == 0) * half
            to = (part * 2 + flip(zh, 1 - k)) * half
            query_all[pl.ds(pl.multiple_of(to, 16), half), :] = blocks[k][
                pl.ds(pl.multiple_of(at, 16), half), :
            ]
    heads = [
        slice(h * HEAD_DIM, (h + 1) * HEAD_DIM) for h in range(sent.shape[1] // HEAD_DIM)
    ]
    scores = [
        lax.dot_general(
            query_all[:, columns],
            key_all[:, columns],
            (((1,), (1,)), ((), ())),
            preferred_element_type=jnp.float32,
        )
        for columns in heads
    ]
    weights = [
        jnp.exp2((score - jnp.max(score, axis=1, keepdims=True)) * (LOG2_E * HEAD_DIM ** (-0.5)))
        for score in scores
    ]
    results = [
        jnp.dot(
            weight.astype(jnp.bfloat16), value_all[:, columns], preferred_element_type=jnp.float32
        )
        for weight, columns in zip(weights, heads)
    ]
    for weight, result, columns in zip(weights, results, heads):
        result = (result / jnp.sum(weight, axis=1, keepdims=True)).astype(sent.dtype)
        sent[:, columns] = result[:rows]
        kept[:, columns] = result[rows:]


def multiply(shards, weight, weight_c, held):
    rows = shards[0].shape[0]
    zh, zl = bits()
    core = lax.axis_index("head")
    for m, shard in enumerate(shards):
        held[m * rows : (m + 1) * rows, :] = shard[...]
    total = None
    for other, block in enumerate((weight, weight_c)):
        low = lax.rem(flip(core, other) + zl, 2)
        left = jnp.concatenate(
            [
                held[pl.ds(pl.multiple_of((2 * flip(zh, high) + low) * rows, 16), rows), :]
                for high in range(2)
            ],
            axis=1,
        )
        term = jnp.dot(left, block[...], preferred_element_type=jnp.float32)
        total = term if total is None else total + term
    return total


def project_kernel(kept, *refs):
    shards, (weight, weight_c, out0, out1, held) = refs[:4], refs[4:]
    total = multiply(shards, weight, weight_c, held)
    half = out0.shape[0]
    _, zl = bits()
    side = lax.rem(lax.axis_index("wt") + zl, 2)
    for high in range(2):
        part = total[high * half : (high + 1) * half].astype(out0.dtype)
        first = flip(side, high) == 1 - kept

        @pl.when(first)
        def _():
            out0[...] = part

        @pl.when(jnp.logical_not(first))
        def _():
            out1[...] = part


def add_kernel(kept, arrived, out):
    out[...] = (kept[...] + arrived[...].astype(jnp.float32)).astype(out.dtype)


def rest_kernel(flags, hidden, cached, out):
    total = hidden[...]
    for layer in range(cached.shape[0]):
        total = total + flags[layer].astype(jnp.float32) * cached[layer]
    out[...] = total


def final_kernel(piece, owned, gate, resting, *refs):
    mixed, fresh, mixed_part, fresh_part, sems = refs[-5:]
    half = owned.shape[0]
    zh, _ = bits()
    side = lax.rem(zh + lax.axis_index("head"), 2)
    rows = pl.ds(pl.multiple_of(flip(side, piece) * half, 16), half)
    delta = owned[...].astype(jnp.float32) * gate[...]
    fresh_part[...] = delta
    copy_fresh = pltpu.make_async_copy(fresh_part, fresh.at[rows, :], sems.at[0])
    copy_fresh.start()
    mixed_part[...] = resting[rows, :] + delta
    copy_mixed = pltpu.make_async_copy(mixed_part, mixed.at[rows, :], sems.at[1])
    copy_mixed.start()
    copy_fresh.wait()
    copy_mixed.wait()


def along(shard, m):
    return lax.ppermute(shard, "seq", [(z, z ^ m) for z in range(4)])


def call(
    kernel,
    args,
    outs,
    scratch=(),
    space=pltpu.VMEM,
    out_space=pltpu.VMEM,
    flops=0,
    vmem=VMEM_BYTES,
):
    spaces = [pltpu.SMEM if arg.dtype == jnp.int32 else space for arg in args]
    return pl.pallas_call(
        kernel,
        in_specs=[pl.BlockSpec(memory_space=place) for place in spaces],
        out_specs=[pl.BlockSpec(memory_space=out_space)] * len(outs),
        out_shape=[jax.ShapeDtypeStruct(shape, dtype) for shape, dtype in outs],
        scratch_shapes=list(scratch),
        compiler_params=pltpu.CompilerParams(vmem_limit_bytes=vmem),
        cost_estimate=pl.CostEstimate(flops=flops, bytes_accessed=0, transcendentals=0),
    )(*args)


def local_heads(
    queries,
    key_vectors,
    value_vectors,
    out_weight,
    gate_values,
    hidden_state,
    cached_deltas,
    skip_flags,
):
    rows, features = queries.shape
    width = features // 2
    depth, columns = out_weight.shape
    swap = [(0, 1), (1, 0)]
    bf16 = jnp.bfloat16

    packed = call(
        pack_kernel,
        (queries, key_vectors, value_vectors),
        [((2 * rows, width), bf16)] * 2 + [((rows, width), bf16)] * 2,
        [pltpu.SemaphoreType.DMA((10,))],
        space=pl.ANY,
        vmem=PACK_BYTES,
    )
    late_weight, _ = lax.optimization_barrier((out_weight, packed[0]))
    weight_c = lax.ppermute(late_weight, "head", swap)
    moved = []
    for k in range(4):
        k1, k0 = k // 2, 1 - k % 2
        pairs = []
        for zz in range(4):
            for cc in range(2):
                to_z = 2 * ((zz // 2) ^ k0) + cc
                pairs.append((zz * 2 + cc, to_z * 2 + ((zz % 2) ^ k1)))
        moved.append(lax.ppermute(packed[k], ("seq", "head"), pairs))
    (joined,) = call(join_kernel, moved, [((4 * rows, width), bf16)])
    sibling = lax.ppermute(joined, "head", swap)
    sibling, _ = lax.optimization_barrier((sibling, weight_c))
    parts = call(
        attention_kernel,
        moved + [sibling],
        [((rows, width), bf16)] * 2,
        [
            pltpu.VMEM((4 * rows, width), bf16),
            pltpu.VMEM((4 * rows, width), bf16),
            pltpu.VMEM((2 * rows, width), bf16),
        ],
        flops=4 * (2 * rows) * (4 * rows) * width,
    )

    half = rows // 2
    flops = 4 * rows * depth * columns
    sent, kept = (
        call(
            functools.partial(project_kernel, i),
            [part] + [along(part, m) for m in (1, 2, 3)] + [out_weight, weight_c],
            [((half, columns), dtype)] * 2,
            [pltpu.VMEM((4 * rows, width), bf16)],
            flops=effort * flops,
        )
        for i, (part, dtype, effort) in enumerate(((parts[0], bf16, 1), (parts[1], jnp.float32, 8)))
    )

    owned = []
    for p in range(2):
        arrived = lax.ppermute(sent[p], "wt", swap)
        (summed,) = call(add_kernel, (kept[p], arrived), [((half, columns), bf16)])
        pairs = []
        for zz in range(4):
            for xx in range(2):
                for cc in range(2):
                    to = ((cc + 2 * (p ^ xx ^ (zz % 2))) * 2 + zz // 2) * 2 + zz % 2
                    pairs.append(((zz * 2 + xx) * 2 + cc, to))
        owned.append(lax.ppermute(summed, ("seq", "wt", "head"), pairs))
    (resting,) = call(
        rest_kernel, (skip_flags, hidden_state, cached_deltas), [((rows, columns), jnp.float32)]
    )
    gate = gate_values[None, :]
    results = ()
    for p, part in enumerate(owned):
        results = pl.pallas_call(
            functools.partial(final_kernel, p),
            in_specs=[pl.BlockSpec(memory_space=pltpu.VMEM)] * 3
            + [pl.BlockSpec(memory_space=pl.ANY)] * len(results),
            out_specs=[pl.BlockSpec(memory_space=pl.ANY)] * 2,
            out_shape=[jax.ShapeDtypeStruct((rows, columns), jnp.float32)] * 2,
            scratch_shapes=[pltpu.VMEM((half, columns), jnp.float32)] * 2
            + [pltpu.SemaphoreType.DMA((2,))],
            input_output_aliases={3 + i: i for i in range(len(results))},
            compiler_params=pltpu.CompilerParams(vmem_limit_bytes=VMEM_BYTES),
            cost_estimate=pl.CostEstimate(flops=0, bytes_accessed=0, transcendentals=0),
        )(part, gate, resting, *results)
    return tuple(results)


def solution(mesh):
    placed = (
        P(("groups", "seq"), ("wt", "head")),
        P(("groups", "seq"), ("wt", "head")),
        P(("groups", "seq"), ("wt", "head")),
        P(("wt", "head"), "seq"),
        P(("groups", "wt", "head")),
        P(("groups", "seq"), ("wt", "head")),
        P(None, ("groups", "seq"), ("wt", "head")),
        P("groups"),
    )

    def local(*args):
        sizes = tuple(mesh.shape[name] for name in ("seq", "wt", "head"))
        rows, features = args[0].shape
        if sizes == (4, 2, 2) and rows % 32 == 0 and features % (2 * HEAD_DIM) == 0:
            return local_heads(*args)
        return local_general(*args)

    return jax.shard_map(
        local,
        mesh=mesh,
        in_specs=placed,
        out_specs=(P(("groups", "seq"), ("wt", "head")), P(("groups", "seq"), ("wt", "head"))),
        check_vma=False,
    )
```

```python
import functools

import jax
import jax.numpy as jnp
from jax import lax
from jax.experimental import pallas as pl
from jax.experimental.pallas import tpu as pltpu
from jax.sharding import PartitionSpec as P

HEAD_DIM = 128
VMEM_BYTES = 48 * 1024 * 1024
PACK_BYTES = 53 * 1024 * 1024 + 128 * 1024
LOG2_E = 1.4426950408889634


def attend(state_in, key_rows, value_rows, query_heads, score_scale):
    key_count = key_rows.shape[0]
    head_count = query_heads.shape[1]
    blocks = -(-key_count // 1024)
    while key_count % blocks:
        blocks = blocks + 1
    block_size = key_count // blocks

    def one_block(block_index, state_now):
        row_peak, row_total, weighted = state_now
        start_row = block_index * block_size
        key_block = lax.dynamic_slice_in_dim(key_rows, start_row, block_size, 0)
        value_block = lax.dynamic_slice_in_dim(value_rows, start_row, block_size, 0)
        key_heads = key_block.reshape(block_size, head_count, HEAD_DIM)
        value_heads = value_block.reshape(block_size, head_count, HEAD_DIM)
        scores = (
            jnp.einsum("ihd,jhd->hij", query_heads, key_heads, preferred_element_type=jnp.float32)
            * score_scale
        )
        new_peak = jnp.maximum(row_peak, jnp.max(scores, axis=2))
        exp_scores = jnp.exp(scores - new_peak[:, :, None])
        rescale = jnp.exp(row_peak - new_peak)
        row_total = row_total * rescale + jnp.sum(exp_scores, axis=2)
        weighted = weighted * rescale[:, :, None] + jnp.einsum(
            "hij,jhd->hid",
            exp_scores.astype(jnp.bfloat16),
            value_heads,
            preferred_element_type=jnp.float32,
        )
        return (new_peak, row_total, weighted)

    return lax.fori_loop(0, blocks, one_block, state_in)


def finish(state_out, row_count):
    row_peak, row_total, weighted = state_out
    normed = weighted / row_total[:, :, None]
    return normed.transpose(1, 0, 2).reshape(row_count, -1).astype(jnp.bfloat16)


def local_general(
    queries,
    key_vectors,
    value_vectors,
    out_weight,
    gate_values,
    hidden_state,
    cached_deltas,
    skip_flags,
):
    row_count = queries.shape[0]
    head_count = queries.shape[1] // HEAD_DIM
    score_scale = HEAD_DIM ** (-0.5)
    query_heads = queries.reshape(row_count, head_count, HEAD_DIM)
    start_state = (
        jnp.full((head_count, row_count), -1e30, jnp.float32),
        jnp.zeros((head_count, row_count), jnp.float32),
        jnp.zeros((head_count, row_count, HEAD_DIM), jnp.float32),
    )
    gathered_keys, gathered_values, gathered_weight = (
        lax.all_gather(key_vectors, "seq", axis=0, tiled=True),
        lax.all_gather(value_vectors, "seq", axis=0, tiled=True),
        lax.all_gather(out_weight, "seq", axis=1, tiled=True),
    )
    final_state = attend(start_state, gathered_keys, gathered_values, query_heads, score_scale)
    attention_out = finish(final_state, row_count)
    partial_sums = jnp.dot(attention_out, gathered_weight, preferred_element_type=jnp.float32)
    head_total = lax.psum_scatter(
        partial_sums.astype(jnp.bfloat16), ("wt", "head"), scatter_dimension=1, tiled=True
    ).astype(jnp.float32)
    fresh_delta = head_total * gate_values[None, :]
    kept_deltas = jnp.sum(skip_flags.astype(jnp.float32)[:, None, None] * cached_deltas, axis=0)
    mixed_state = hidden_state + kept_deltas + fresh_delta
    return (mixed_state, fresh_delta)


def bits():
    z = lax.axis_index("seq")
    return lax.div(z, 2), lax.rem(z, 2)


def flip(bit, value):
    return 1 - bit if value else bit


def pack_kernel(queries, keys, values, *refs):
    outs, sems = refs[:4], refs[4]
    rows, width = queries.shape[0], outs[0].shape[1]
    half = rows // 2
    zh, zl = bits()
    copies = []
    for k in range(4):
        part = pl.ds(pl.multiple_of(flip(zl, k // 2) * half, 16), half)
        columns = pl.ds(pl.multiple_of(flip(zh, 1 - k % 2) * width, 128), width)
        moves = [
            (keys.at[part, columns], outs[k].at[pl.ds(0, half), :]),
            (values.at[part, columns], outs[k].at[pl.ds(half, half), :]),
        ]
        if k < 2:
            moves.append((queries.at[:, columns], outs[k].at[pl.ds(rows, rows), :]))
        for start, end in moves:
            copies.append(pltpu.make_async_copy(start, end, sems.at[len(copies)]))
    for copy in copies:
        copy.start()
    for copy in copies:
        copy.wait()


def join_kernel(*refs):
    blocks, joined = refs[:4], refs[4]
    rows = joined.shape[0] // 4
    for k, block in enumerate(blocks):
        joined[k * rows : (k + 1) * rows, :] = block[:rows, :]


def attention_kernel(*refs):
    blocks, sibling = refs[:4], refs[4]
    sent, kept, key_all, value_all, query_all = refs[5:]
    rows = sent.shape[0]
    half = rows // 2
    for k in range(4):
        here, there = slice(k * half, (k + 1) * half), slice((4 + k) * half, (5 + k) * half)
        key_all[here, :] = blocks[k][:half, :]
        value_all[here, :] = blocks[k][half:rows, :]
        key_all[there, :] = sibling[k * rows : k * rows + half, :]
        value_all[there, :] = sibling[k * rows + half : (k + 1) * rows, :]
    zh, _ = bits()
    x = lax.axis_index("wt")
    for k in range(2):
        for part in range(2):
            at = rows + flip(x, part == 0) * half
            to = (part * 2 + flip(zh, 1 - k)) * half
            query_all[pl.ds(pl.multiple_of(to, 16), half), :] = blocks[k][
                pl.ds(pl.multiple_of(at, 16), half), :
            ]
    heads = [
        slice(h * HEAD_DIM, (h + 1) * HEAD_DIM) for h in range(sent.shape[1] // HEAD_DIM)
    ]
    scores = [
        lax.dot_general(
            query_all[:, columns],
            key_all[:, columns],
            (((1,), (1,)), ((), ())),
            preferred_element_type=jnp.float32,
        )
        for columns in heads
    ]
    weights = [
        jnp.exp2((score - jnp.max(score, axis=1, keepdims=True)) * (LOG2_E * HEAD_DIM ** (-0.5)))
        for score in scores
    ]
    results = [
        jnp.dot(
            weight.astype(jnp.bfloat16), value_all[:, columns], preferred_element_type=jnp.float32
        )
        for weight, columns in zip(weights, heads)
    ]
    for weight, result, columns in zip(weights, results, heads):
        result = (result / jnp.sum(weight, axis=1, keepdims=True)).astype(sent.dtype)
        sent[:, columns] = result[:rows]
        kept[:, columns] = result[rows:]


def multiply(shards, weight, weight_c, held):
    rows = shards[0].shape[0]
    zh, zl = bits()
    core = lax.axis_index("head")
    for m, shard in enumerate(shards):
        held[m * rows : (m + 1) * rows, :] = shard[...]
    total = None
    for other, block in enumerate((weight, weight_c)):
        low = lax.rem(flip(core, other) + zl, 2)
        left = jnp.concatenate(
            [
                held[pl.ds(pl.multiple_of((2 * flip(zh, high) + low) * rows, 16), rows), :]
                for high in range(2)
            ],
            axis=1,
        )
        term = jnp.dot(left, block[...], preferred_element_type=jnp.float32)
        total = term if total is None else total + term
    return total


def project_kernel(kept, *refs):
    shards, (weight, weight_c), outs, held = refs[:4], refs[4:6], refs[6:-1], refs[-1]
    total = multiply(shards, weight, weight_c, held)
    half = total.shape[0] // 2
    if len(outs) == 1:
        out0, out1 = outs[0].at[:half, :], outs[0].at[half:, :]
    else:
        out0, out1 = outs
    _, zl = bits()
    side = lax.rem(lax.axis_index("wt") + zl, 2)
    for high in range(2):
        part = total[high * half : (high + 1) * half].astype(outs[0].dtype)
        first = flip(side, high) == 1 - kept

        @pl.when(first)
        def _():
            out0[...] = part

        @pl.when(jnp.logical_not(first))
        def _():
            out1[...] = part


def add_kernel(piece, kept, arrived, out):
    rows = slice(piece * kept.shape[0], (piece + 1) * kept.shape[0])
    out[...] = (kept[...] + arrived[rows, :].astype(jnp.float32)).astype(out.dtype)


def rest_kernel(flags, hidden, cached, out):
    total = hidden[...]
    for layer in range(cached.shape[0]):
        total = total + flags[layer].astype(jnp.float32) * cached[layer]
    out[...] = total


def final_kernel(piece, owned, gate, resting, *refs):
    mixed, fresh, mixed_part, fresh_part, sems = refs[-5:]
    half = owned.shape[0]
    zh, _ = bits()
    side = lax.rem(zh + lax.axis_index("head"), 2)
    rows = pl.ds(pl.multiple_of(flip(side, piece) * half, 16), half)
    delta = owned[...].astype(jnp.float32) * gate[...]
    fresh_part[...] = delta
    copy_fresh = pltpu.make_async_copy(fresh_part, fresh.at[rows, :], sems.at[0])
    copy_fresh.start()
    mixed_part[...] = resting[rows, :] + delta
    copy_mixed = pltpu.make_async_copy(mixed_part, mixed.at[rows, :], sems.at[1])
    copy_mixed.start()
    copy_fresh.wait()
    copy_mixed.wait()


def along(shard, m):
    return lax.ppermute(shard, "seq", [(z, z ^ m) for z in range(4)])


def call(
    kernel,
    args,
    outs,
    scratch=(),
    space=pltpu.VMEM,
    out_space=pltpu.VMEM,
    flops=0,
    vmem=VMEM_BYTES,
):
    spaces = [pltpu.SMEM if arg.dtype == jnp.int32 else space for arg in args]
    return pl.pallas_call(
        kernel,
        in_specs=[pl.BlockSpec(memory_space=place) for place in spaces],
        out_specs=[pl.BlockSpec(memory_space=out_space)] * len(outs),
        out_shape=[jax.ShapeDtypeStruct(shape, dtype) for shape, dtype in outs],
        scratch_shapes=list(scratch),
        compiler_params=pltpu.CompilerParams(vmem_limit_bytes=vmem),
        cost_estimate=pl.CostEstimate(flops=flops, bytes_accessed=0, transcendentals=0),
    )(*args)


def local_heads(
    queries,
    key_vectors,
    value_vectors,
    out_weight,
    gate_values,
    hidden_state,
    cached_deltas,
    skip_flags,
):
    rows, features = queries.shape
    width = features // 2
    depth, columns = out_weight.shape
    swap = [(0, 1), (1, 0)]
    bf16 = jnp.bfloat16

    packed = call(
        pack_kernel,
        (queries, key_vectors, value_vectors),
        [((2 * rows, width), bf16)] * 2 + [((rows, width), bf16)] * 2,
        [pltpu.SemaphoreType.DMA((10,))],
        space=pl.ANY,
        vmem=PACK_BYTES,
    )
    late_weight, _ = lax.optimization_barrier((out_weight, packed[0]))
    weight_c = lax.ppermute(late_weight, "head", swap)
    moved = []
    for k in range(4):
        k1, k0 = k // 2, 1 - k % 2
        pairs = []
        for zz in range(4):
            for cc in range(2):
                to_z = 2 * ((zz // 2) ^ k0) + cc
                pairs.append((zz * 2 + cc, to_z * 2 + ((zz % 2) ^ k1)))
        moved.append(lax.ppermute(packed[k], ("seq", "head"), pairs))
    (joined,) = call(join_kernel, moved, [((4 * rows, width), bf16)])
    sibling = lax.ppermute(joined, "head", swap)
    sibling, _ = lax.optimization_barrier((sibling, weight_c))
    parts = call(
        attention_kernel,
        moved + [sibling],
        [((rows, width), bf16)] * 2,
        [
            pltpu.VMEM((4 * rows, width), bf16),
            pltpu.VMEM((4 * rows, width), bf16),
            pltpu.VMEM((2 * rows, width), bf16),
        ],
        flops=4 * (2 * rows) * (4 * rows) * width,
    )

    half = rows // 2
    flops = 4 * rows * depth * columns
    sent, kept = (
        call(
            functools.partial(project_kernel, i),
            [part] + [along(part, m) for m in (1, 2, 3)] + [out_weight, weight_c],
            shapes,
            [pltpu.VMEM((4 * rows, width), bf16)],
            flops=effort * flops,
        )
        for i, (part, shapes, effort) in enumerate(
            (
                (parts[0], [((rows, columns), bf16)], 1),
                (parts[1], [((half, columns), jnp.float32)] * 2, 8),
            )
        )
    )

    owned = []
    arrived = lax.ppermute(sent[0], "wt", swap)
    for p in range(2):
        (summed,) = call(
            functools.partial(add_kernel, p), (kept[p], arrived), [((half, columns), bf16)]
        )
        pairs = []
        for zz in range(4):
            for xx in range(2):
                for cc in range(2):
                    to = ((cc + 2 * (p ^ xx ^ (zz % 2))) * 2 + zz // 2) * 2 + zz % 2
                    pairs.append(((zz * 2 + xx) * 2 + cc, to))
        owned.append(lax.ppermute(summed, ("seq", "wt", "head"), pairs))
    (resting,) = call(
        rest_kernel, (skip_flags, hidden_state, cached_deltas), [((rows, columns), jnp.float32)]
    )
    gate = gate_values[None, :]
    results = ()
    for p, part in enumerate(owned):
        results = pl.pallas_call(
            functools.partial(final_kernel, p),
            in_specs=[pl.BlockSpec(memory_space=pltpu.VMEM)] * 3
            + [pl.BlockSpec(memory_space=pl.ANY)] * len(results),
            out_specs=[pl.BlockSpec(memory_space=pl.ANY)] * 2,
            out_shape=[jax.ShapeDtypeStruct((rows, columns), jnp.float32)] * 2,
            scratch_shapes=[pltpu.VMEM((half, columns), jnp.float32)] * 2
            + [pltpu.SemaphoreType.DMA((2,))],
            input_output_aliases={3 + i: i for i in range(len(results))},
            compiler_params=pltpu.CompilerParams(vmem_limit_bytes=VMEM_BYTES),
            cost_estimate=pl.CostEstimate(flops=0, bytes_accessed=0, transcendentals=0),
        )(part, gate, resting, *results)
    return tuple(results)


def solution(mesh):
    placed = (
        P(("groups", "seq"), ("wt", "head")),
        P(("groups", "seq"), ("wt", "head")),
        P(("groups", "seq"), ("wt", "head")),
        P(("wt", "head"), "seq"),
        P(("groups", "wt", "head")),
        P(("groups", "seq"), ("wt", "head")),
        P(None, ("groups", "seq"), ("wt", "head")),
        P("groups"),
    )

    def local(*args):
        sizes = tuple(mesh.shape[name] for name in ("seq", "wt", "head"))
        rows, features = args[0].shape
        if sizes == (4, 2, 2) and rows % 32 == 0 and features % (2 * HEAD_DIM) == 0:
            return local_heads(*args)
        return local_general(*args)

    return jax.shard_map(
        local,
        mesh=mesh,
        in_specs=placed,
        out_specs=(P(("groups", "seq"), ("wt", "head")), P(("groups", "seq"), ("wt", "head"))),
        check_vma=False,
    )
```
